128 devices in a mesh: ctx: 32 (over x, y_lo, z), tp: 4 (over y_hi, core).
Axes of the slice: x: 4, y: 4 (y_hi: 2, y_lo: 2; y = y_hi * 2 + y_lo), z: 4, core: 2. Of those that a mesh axis runs over, the one named last changes fastest.
Arguments:
- stream_in: bfloat16 [4096, 6144], P(('ctx', 'tp')), may hold values from -3 to 3
- queries: bfloat16 [4096, 3072], P('ctx', 'tp'), may hold values from -5 to 5
- rotated_key_heads: bfloat16 [4096, 512], P('ctx', 'tp'), may hold values from -5 to 5
- values: bfloat16 [4096, 512], P('ctx', 'tp'), may hold values from -6 to 6
- doc_ids: int32 [4096], P('ctx'), may hold values from 0 to 7, never falling along the last dimension, each value on 1 to 2048 neighbouring positions
- out_proj: bfloat16 [3072, 6144], P('tp', 'ctx'), may hold values from -0.4375 to 0.4375
- norm_gain: float32 [6144], replicated, may hold values from 0.1 to 1.9
- router: float32 [6144, 8], replicated, may hold values from -0.078125 to 0.078125
- w_gate: bfloat16 [6144, 65536], P(None, ('ctx', 'tp')), may hold values from -0.078125 to 0.078125
- w_up: bfloat16 [6144, 65536], P(None, ('ctx', 'tp')), may hold values from -0.078125 to 0.078125
- w_down: bfloat16 [65536, 6144], P(('ctx', 'tp')), may hold values from -0.0625 to 0.0625
- routes: int32 [4096, 2], P(('ctx', 'tp')), may hold values from 0 to 7, all different within a row; in each aligned block of 32 rows (0 to 31, 32 to 63, ...) at most 9 rows name the same one
Outputs:
- layer_out: bfloat16 [4096, 6144], P(('ctx', 'tp'))
The draws below stay inside these ranges and needn't reach their ends.
Inputs may be any that keep to these rules, and one draw needn't show every extreme that they name: `doc_ids`: starts at 0 and never falls; each document holds 1 to 2048 positions, and one holds exactly 2048. `routes`: each row names two different experts; in each aligned block of 32 rows (the rows of one device) no expert is named by more than 9 rows, and in every draw some block names some expert exactly 9 times.
All inputs are finite; a program needn't handle non-finite values.
Results may differ from the reference program's by a relative error of at most 0.019.
Values may be sent and summed in bfloat16 or wider, within the bound.
No kernel may reach another device: no remote copies, remote signals or barrier semaphores. Data moves between devices by JAX's collectives and lax.ppermute only.
A program may use at most 192 MiB of HBM per device.

```python
import math
import jax
import jax.numpy as jnp
import numpy as np
from jax import lax

D = 6144
HEAD_WIDTH = 128
QUERY_HEADS = 24
KEY_VALUE_HEADS = 4
EXPERTS = 8
FF = 8192
DOCS = 8
TOKEN_COUNT = 4096
ROWS = 32
CAP = 9
DOC_MAX = 2048
N_CTX = 32
N_TP = 4


def draw_rotated_key_heads(key, part):
    key = jax.random.fold_in(key, 7)
    rotary_base = jnp.clip(jax.random.normal(key, (TOKEN_COUNT, KEY_VALUE_HEADS * HEAD_WIDTH), jnp.float32), -5.0, 5.0)
    return rotary_base.astype(jnp.bfloat16)


def draw_queries(key, part):
    key = jax.random.fold_in(key, 8)
    rotary_base = jnp.clip(jax.random.normal(key, (TOKEN_COUNT, QUERY_HEADS * HEAD_WIDTH), jnp.float32), -5.0, 5.0)
    return rotary_base.astype(jnp.bfloat16)


def level_of(own_key, shape, pieces, least, top_value):
    level = 1.0
    for axis_at, parts in pieces:
        draws = jax.random.uniform(jax.random.fold_in(jax.random.fold_in(own_key, 6), axis_at), (parts,), jnp.float32, least / len(pieces), top_value / len(pieces))
        level = level * jnp.repeat(jnp.exp(draws), shape[axis_at] // parts).reshape((-1,) + (1,) * (len(shape) - 1 - axis_at))
    return level


def split_up(count, total, most, lean):
    loads = [(1 << 20) // math.isqrt(standing ** lean) + 1 for standing in range(2, count + 1)]
    surplus, counts = total - most - (count - 1), [1] * (count - 1)
    while surplus > 0:
        free = [i for i in range(count - 1) if counts[i] < most]
        mass, budget = sum([loads[i] for i in free]), surplus
        for i in free:
            more = min(most - counts[i], max(1, budget * loads[i] // mass), surplus)
            counts[i] = counts[i] + more
            surplus = surplus - more
    return np.array([most] + counts)


def ragged_sizes(rng, amount, total, most, slope):
    if amount == 2:
        one = jax.random.randint(rng, (), max(1, total - most), min(most, total - 1) + 1)
        return jnp.stack([one, total - one])
    tallies = jnp.asarray(split_up(amount, total, most, slope), jnp.int32)
    pairs = (amount - 1) // 2
    donor, receiver = tallies[1:1 + 2 * pairs:2], tallies[2:2 + 2 * pairs:2]
    margin = jnp.minimum(donor - 1, most - receiver)
    passed = jax.random.randint(jax.random.fold_in(rng, 1), (pairs,), 0, 1 << 20) % (margin + 1)
    tallies = tallies.at[1:1 + 2 * pairs:2].set(donor - passed).at[2:2 + 2 * pairs:2].set(receiver + passed)
    return tallies[jax.random.permutation(jax.random.fold_in(rng, 2), amount)]


def routed_block(key, own, number, rows, number_of, top, limit, slope):
    sequence = jax.random.permutation(key, number_of)
    crowded, usual = portions_of(number_of, rows * top, limit, slope, True), portions_of(number_of, rows * top, limit, slope, False)
    places = jnp.arange(number_of)

    def named(sizes, turn):
        used = int((sizes > 0).sum())
        fixed = max(1, used // 4)
        shifted = fixed + (places - fixed + turn * (used - fixed)) % max(1, number_of - fixed)
        return jnp.zeros((number_of,), jnp.int32).at[sequence[jnp.where(places < fixed, places, shifted)]].set(jnp.asarray(sizes, jnp.int32))

    sizes = jnp.where(number % 4 == 0, named(crowded, number // 4), named(usual, number - number // 4 - 1))
    mixed = jax.random.permutation(jax.random.fold_in(own, 3), number_of)
    source_of, taker = mixed[0:number_of // 2 * 2:2], mixed[1:number_of // 2 * 2:2]
    slack = jnp.minimum(sizes[source_of] - 1, limit - sizes[taker]) // 2
    slack = jnp.where((source_of == sequence[0]) | (taker == sequence[0]) | (sizes[taker] == 0), 0, jnp.maximum(slack, 0))
    shifted = jax.random.randint(jax.random.fold_in(own, 4), (number_of // 2,), 0, 1 << 20) % (slack + 1)
    sizes = sizes.at[source_of].add(-shifted).at[taker].add(shifted)
    items = jnp.searchsorted(jnp.cumsum(sizes), jnp.arange(rows * top), side="right").astype(jnp.int32)
    table = items.reshape(top, rows).T
    table = table[jax.random.permutation(jax.random.fold_in(own, 1), rows)]
    turn = jax.random.randint(jax.random.fold_in(own, 2), (rows, 1), 0, top)
    return jnp.take_along_axis(table, (jnp.arange(top)[None, :] + turn) % top, axis=1)


def portions_of(number_of, total, bound, skew, full):
    loads = [(1 << 20) // math.isqrt(rank ** skew) + 1 for rank in range(1, number_of + 1)]
    largest = bound if full else min(bound, max(-(-total // number_of), total * loads[0] // sum(loads)))
    least = 1 if total - largest >= number_of - 1 else 0
    given, spare = [largest] + [least] * (number_of - 1), total - largest - least * (number_of - 1)
    while spare > 0:
        candidates = [i for i in range(1, number_of) if given[i] < largest] or [i for i in range(1, number_of) if given[i] < bound]
        pool, budget = sum([loads[i] for i in candidates]), spare
        for i in candidates:
            extra = min(bound - given[i], max(1, budget * loads[i] // pool), spare)
            given[i] = given[i] + extra
            spare = spare - extra
    return np.array(given)


def scatter_about(stream_key, shape, spread, most, pieces=(), kind=jnp.bfloat16):
    loudness = level_of(stream_key, shape, pieces, -0.22, 0.18) if pieces else 1.0
    entries = jax.random.normal(stream_key, shape, jnp.float32) * spread * loudness
    return jnp.minimum(jnp.maximum(entries, -most), most).astype(kind)


def setup_inputs(seed: int = 0) -> dict:
    key_of = jax.random.split(jax.random.key(seed), 13)
    stream_in = scatter_about(key_of[0], (TOKEN_COUNT, D), 0.5, 3.0, ((0, 128),))
    queries = draw_queries(jax.random.fold_in(key_of[12], 71), 0)
    rotated_key_heads = draw_rotated_key_heads(jax.random.fold_in(key_of[12], 71), 0)
    values = scatter_about(key_of[3], (TOKEN_COUNT, KEY_VALUE_HEADS * HEAD_WIDTH), 1.0, 6.0, ((0, 32), (1, 4)))
    doc_ids = jnp.searchsorted(jnp.cumsum(ragged_sizes(key_of[4], DOCS, TOKEN_COUNT, DOC_MAX, 2)), jnp.arange(TOKEN_COUNT), side="right").astype(jnp.int32)
    out_proj = scatter_about(key_of[5], (QUERY_HEADS * HEAD_WIDTH, D), (QUERY_HEADS * HEAD_WIDTH // 16) ** -0.5, 0.4375, ((0, 4), (1, 32)))
    norm_gain = jnp.clip(1.0 + 0.18 * jax.random.normal(key_of[6], (D,), jnp.float32), 0.1, 1.9)
    router = scatter_about(key_of[7], (D, EXPERTS), D ** -0.5, 0.078125, (), jnp.float32)
    w_gate = scatter_about(key_of[8], (D, EXPERTS * FF), D ** -0.5, 0.078125, ((1, 128),))
    w_up = scatter_about(key_of[9], (D, EXPERTS * FF), D ** -0.5, 0.078125, ((1, 128),))
    w_down = scatter_about(key_of[10], (EXPERTS * FF, D), FF ** -0.5, 0.0625, ((0, 128),))
    routes_keys = jax.random.split(jax.random.fold_in(key_of[11], 1), TOKEN_COUNT // ROWS)
    routes_turns = jax.random.permutation(jax.random.fold_in(key_of[11], 3), TOKEN_COUNT // ROWS)
    routes = jax.vmap(lambda own, number: routed_block(jax.random.fold_in(key_of[11], 2), own, number, ROWS, EXPERTS, 2, CAP, 2))(routes_keys, routes_turns).reshape((TOKEN_COUNT, 2))
    return {"stream_in": stream_in, "queries": queries, "rotated_key_heads": rotated_key_heads, "values": values, "doc_ids": doc_ids, "out_proj": out_proj, "norm_gain": norm_gain, "router": router, "w_gate": w_gate, "w_up": w_up, "w_down": w_down, "routes": routes}


def reference(stream_in, queries, rotated_key_heads, values, doc_ids, out_proj, norm_gain, router, w_gate, w_up, w_down, routes):
    head_group = QUERY_HEADS // KEY_VALUE_HEADS
    scale = HEAD_WIDTH ** (-0.5)
    places = jnp.arange(TOKEN_COUNT, dtype=jnp.int32)
    allowed = (places[None, :] <= places[:, None]) & (doc_ids[None, :] == doc_ids[:, None])
    q_heads = queries.reshape(TOKEN_COUNT, QUERY_HEADS, HEAD_WIDTH).transpose(1, 0, 2)
    key_head_rows = rotated_key_heads.reshape(TOKEN_COUNT, KEY_VALUE_HEADS, HEAD_WIDTH).transpose(1, 0, 2)
    value_head_rows = values.reshape(TOKEN_COUNT, KEY_VALUE_HEADS, HEAD_WIDTH).transpose(1, 0, 2)

    def one_head(index):
        query = q_heads[index]
        key_head = key_head_rows[index // head_group]
        value_head = value_head_rows[index // head_group]
        scores = jnp.dot(query, key_head.T, preferred_element_type=jnp.float32) * scale
        top = lax.optimization_barrier(jnp.max(jnp.where(allowed, scores, -jnp.inf), axis=1, keepdims=True))
        expo = jnp.where(allowed, jnp.exp(scores - top), 0.0)
        total = lax.optimization_barrier(jnp.sum(expo, axis=1, keepdims=True))
        return jnp.dot(expo.astype(jnp.bfloat16), value_head, preferred_element_type=jnp.float32) / total
    heads = lax.map(one_head, jnp.arange(QUERY_HEADS, dtype=jnp.int32))
    heads_out = heads.transpose(1, 0, 2).reshape(TOKEN_COUNT, QUERY_HEADS * HEAD_WIDTH).astype(jnp.bfloat16)
    width = QUERY_HEADS * HEAD_WIDTH // N_TP
    summed = jnp.zeros((TOKEN_COUNT, D), jnp.float32)
    for group_index in range(N_TP):
        part = jnp.dot(heads_out[:, group_index * width:(group_index + 1) * width], out_proj[group_index * width:(group_index + 1) * width], preferred_element_type=jnp.float32).astype(jnp.bfloat16)
        part = lax.optimization_barrier(part)
        summed = summed + part.astype(jnp.float32)
    resid = stream_in.astype(jnp.float32) + summed
    normed = (resid * lax.rsqrt(lax.optimization_barrier(jnp.mean(resid * resid, axis=1, keepdims=True)) + 1e-05) * norm_gain).astype(jnp.bfloat16)
    logits = jnp.dot(normed.astype(jnp.float32), router, precision=lax.Precision.HIGHEST)
    first = jnp.take_along_axis(logits, routes[:, 0:1], axis=1)[:, 0]
    second = jnp.take_along_axis(logits, routes[:, 1:2], axis=1)[:, 0]
    gate_pair = jnp.stack([1.0 / (1.0 + jnp.exp(second - first)), 1.0 / (1.0 + jnp.exp(first - second))], axis=1)
    slices = N_CTX * N_TP // EXPERTS
    ff_slice = FF // slices
    groups = N_CTX // EXPERTS
    most_rows = N_CTX * N_TP * CAP

    def add_expert(mixture, expert):
        hit = routes == expert
        row_hit = jnp.any(hit, axis=1)
        weight = lax.optimization_barrier(jnp.sum(jnp.where(hit, gate_pair, 0.0), axis=1))
        index = jnp.nonzero(row_hit, size=most_rows, fill_value=0)[0].astype(jnp.int32)
        valid = jnp.arange(most_rows, dtype=jnp.int32) < jnp.sum(row_hit.astype(jnp.int32))
        chosen = normed[index]
        start = expert * FF
        gate_cols = lax.dynamic_slice_in_dim(w_gate, start, FF, 1)
        up_cols = lax.dynamic_slice_in_dim(w_up, start, FF, 1)
        down_rows = lax.dynamic_slice_in_dim(w_down, start, FF, 0)
        hidden = (jax.nn.silu(jnp.dot(chosen, gate_cols, preferred_element_type=jnp.float32)) * jnp.dot(chosen, up_cols, preferred_element_type=jnp.float32)).astype(jnp.bfloat16)

        def group_sum(block):
            total = jnp.zeros((most_rows, D), jnp.float32)
            for inner in range(N_TP):
                offset = ((block * N_TP + inner) * ff_slice).astype(jnp.int32)
                part = jnp.dot(lax.dynamic_slice_in_dim(hidden, offset, ff_slice, 1), lax.dynamic_slice_in_dim(down_rows, offset, ff_slice, 0), preferred_element_type=jnp.float32).astype(jnp.bfloat16)
                part = lax.optimization_barrier(part)
                total = total + part.astype(jnp.float32)
            return total.astype(jnp.bfloat16)
        grouped = lax.map(group_sum, jnp.arange(groups, dtype=jnp.int32))
        output = lax.optimization_barrier(jnp.sum(grouped.astype(jnp.float32), axis=0))
        scaled = jnp.where(valid[:, None], weight[index][:, None] * output, 0.0)
        return (mixture.at[index].add(scaled), None)
    mixture, unused = lax.scan(add_expert, jnp.zeros((TOKEN_COUNT, D), jnp.float32), jnp.arange(EXPERTS, dtype=jnp.int32))
    return (resid + mixture).astype(jnp.bfloat16)
```

```python
import jax
import jax.numpy as jnp
from jax import lax
from jax.sharding import Mesh, PartitionSpec as P

HEAD_WIDTH = 128
LONGEST = 2048
GROUPS = 8
NX, NYL, NZ, NYH, NC = 4, 2, 4, 2, 2
SWAP = [(0, 1), (1, 0)]
UP = [(i, (i + 1) % NZ) for i in range(NZ)]
DOWN = [((i + 1) % NZ, i) for i in range(NZ)]


def add(*terms):
    total = terms[0].astype(jnp.float32)
    for term in terms[1:]:
        total = total + term.astype(jnp.float32)
    return total.astype(jnp.bfloat16)


def gather_keys(keys, values, doc_ids):
    tok = keys.shape[0]
    docs = jnp.pad(doc_ids.astype(jnp.bfloat16)[None, :], ((0, 15), (0, 0)))
    own = jnp.concatenate([keys, values, docs], axis=0)
    one = lax.ppermute(own, "x", [(i, i + 1) for i in range(NX - 1)])
    two = lax.ppermute(own, "x", [(i, i + 2) for i in range(NX - 2)])
    mine = jnp.concatenate([own, one, two], axis=0)
    other = lax.ppermute(mine, "yl", SWAP)
    here = jnp.concatenate([mine, other], axis=0)
    below = lax.ppermute(here, "z", UP)
    above = lax.ppermute(here, "z", DOWN)
    half = here.shape[0] // 2
    far_first = lax.ppermute(below[:half], "z", UP)
    far_second = lax.ppermute(above[half:], "z", DOWN)
    blocks = jnp.concatenate([here, below, above, far_first, far_second], axis=0)
    blocks = blocks.reshape(NZ, NYL, 3, own.shape[0], HEAD_WIDTH)
    x, yl, z = lax.axis_index("x"), lax.axis_index("yl"), lax.axis_index("z")
    at_x = x - jnp.arange(3, dtype=jnp.int32)
    at_yl = jnp.stack([yl, 1 - yl])
    at_z = (z + jnp.array([0, 3, 1, 2], jnp.int32)) % NZ
    base = (at_x[None, None, :] * NYL + at_yl[None, :, None]) * NZ + at_z[:, None, None]
    place = base[..., None] * tok + jnp.arange(tok, dtype=jnp.int32)
    place = jnp.where(at_x[None, None, :, None] >= 0, place, 1 << 30)
    key_all = blocks[..., :tok, :].reshape(-1, HEAD_WIDTH)
    value_all = blocks[..., tok : 2 * tok, :].reshape(-1, HEAD_WIDTH)
    doc_all = blocks[..., 2 * tok, :].astype(jnp.int32).reshape(-1)
    return key_all, value_all, doc_all, place.reshape(-1)


def attention(queries, keys, values, doc_ids):
    tok = queries.shape[0]
    heads = queries.shape[1] // HEAD_WIDTH
    key_all, value_all, doc_all, key_place = gather_keys(keys, values, doc_ids)
    ctx = (lax.axis_index("x") * NYL + lax.axis_index("yl")) * NZ + lax.axis_index("z")
    query_place = ctx * tok + jnp.arange(tok, dtype=jnp.int32)
    allowed = (key_place[None, :] <= query_place[:, None]) & (doc_ids[:, None] == doc_all[None, :])
    query_three = queries.reshape(tok, heads, HEAD_WIDTH)
    scores = jnp.einsum(
        "tgd,pd->gtp", query_three, key_all, preferred_element_type=jnp.float32
    ) * (HEAD_WIDTH ** (-0.5))
    masked = jnp.where(allowed, scores, -1e30)
    top = jnp.max(masked, axis=-1, keepdims=True)
    expo = jnp.where(allowed, jnp.exp(scores - top), 0.0)
    total = jnp.sum(expo, axis=-1)
    accum = jnp.einsum(
        "gtp,pd->gtd", expo.astype(jnp.bfloat16), value_all, preferred_element_type=jnp.float32
    )
    out = (accum / total[..., None]).transpose(1, 0, 2)
    return out.reshape(tok, heads * HEAD_WIDTH).astype(jnp.bfloat16)


def project(heads_out, out_proj):
    tok = heads_out.shape[0]
    weight = lax.all_gather(out_proj, ("yl", "z"), axis=1, tiled=True)
    width = weight.shape[1]
    rows = tok // (NYH * NC)
    spread = jnp.broadcast_to(heads_out[None], (NX,) + heads_out.shape)
    all_x = lax.all_to_all(spread, "x", split_axis=0, concat_axis=0, tiled=True)
    part = jnp.dot(
        all_x.reshape(NX * tok, -1), weight, preferred_element_type=jnp.float32
    ).astype(jnp.bfloat16)
    part = part.reshape(NX, NYH, NC, rows, width)
    c, yh = lax.axis_index("c"), lax.axis_index("yh")
    got = lax.ppermute(lax.dynamic_index_in_dim(part, 1 - c, 2, False), "c", SWAP)
    part = add(lax.dynamic_index_in_dim(part, c, 2, False), got)
    got = lax.ppermute(lax.dynamic_index_in_dim(part, 1 - yh, 1, False), "yh", SWAP)
    part = add(lax.dynamic_index_in_dim(part, yh, 1, False), got)
    columns = lax.all_to_all(part, "x", split_axis=0, concat_axis=0, tiled=True)
    return columns.transpose(1, 0, 2).reshape(rows, NX * width)


def expert_part(rows, w_gate, w_up, w_down):
    gate_val = jnp.dot(rows, w_gate, preferred_element_type=jnp.float32)
    up_val = jnp.dot(rows, w_up, preferred_element_type=jnp.float32)
    hidden = (jax.nn.silu(gate_val) * up_val).astype(jnp.bfloat16)
    return jnp.dot(hidden, w_down, preferred_element_type=jnp.float32).astype(jnp.bfloat16)


def spread_z(own):
    cut = own.shape[0] // 16 * 8
    below = lax.ppermute(own, "z", UP)
    above = lax.ppermute(own, "z", DOWN)
    far_first = lax.ppermute(below[:cut], "z", UP)
    far_second = lax.ppermute(above[cut:], "z", DOWN)
    return own, below, above, jnp.concatenate([far_first, far_second], axis=0)


def collect_z(own, below, above, far):
    cut = own.shape[0] // 16 * 8
    from_above = lax.ppermute(far[:cut], "z", DOWN)
    from_below = lax.ppermute(far[cut:], "z", UP)
    below = jnp.concatenate([add(below[:cut], from_above), below[cut:]], axis=0)
    above = jnp.concatenate([above[:cut], add(above[cut:], from_below)], axis=0)
    return add(own, lax.ppermute(below, "z", DOWN), lax.ppermute(above, "z", UP))


def per_device(
    stream_in,
    queries,
    rotated_key_heads,
    values,
    doc_ids,
    out_proj,
    norm_gain,
    router,
    w_gate,
    w_up,
    w_down,
    routes,
):
    heads_out = attention(queries, rotated_key_heads, values, doc_ids)
    summed = project(heads_out, out_proj)
    resid = stream_in.astype(jnp.float32) + summed.astype(jnp.float32)
    width = resid.shape[1]
    normed = (
        resid * lax.rsqrt(jnp.mean(resid * resid, axis=1, keepdims=True) + 1e-05) * norm_gain
    ).astype(jnp.bfloat16)
    logits = jnp.dot(normed.astype(jnp.float32), router, precision=lax.Precision.HIGHEST)
    experts = router.shape[1]
    rows = normed.shape[0]
    cap = rows * 9 // 32
    slots = experts * cap
    hits = routes[:, :, None] == jnp.arange(experts, dtype=jnp.int32)
    flat_hits = hits.astype(jnp.int32).reshape(rows * 2, experts)
    before = jnp.cumsum(flat_hits, axis=0) - flat_hits
    slot = jnp.sum(before.reshape(rows, 2, experts) * hits.astype(jnp.int32), axis=-1)
    target = routes * cap + slot
    placed = target[:, :, None] == jnp.arange(slots, dtype=jnp.int32)[None, None, :]
    chooser = jnp.any(placed, axis=1).astype(jnp.bfloat16).T
    pair_logits = jnp.sum(jnp.where(hits, logits[:, None, :], 0.0), axis=-1)
    first_gate = 1.0 / (1.0 + jnp.exp(pair_logits[:, 1] - pair_logits[:, 0]))
    second_gate = 1.0 / (1.0 + jnp.exp(pair_logits[:, 0] - pair_logits[:, 1]))
    gate_pair = jnp.stack([first_gate, second_gate], axis=1)
    combiner = jnp.sum(jnp.where(placed, gate_pair[:, :, None], 0.0), axis=1)

    packed = jnp.dot(chooser, normed, preferred_element_type=jnp.float32).astype(jnp.bfloat16)
    arrived = lax.all_to_all(
        packed.reshape(experts, cap, width), ("x", "yl"), split_axis=0, concat_axis=0, tiled=True
    ).reshape(slots, width)
    over = lax.ppermute(arrived, "yh", SWAP)
    blocks = spread_z(arrived) + spread_z(over)
    sent = []
    for block in blocks:
        both = jnp.concatenate([block, lax.ppermute(block, "c", SWAP)], axis=0)
        out = expert_part(both, w_gate, w_up, w_down)
        sent.append(add(out[:slots], lax.ppermute(out[slots:], "c", SWAP)))
    home = add(collect_z(*sent[:4]), lax.ppermute(collect_z(*sent[4:]), "yh", SWAP))
    returned = lax.all_to_all(
        home.reshape(experts, cap, width), ("x", "yl"), split_axis=0, concat_axis=0, tiled=True
    ).reshape(slots, width)
    mixture = jnp.dot(combiner, returned.astype(jnp.float32), precision=lax.Precision.HIGHEST)
    return (resid + mixture).astype(jnp.bfloat16)


def solution(mesh):
    fine = Mesh(mesh.devices.reshape(NX, NYL, NZ, NYH, NC), ("x", "yl", "z", "yh", "c"))
    ctx, tp = ("x", "yl", "z"), ("yh", "c")
    placed = (
        P(ctx + tp, None),
        P(ctx, tp),
        P(ctx, tp),
        P(ctx, tp),
        P(ctx),
        P(tp, ctx),
        P(),
        P(),
        P(None, ctx + tp),
        P(None, ctx + tp),
        P(ctx + tp, None),
        P(ctx + tp, None),
    )
    return jax.shard_map(
        per_device, mesh=fine, in_specs=placed, out_specs=P(ctx + tp, None), check_vma=False
    )
```

```python
import functools

import jax
import jax.numpy as jnp
from jax import lax
from jax.experimental import pallas as pl
from jax.experimental.pallas import tpu as pltpu
from jax.sharding import Mesh, PartitionSpec as P

HEAD_WIDTH = 128
LONGEST = 2048
GROUPS = 8
NX, NYL, NZ, NYH, NC = 4, 2, 4, 2, 2
SWAP = [(0, 1), (1, 0)]
UP = [(i, (i + 1) % NZ) for i in range(NZ)]
DOWN = [((i + 1) % NZ, i) for i in range(NZ)]


def add(*terms):
    total = terms[0].astype(jnp.float32)
    for term in terms[1:]:
        total = total + term.astype(jnp.float32)
    return total.astype(jnp.bfloat16)


def gather_keys(keys, values, doc_ids):
    tok = keys.shape[0]
    docs = jnp.pad(doc_ids.astype(jnp.bfloat16)[None, :], ((0, 15), (0, 0)))
    own = jnp.concatenate([keys, values, docs], axis=0)
    one = lax.ppermute(own, "x", [(i, i + 1) for i in range(NX - 1)])
    two = lax.ppermute(own, "x", [(i, i + 2) for i in range(NX - 2)])
    mine = jnp.concatenate([own, one, two], axis=0)
    other = lax.ppermute(mine, "yl", SWAP)
    here = jnp.concatenate([mine, other], axis=0)
    below = lax.ppermute(here, "z", UP)
    above = lax.ppermute(here, "z", DOWN)
    half = here.shape[0] // 2
    far_first = lax.ppermute(below[:half], "z", UP)
    far_second = lax.ppermute(above[half:], "z", DOWN)
    blocks = jnp.concatenate([here, below, above, far_first, far_second], axis=0)
    blocks = blocks.reshape(NZ, NYL, 3, own.shape[0], HEAD_WIDTH)
    x, yl, z = lax.axis_index("x"), lax.axis_index("yl"), lax.axis_index("z")
    at_x = x - jnp.arange(3, dtype=jnp.int32)
    at_yl = jnp.stack([yl, 1 - yl])
    at_z = (z + jnp.array([0, 3, 1, 2], jnp.int32)) % NZ
    base = (at_x[None, None, :] * NYL + at_yl[None, :, None]) * NZ + at_z[:, None, None]
    place = base[..., None] * tok + jnp.arange(tok, dtype=jnp.int32)
    place = jnp.where(at_x[None, None, :, None] >= 0, place, 1 << 30)
    key_all = blocks[..., :tok, :].reshape(-1, HEAD_WIDTH)
    value_all = blocks[..., tok : 2 * tok, :].reshape(-1, HEAD_WIDTH)
    doc_all = blocks[..., 2 * tok, :].astype(jnp.int32).reshape(-1)
    return key_all, value_all, doc_all, place.reshape(-1)


def attention(queries, keys, values, doc_ids):
    tok = queries.shape[0]
    heads = queries.shape[1] // HEAD_WIDTH
    key_all, value_all, doc_all, key_place = gather_keys(keys, values, doc_ids)
    ctx = (lax.axis_index("x") * NYL + lax.axis_index("yl")) * NZ + lax.axis_index("z")
    query_place = ctx * tok + jnp.arange(tok, dtype=jnp.int32)
    allowed = (key_place[None, :] <= query_place[:, None]) & (doc_ids[:, None] == doc_all[None, :])
    query_three = queries.reshape(tok, heads, HEAD_WIDTH)
    scores = jnp.einsum(
        "tgd,pd->gtp", query_three, key_all, preferred_element_type=jnp.float32
    ) * (HEAD_WIDTH ** (-0.5))
    masked = jnp.where(allowed, scores, -1e30)
    top = jnp.max(masked, axis=-1, keepdims=True)
    expo = jnp.where(allowed, jnp.exp(scores - top), 0.0)
    total = jnp.sum(expo, axis=-1)
    accum = jnp.einsum(
        "gtp,pd->gtd", expo.astype(jnp.bfloat16), value_all, preferred_element_type=jnp.float32
    )
    out = (accum / total[..., None]).transpose(1, 0, 2)
    return out.reshape(tok, heads * HEAD_WIDTH).astype(jnp.bfloat16)


def project(heads_out, out_proj):
    tok = heads_out.shape[0]
    weight = lax.all_gather(out_proj, ("yl", "z"), axis=1, tiled=True)
    width = weight.shape[1]
    rows = tok // (NYH * NC)
    spread = jnp.broadcast_to(heads_out[None], (NX,) + heads_out.shape)
    all_x = lax.all_to_all(spread, "x", split_axis=0, concat_axis=0, tiled=True)
    part = jnp.dot(
        all_x.reshape(NX * tok, -1), weight, preferred_element_type=jnp.float32
    ).astype(jnp.bfloat16)
    part = part.reshape(NX, NYH, NC, rows, width)
    c, yh = lax.axis_index("c"), lax.axis_index("yh")
    got = lax.ppermute(lax.dynamic_index_in_dim(part, 1 - c, 2, False), "c", SWAP)
    part = add(lax.dynamic_index_in_dim(part, c, 2, False), got)
    got = lax.ppermute(lax.dynamic_index_in_dim(part, 1 - yh, 1, False), "yh", SWAP)
    part = add(lax.dynamic_index_in_dim(part, yh, 1, False), got)
    columns = lax.all_to_all(part, "x", split_axis=0, concat_axis=0, tiled=True)
    return columns.transpose(1, 0, 2).reshape(rows, NX * width)


def expert_kernel(count, core_ref, *refs):
    own, other = refs[:count], refs[count : 2 * count]
    gate_w, up_w, down_w = refs[2 * count : 2 * count + 3]
    send, keep = refs[2 * count + 3 : 3 * count + 3], refs[3 * count + 3 : 4 * count + 3]
    gate_sum, up_sum, hidden = refs[4 * count + 3 :]
    step = pl.program_id(0)
    high = own[0].shape[0]

    def contract(parts, first):
        for i, part in enumerate(parts):
            at = pl.ds(i * high, high)
            gate = jnp.dot(part[...], gate_w[...], preferred_element_type=jnp.float32)
            up = jnp.dot(part[...], up_w[...], preferred_element_type=jnp.float32)
            if first:
                gate_sum[at], up_sum[at] = gate, up
            else:
                gate_sum[at] += gate
                up_sum[at] += up

    def expand(outs):
        value = jnp.dot(hidden[...], down_w[...], preferred_element_type=jnp.float32)
        for i, out in enumerate(outs):
            out[...] = value[i * high : (i + 1) * high].astype(out.dtype)

    @pl.when(step == 0)
    def _():
        contract(own, True)

    @pl.when(step == 1)
    def _():
        contract(own, False)

    @pl.when((step == 2) | (step == 3))
    def _():
        contract(other, False)

    @pl.when(step == 3)
    def _():
        gate = gate_sum[...]
        hidden[...] = (gate / (1.0 + jnp.exp(-gate)) * up_sum[...]).astype(hidden.dtype)

    @pl.when((step == 4) | (step == 5))
    def _():
        expand(send)

    @pl.when(step >= 6)
    def _():
        expand(keep)


def expert_part(core, own, other, w_gate, w_up, w_down):
    count = len(own)
    high, half = own[0].shape
    quarter = half // 2
    units = w_gate.shape[1]

    def place(first):
        return pl.BlockSpec((high, quarter), lambda s, c: (0, jnp.clip(s - first, 0, 1)))

    def in_quarter(s, c):
        s = jnp.minimum(s, 3)
        return jnp.where(s < 2, 2 * c[0] + s, 2 * (1 - c[0]) + s - 2)

    def out_quarter(s, c):
        s = jnp.maximum(s, 4) - 4
        return jnp.where(s < 2, 2 * (1 - c[0]) + s, 2 * c[0] + s - 2)

    rows = count * high
    outs = pl.pallas_call(
        functools.partial(expert_kernel, count),
        grid_spec=pltpu.PrefetchScalarGridSpec(
            num_scalar_prefetch=1,
            grid=(8,),
            in_specs=[place(0)] * count
            + [place(2)] * count
            + [
                pl.BlockSpec((quarter, units), lambda s, c: (in_quarter(s, c), 0)),
                pl.BlockSpec((quarter, units), lambda s, c: (in_quarter(s, c), 0)),
                pl.BlockSpec((units, quarter), lambda s, c: (0, out_quarter(s, c))),
            ],
            out_specs=[place(4)] * count + [place(6)] * count,
            scratch_shapes=[
                pltpu.VMEM((rows, units), jnp.float32),
                pltpu.VMEM((rows, units), jnp.float32),
                pltpu.VMEM((rows, units), jnp.bfloat16),
            ],
        ),
        out_shape=[jax.ShapeDtypeStruct((high, half), jnp.bfloat16)] * (2 * count),
        compiler_params=pltpu.CompilerParams(vmem_limit_bytes=48 * 1024 * 1024),
        cost_estimate=pl.CostEstimate(
            flops=6 * rows * 2 * half * units,
            bytes_accessed=12 * half * units + 8 * rows * half,
            transcendentals=rows * units,
        ),
        name="expert_part",
    )(core, *own, *other, w_gate, w_up, w_down)
    return outs[:count], outs[count:]


def after(value, *others):
    return lax.optimization_barrier((value, *others))[0]


def experts_of(own, w_gate, w_up, w_down):
    cut = own.shape[0] // 32 * 16
    c = lax.axis_index("c").astype(jnp.int32).reshape(1)

    def run(*blocks):
        other = [lax.ppermute(block, "c", SWAP) for block in blocks]
        send, keep = expert_part(c, blocks, other, w_gate, w_up, w_down)
        return [add(mine, lax.ppermute(his, "c", SWAP)) for mine, his in zip(keep, send)]

    def near(block):
        return lax.ppermute(block, "z", UP), lax.ppermute(block, "z", DOWN)

    def far(below, above):
        return jnp.concatenate(
            [lax.ppermute(below[:cut], "z", UP), lax.ppermute(above[cut:], "z", DOWN)], axis=0
        )

    def far_back(block):
        return lax.ppermute(block[:cut], "z", DOWN), lax.ppermute(block[cut:], "z", UP)

    def near_back(below, above, from_above, from_below):
        below = jnp.concatenate([add(below[:cut], from_above), below[cut:]], axis=0)
        above = jnp.concatenate([above[:cut], add(above[cut:], from_below)], axis=0)
        return lax.ppermute(below, "z", DOWN), lax.ppermute(above, "z", UP)

    over = lax.ppermute(own, "yh", SWAP)
    below, above = near(own)
    far_own = far(below, above)
    over_below, over_above = near(after(over, below, above))
    far_over = far(over_below, over_above)
    own, below, above = run(own, below, above)
    far_own, over = run(far_own, over)
    over_below, over_above = run(over_below, over_above)
    (far_over,) = run(far_over)
    own_far_back = far_back(far_own)
    over_far_back = far_back(after(far_over, *own_far_back))
    over_back = near_back(over_below, over_above, *over_far_back)
    own_back = near_back(after(below, *over_back), above, *own_far_back)
    over = lax.ppermute(add(over, *over_back), "yh", SWAP)
    return add(own, *own_back, over)


def per_device(
    stream_in,
    queries,
    rotated_key_heads,
    values,
    doc_ids,
    out_proj,
    norm_gain,
    router,
    w_gate,
    w_up,
    w_down,
    routes,
):
    heads_out = attention(queries, rotated_key_heads, values, doc_ids)
    summed = project(heads_out, out_proj)
    resid = stream_in.astype(jnp.float32) + summed.astype(jnp.float32)
    width = resid.shape[1]
    normed = (
        resid * lax.rsqrt(jnp.mean(resid * resid, axis=1, keepdims=True) + 1e-05) * norm_gain
    ).astype(jnp.bfloat16)
    logits = jnp.dot(normed.astype(jnp.float32), router, precision=lax.Precision.HIGHEST)
    experts = router.shape[1]
    rows = normed.shape[0]
    cap = 2 * rows * 9 // 32
    slots = experts * cap
    c = lax.axis_index("c")
    half = width // 2

    def columns(array, core):
        return lax.dynamic_slice_in_dim(array, core * half, half, axis=1)

    def in_order(mine, his, axis):
        return jnp.where(
            c == 0,
            jnp.concatenate([mine, his], axis=axis),
            jnp.concatenate([his, mine], axis=axis),
        )

    pair_routes = in_order(routes, lax.ppermute(routes, "c", SWAP), 0)
    pair_normed = in_order(columns(normed, c), lax.ppermute(columns(normed, 1 - c), "c", SWAP), 0)
    rows2 = 2 * rows
    hits = pair_routes[:, :, None] == jnp.arange(experts, dtype=jnp.int32)
    flat_hits = hits.astype(jnp.int32).reshape(rows2 * 2, experts)
    before = jnp.cumsum(flat_hits, axis=0) - flat_hits
    slot = jnp.sum(before.reshape(rows2, 2, experts) * hits.astype(jnp.int32), axis=-1)
    target = pair_routes * cap + slot
    placed = target[:, :, None] == jnp.arange(slots, dtype=jnp.int32)[None, None, :]
    chooser = jnp.any(placed, axis=1).astype(jnp.bfloat16).T
    own_hits = routes[:, :, None] == jnp.arange(experts, dtype=jnp.int32)
    pair_logits = jnp.sum(jnp.where(own_hits, logits[:, None, :], 0.0), axis=-1)
    first_gate = 1.0 / (1.0 + jnp.exp(pair_logits[:, 1] - pair_logits[:, 0]))
    second_gate = 1.0 / (1.0 + jnp.exp(pair_logits[:, 0] - pair_logits[:, 1]))
    own_gates = jnp.stack([first_gate, second_gate], axis=1)
    gate_pair = in_order(own_gates, lax.ppermute(own_gates, "c", SWAP), 0)
    combiner = jnp.sum(jnp.where(placed, gate_pair[:, :, None], 0.0), axis=1)

    packed = jnp.dot(chooser, pair_normed, preferred_element_type=jnp.float32).astype(jnp.bfloat16)
    arrived = lax.all_to_all(
        packed.reshape(experts, cap, half), ("x", "yl"), split_axis=0, concat_axis=0, tiled=True
    ).reshape(slots, half)
    home = experts_of(arrived, w_gate, w_up, w_down)
    returned = lax.all_to_all(
        home.reshape(experts, cap, half), ("x", "yl"), split_axis=0, concat_axis=0, tiled=True
    ).reshape(slots, half)
    mixture = jnp.dot(combiner, returned.astype(jnp.float32), precision=lax.Precision.HIGHEST)
    mine = lax.dynamic_slice_in_dim(mixture, c * rows, rows, axis=0)
    his = lax.dynamic_slice_in_dim(mixture, (1 - c) * rows, rows, axis=0)
    mixture = in_order(mine, lax.ppermute(his, "c", SWAP), 1)
    return (resid + mixture).astype(jnp.bfloat16)


def solution(mesh):
    fine = Mesh(mesh.devices.reshape(NX, NYL, NZ, NYH, NC), ("x", "yl", "z", "yh", "c"))
    ctx, tp = ("x", "yl", "z"), ("yh", "c")
    placed = (
        P(ctx + tp, None),
        P(ctx, tp),
        P(ctx, tp),
        P(ctx, tp),
        P(ctx),
        P(tp, ctx),
        P(),
        P(),
        P(None, ctx + tp),
        P(None, ctx + tp),
        P(ctx + tp, None),
        P(ctx + tp, None),
    )
    return jax.shard_map(
        per_device, mesh=fine, in_specs=placed, out_specs=P(ctx + tp, None), check_vma=False
    )
```

```python
import functools

import jax
import jax.numpy as jnp
from jax import lax
from jax.experimental import pallas as pl
from jax.experimental.pallas import tpu as pltpu
from jax.sharding import Mesh, PartitionSpec as P

HEAD_WIDTH = 128
LONGEST = 2048
GROUPS = 8
NX, NYL, NZ, NYH, NC = 4, 2, 4, 2, 2
SWAP = [(0, 1), (1, 0)]
UP = [(i, (i + 1) % NZ) for i in range(NZ)]
DOWN = [((i + 1) % NZ, i) for i in range(NZ)]


def add(*terms):
    total = terms[0].astype(jnp.float32)
    for term in terms[1:]:
        total = total + term.astype(jnp.float32)
    return total.astype(jnp.bfloat16)


def gather_keys(keys, values, doc_ids):
    tok = keys.shape[0]
    docs = jnp.pad(doc_ids.astype(jnp.bfloat16)[None, :], ((0, 15), (0, 0)))
    own = jnp.concatenate([keys, values, docs], axis=0)
    pieces = [own]
    for flip in range(NYL):
        for back in range(3):
            if flip or back:
                route = [
                    (x * NYL + yl, (x + back) * NYL + (yl ^ flip))
                    for x in range(NX - back)
                    for yl in range(NYL)
                ]
                pieces.append(lax.ppermute(own, ("x", "yl"), route))
    here = jnp.concatenate(pieces, axis=0)
    below = lax.ppermute(here, "z", UP)
    above = lax.ppermute(here, "z", DOWN)
    half = here.shape[0] // 2
    far_first = lax.ppermute(below[:half], "z", UP)
    far_second = lax.ppermute(above[half:], "z", DOWN)
    blocks = jnp.concatenate([here, below, above, far_first, far_second], axis=0)
    blocks = blocks.reshape(NZ, NYL, 3, own.shape[0], HEAD_WIDTH)
    x, yl, z = lax.axis_index("x"), lax.axis_index("yl"), lax.axis_index("z")
    at_x = x - jnp.arange(3, dtype=jnp.int32)
    at_yl = jnp.stack([yl, 1 - yl])
    at_z = (z + jnp.array([0, 3, 1, 2], jnp.int32)) % NZ
    base = (at_x[None, None, :] * NYL + at_yl[None, :, None]) * NZ + at_z[:, None, None]
    place = base[..., None] * tok + jnp.arange(tok, dtype=jnp.int32)
    place = jnp.where(at_x[None, None, :, None] >= 0, place, 1 << 30)
    key_all = blocks[..., :tok, :].reshape(-1, HEAD_WIDTH)
    value_all = blocks[..., tok : 2 * tok, :].reshape(-1, HEAD_WIDTH)
    doc_all = blocks[..., 2 * tok, :].astype(jnp.int32).reshape(-1)
    return key_all, value_all, doc_all, place.reshape(-1)


def attention(queries, keys, values, doc_ids):
    tok = queries.shape[0]
    heads = queries.shape[1] // HEAD_WIDTH
    key_all, value_all, doc_all, key_place = gather_keys(keys, values, doc_ids)
    ctx = (lax.axis_index("x") * NYL + lax.axis_index("yl")) * NZ + lax.axis_index("z")
    query_place = ctx * tok + jnp.arange(tok, dtype=jnp.int32)
    allowed = (key_place[None, :] <= query_place[:, None]) & (doc_ids[:, None] == doc_all[None, :])
    query_three = queries.reshape(tok, heads, HEAD_WIDTH)
    scores = jnp.einsum(
        "tgd,pd->gtp", query_three, key_all, preferred_element_type=jnp.float32
    ) * (HEAD_WIDTH ** (-0.5))
    masked = jnp.where(allowed, scores, -1e30)
    top = jnp.max(masked, axis=-1, keepdims=True)
    expo = jnp.where(allowed, jnp.exp(scores - top), 0.0)
    total = jnp.sum(expo, axis=-1)
    accum = jnp.einsum(
        "gtp,pd->gtd", expo.astype(jnp.bfloat16), value_all, preferred_element_type=jnp.float32
    )
    out = (accum / total[..., None]).transpose(1, 0, 2)
    return out.reshape(tok, heads * HEAD_WIDTH).astype(jnp.bfloat16)


def project(heads_out, out_proj):
    tok = heads_out.shape[0]
    depth = out_proj.shape[1]
    weight = lax.all_gather(out_proj, ("x", "yl"), axis=1, tiled=True)
    width = weight.shape[1]
    rows = tok // (NYH * NC)
    spread = jnp.broadcast_to(heads_out[None], (NZ,) + heads_out.shape)
    all_z = lax.all_to_all(spread, "z", split_axis=0, concat_axis=0, tiled=True)
    part = jnp.dot(
        all_z.reshape(NZ * tok, -1), weight, preferred_element_type=jnp.float32
    ).astype(jnp.bfloat16)
    part = part.reshape(NZ, NYH, NC, rows, width)
    c = lax.axis_index("c")
    got = lax.ppermute(lax.dynamic_index_in_dim(part, 1 - c, 2, False), "c", SWAP)
    part = add(lax.dynamic_index_in_dim(part, c, 2, False), got)
    part = lax.all_to_all(
        part.reshape(NZ * NYH, rows, width), ("z", "yh"), split_axis=0, concat_axis=0, tiled=True
    )
    part = part.reshape(NZ, NYH, rows, NX * NYL, depth)
    total = part[:, 0].astype(jnp.float32) + part[:, 1].astype(jnp.float32)
    return total.transpose(1, 2, 0, 3).reshape(rows, NX * NYL * NZ * depth)


def expert_kernel(count, core_ref, *refs):
    own, other = refs[:count], refs[count : 2 * count]
    gate_w, up_w, down_w = refs[2 * count : 2 * count + 3]
    send, keep = refs[2 * count + 3 : 3 * count + 3], refs[3 * count + 3 : 4 * count + 3]
    gate_sum, up_sum, hidden = refs[4 * count + 3 :]
    step = pl.program_id(0)
    high = own[0].shape[0]

    def contract(parts, first):
        rows = jnp.concatenate([part[...] for part in parts], axis=0)
        gate = jnp.dot(rows, gate_w[...], preferred_element_type=jnp.float32)
        up = jnp.dot(rows, up_w[...], preferred_element_type=jnp.float32)
        if first:
            gate_sum[...], up_sum[...] = gate, up
        else:
            gate_sum[...] += gate
            up_sum[...] += up

    def expand(outs):
        value = jnp.dot(hidden[...], down_w[...], preferred_element_type=jnp.float32)
        for i, out in enumerate(outs):
            out[...] = value[i * high : (i + 1) * high].astype(out.dtype)

    @pl.when(step == 0)
    def _():
        contract(own, True)

    @pl.when(step == 1)
    def _():
        contract(own, False)

    @pl.when((step == 2) | (step == 3))
    def _():
        contract(other, False)

    @pl.when(step == 3)
    def _():
        gate = gate_sum[...]
        hidden[...] = (gate / (1.0 + jnp.exp(-gate)) * up_sum[...]).astype(hidden.dtype)

    @pl.when((step == 4) | (step == 5))
    def _():
        expand(send)

    @pl.when(step >= 6)
    def _():
        expand(keep)


def expert_part(core, own, other, w_gate, w_up, w_down):
    count = len(own)
    high, half = own[0].shape
    quarter = half // 2
    units = w_gate.shape[1]

    def place(first):
        return pl.BlockSpec((high, quarter), lambda s, c: (0, jnp.clip(s - first, 0, 1)))

    def in_quarter(s, c):
        s = jnp.minimum(s, 3)
        return jnp.where(s < 2, 2 * c[0] + s, 2 * (1 - c[0]) + s - 2)

    def out_quarter(s, c):
        s = jnp.maximum(s, 4) - 4
        return jnp.where(s < 2, 2 * (1 - c[0]) + s, 2 * c[0] + s - 2)

    rows = count * high
    outs = pl.pallas_call(
        functools.partial(expert_kernel, count),
        grid_spec=pltpu.PrefetchScalarGridSpec(
            num_scalar_prefetch=1,
            grid=(8,),
            in_specs=[place(0)] * count
            + [place(2)] * count
            + [
                pl.BlockSpec((quarter, units), lambda s, c: (in_quarter(s, c), 0)),
                pl.BlockSpec((quarter, units), lambda s, c: (in_quarter(s, c), 0)),
                pl.BlockSpec((units, quarter), lambda s, c: (0, out_quarter(s, c))),
            ],
            out_specs=[place(4)] * count + [place(6)] * count,
            scratch_shapes=[
                pltpu.VMEM((rows, units), jnp.float32),
                pltpu.VMEM((rows, units), jnp.float32),
                pltpu.VMEM((rows, units), jnp.bfloat16),
            ],
        ),
        out_shape=[jax.ShapeDtypeStruct((high, half), jnp.bfloat16)] * (2 * count),
        compiler_params=pltpu.CompilerParams(vmem_limit_bytes=48 * 1024 * 1024),
        cost_estimate=pl.CostEstimate(
            flops=6 * rows * 2 * half * units,
            bytes_accessed=12 * half * units + 8 * rows * half,
            transcendentals=rows * units,
        ),
        name="expert_part",
    )(core, *own, *other, w_gate, w_up, w_down)
    return outs[:count], outs[count:]


def after(value, *others):
    return lax.optimization_barrier((value, *others))[0]


def experts_of(own, w_gate, w_up, w_down):
    cut = own.shape[0] // 32 * 16
    c = lax.axis_index("c").astype(jnp.int32).reshape(1)

    def run(*blocks):
        other = [lax.ppermute(block, "c", SWAP) for block in blocks]
        send, keep = expert_part(c, blocks, other, w_gate, w_up, w_down)
        return [add(mine, lax.ppermute(his, "c", SWAP)) for mine, his in zip(keep, send)]

    def near(block):
        return lax.ppermute(block, "z", UP), lax.ppermute(block, "z", DOWN)

    def far(below, above):
        return jnp.concatenate(
            [lax.ppermute(below[:cut], "z", UP), lax.ppermute(above[cut:], "z", DOWN)], axis=0
        )

    def far_back(block):
        return lax.ppermute(block[:cut], "z", DOWN), lax.ppermute(block[cut:], "z", UP)

    def near_back(below, above, from_above, from_below):
        below = jnp.concatenate([add(below[:cut], from_above), below[cut:]], axis=0)
        above = jnp.concatenate([above[:cut], add(above[cut:], from_below)], axis=0)
        return lax.ppermute(below, "z", DOWN), lax.ppermute(above, "z", UP)

    over = lax.ppermute(own, "yh", SWAP)
    below, above = near(own)
    over_below, over_above = near(after(over, below, above))
    far_own = far(below, above)
    own, below, above = run(own, below, above)
    far_over = far(*lax.optimization_barrier((over_below, over_above, own))[:2])
    far_own, over = run(far_own, over)
    over_below, over_above, far_over = run(over_below, over_above, after(far_over, far_own))
    own_far_back = far_back(far_own)
    over_far_back = far_back(after(far_over, *own_far_back))
    over_back = near_back(over_below, over_above, *over_far_back)
    own_back = near_back(after(below, *over_back), above, *own_far_back)
    over = lax.ppermute(add(over, *over_back), "yh", SWAP)
    return add(own, *own_back, over)


def per_device(
    stream_in,
    queries,
    rotated_key_heads,
    values,
    doc_ids,
    out_proj,
    norm_gain,
    router,
    w_gate,
    w_up,
    w_down,
    routes,
):
    heads_out = attention(queries, rotated_key_heads, values, doc_ids)
    summed = project(heads_out, out_proj)
    resid = stream_in.astype(jnp.float32) + summed.astype(jnp.float32)
    width = resid.shape[1]
    normed = (
        resid * lax.rsqrt(jnp.mean(resid * resid, axis=1, keepdims=True) + 1e-05) * norm_gain
    ).astype(jnp.bfloat16)
    logits = jnp.dot(normed.astype(jnp.float32), router, precision=lax.Precision.HIGHEST)
    experts = router.shape[1]
    rows = normed.shape[0]
    cap = 2 * rows * 9 // 32
    slots = experts * cap
    c = lax.axis_index("c")
    half = width // 2

    def columns(array, core):
        return lax.dynamic_slice_in_dim(array, core * half, half, axis=1)

    def in_order(mine, his, axis):
        return jnp.where(
            c == 0,
            jnp.concatenate([mine, his], axis=axis),
            jnp.concatenate([his, mine], axis=axis),
        )

    pair_routes = in_order(routes, lax.ppermute(routes, "c", SWAP), 0)
    pair_normed = in_order(columns(normed, c), lax.ppermute(columns(normed, 1 - c), "c", SWAP), 0)
    rows2 = 2 * rows
    hits = pair_routes[:, :, None] == jnp.arange(experts, dtype=jnp.int32)
    flat_hits = hits.astype(jnp.int32).reshape(rows2 * 2, experts)
    before = jnp.cumsum(flat_hits, axis=0) - flat_hits
    slot = jnp.sum(before.reshape(rows2, 2, experts) * hits.astype(jnp.int32), axis=-1)
    target = pair_routes * cap + slot
    placed = target[:, :, None] == jnp.arange(slots, dtype=jnp.int32)[None, None, :]
    chooser = jnp.any(placed, axis=1).astype(jnp.bfloat16).T
    own_hits = routes[:, :, None] == jnp.arange(experts, dtype=jnp.int32)
    pair_logits = jnp.sum(jnp.where(own_hits, logits[:, None, :], 0.0), axis=-1)
    first_gate = 1.0 / (1.0 + jnp.exp(pair_logits[:, 1] - pair_logits[:, 0]))
    second_gate = 1.0 / (1.0 + jnp.exp(pair_logits[:, 0] - pair_logits[:, 1]))
    own_gates = jnp.stack([first_gate, second_gate], axis=1)
    gate_pair = in_order(own_gates, lax.ppermute(own_gates, "c", SWAP), 0)
    combiner = jnp.sum(jnp.where(placed, gate_pair[:, :, None], 0.0), axis=1)

    packed = jnp.dot(chooser, pair_normed, preferred_element_type=jnp.float32).astype(jnp.bfloat16)
    arrived = lax.all_to_all(
        packed.reshape(experts, cap, half), ("x", "yl"), split_axis=0, concat_axis=0, tiled=True
    ).reshape(slots, half)
    home = experts_of(arrived, w_gate, w_up, w_down)
    returned = lax.all_to_all(
        home.reshape(experts, cap, half), ("x", "yl"), split_axis=0, concat_axis=0, tiled=True
    ).reshape(slots, half)
    mixture = jnp.dot(combiner, returned.astype(jnp.float32), precision=lax.Precision.HIGHEST)
    mine = lax.dynamic_slice_in_dim(mixture, c * rows, rows, axis=0)
    his = lax.dynamic_slice_in_dim(mixture, (1 - c) * rows, rows, axis=0)
    mixture = in_order(mine, lax.ppermute(his, "c", SWAP), 1)
    return (resid + mixture).astype(jnp.bfloat16)


def solution(mesh):
    fine = Mesh(mesh.devices.reshape(NX, NYL, NZ, NYH, NC), ("x", "yl", "z", "yh", "c"))
    ctx, tp = ("x", "yl", "z"), ("yh", "c")
    placed = (
        P(ctx + tp, None),
        P(ctx, tp),
        P(ctx, tp),
        P(ctx, tp),
        P(ctx),
        P(tp, ctx),
        P(),
        P(),
        P(None, ctx + tp),
        P(None, ctx + tp),
        P(ctx + tp, None),
        P(ctx + tp, None),
    )
    return jax.shard_map(
        per_device, mesh=fine, in_specs=placed, out_specs=P(ctx + tp, None), check_vma=False
    )
```

```python
import functools

import jax
import jax.numpy as jnp
from jax import lax
from jax.experimental import pallas as pl
from jax.experimental.pallas import tpu as pltpu
from jax.sharding import Mesh, PartitionSpec as P

HEAD_WIDTH = 128
NX, NYL, NZ, NYH, NC = 4, 2, 4, 2, 2
SWAP = [(0, 1), (1, 0)]
UP = [(i, (i + 1) % NZ) for i in range(NZ)]
DOWN = [((i + 1) % NZ, i) for i in range(NZ)]


def add(*terms):
    total = terms[0].astype(jnp.float32)
    for term in terms[1:]:
        total = total + term.astype(jnp.float32)
    return total.astype(jnp.bfloat16)


def after(value, *others):
    return lax.optimization_barrier((value, *others))[0]


def from_behind(array, back, flip):
    route = [
        (x * NYL + yl, (x + back) * NYL + (yl ^ flip)) for x in range(NX - back) for yl in range(NYL)
    ]
    return lax.ppermute(array, ("x", "yl"), route)


def gather_keys(keys, values, doc_ids):
    tok = keys.shape[0]
    docs = jnp.pad(doc_ids.astype(jnp.bfloat16)[None, :], ((0, 15), (0, 0)))
    own = jnp.concatenate([keys, values, docs], axis=0)
    order = [(flip, back) for flip in range(NYL) for back in range(3)]
    pieces = [from_behind(own, back, flip) if flip or back else own for flip, back in order]
    here = jnp.concatenate(pieces, axis=0)
    below = lax.ppermute(here, "z", UP)
    above = lax.ppermute(here, "z", DOWN)
    half = here.shape[0] // 2
    far_first = lax.ppermute(below[:half], "z", UP)
    far_second = lax.ppermute(above[half:], "z", DOWN)
    x, yl, z = lax.axis_index("x"), lax.axis_index("yl"), lax.axis_index("z")
    at_x = x - jnp.arange(3, dtype=jnp.int32)
    at_yl = jnp.stack([yl, 1 - yl])
    at_z = (z + jnp.array([0, 3, 1, 2], jnp.int32)) % NZ
    base = (at_x[None, None, :] * NYL + at_yl[None, :, None]) * NZ + at_z[:, None, None]
    base = jnp.where(at_x[None, None, :] >= 0, base * tok, 1 << 30).reshape(-1)
    own_base = ((x * NYL + yl) * NZ + z) * tok
    return (here, below, above, far_first, far_second), jnp.append(base, own_base)


def attention_kernel(base, query, query_doc, here, below, above, far_a, far_b, out, *scratch):
    rows, keys, vals, bias, scores, peak, total, accum = scratch
    tok = query.shape[0]
    heads = query.shape[1] // HEAD_WIDTH
    width = HEAD_WIDTH
    step = here.shape[0] // 6
    blocks = [(ref, i * step) for ref in (here, below, above) for i in range(6)]
    blocks += [(ref, i * step) for ref in (far_a, far_b) for i in range(3)]
    count = len(blocks)
    wide = 4 * tok
    for h in range(heads):
        rows[h * tok : (h + 1) * tok] = query[:, h * width : (h + 1) * width]
    query_at = base[count] + lax.broadcasted_iota(jnp.int32, (tok, tok), 0)
    lane = lax.broadcasted_iota(jnp.int32, (tok, tok), 1)
    for i, (ref, first) in enumerate(blocks):
        keys[i * tok : (i + 1) * tok] = ref[first : first + tok]
        vals[i * tok : (i + 1) * tok] = ref[first + tok : first + 2 * tok]
        docs = ref[first + 2 * tok : first + step].astype(jnp.float32)[0:1]
        allowed = (docs == query_doc[...]) & (base[i] + lane <= query_at)
        bias[i // 4, :, (i % 4) * tok : (i % 4 + 1) * tok] = jnp.where(allowed, 0.0, -1e30)
    peak[...] = jnp.full(peak.shape, -1e30, jnp.float32)
    total[...] = jnp.zeros_like(total)
    accum[...] = jnp.zeros_like(accum)

    def lanes(array):
        return [array[:, i * width : (i + 1) * width] for i in range(wide // width)]

    @pl.loop(0, count // 4)
    def _(i):
        at = pl.ds(pl.multiple_of(i * wide, wide), wide)
        value = lax.dot_general(
            rows[...], keys[at], (((1,), (1,)), ((), ())), preferred_element_type=jnp.float32
        )
        value = value.reshape(heads, tok, wide) * (width ** (-0.5)) + bias[i][None]
        value = value.reshape(heads * tok, wide)
        scores[i] = value
        peak[...] = functools.reduce(jnp.maximum, lanes(value), peak[...])

    top = jnp.max(peak[...], axis=1, keepdims=True)
    peak[...] = jnp.broadcast_to(top, peak.shape)

    @pl.loop(0, count // 4)
    def _(i):
        at = pl.ds(pl.multiple_of(i * wide, wide), wide)
        expo = jnp.exp(scores[i] - jnp.concatenate([peak[...]] * (wide // width), axis=1))
        total[...] = functools.reduce(jnp.add, lanes(expo), total[...])
        accum[...] += jnp.dot(
            expo.astype(jnp.bfloat16), vals[at], preferred_element_type=jnp.float32
        )

    result = accum[...] / jnp.sum(total[...], axis=1, keepdims=True)
    for h in range(heads):
        out[:, h * width : (h + 1) * width] = result[h * tok : (h + 1) * tok].astype(out.dtype)


def attention(queries, keys, values, doc_ids):
    tok, columns = queries.shape
    heads = columns // HEAD_WIDTH
    arrays, base = gather_keys(keys, values, doc_ids)
    whole = pl.BlockSpec(memory_space=pltpu.VMEM)
    return pl.pallas_call(
        attention_kernel,
        in_specs=[pl.BlockSpec(memory_space=pltpu.SMEM)] + [whole] * 7,
        out_specs=whole,
        out_shape=jax.ShapeDtypeStruct(queries.shape, jnp.bfloat16),
        scratch_shapes=[
            pltpu.VMEM((heads * tok, HEAD_WIDTH), jnp.bfloat16),
            pltpu.VMEM((24 * tok, HEAD_WIDTH), jnp.bfloat16),
            pltpu.VMEM((24 * tok, HEAD_WIDTH), jnp.bfloat16),
            pltpu.VMEM((6, tok, 4 * tok), jnp.float32),
            pltpu.VMEM((6, heads * tok, 4 * tok), jnp.float32),
            pltpu.VMEM((heads * tok, HEAD_WIDTH), jnp.float32),
            pltpu.VMEM((heads * tok, HEAD_WIDTH), jnp.float32),
            pltpu.VMEM((heads * tok, HEAD_WIDTH), jnp.float32),
        ],
        compiler_params=pltpu.CompilerParams(vmem_limit_bytes=40 * 1024 * 1024),
        cost_estimate=pl.CostEstimate(
            flops=4 * heads * tok * 24 * tok * HEAD_WIDTH,
            bytes_accessed=4 * 24 * tok * HEAD_WIDTH,
            transcendentals=heads * tok * 24 * tok,
        ),
        name="attention",
    )(base, queries, doc_ids.astype(jnp.float32)[:, None], *arrays), arrays[0]


def gather_projection(out_proj):
    own = out_proj.T
    x, yl = lax.axis_index("x"), lax.axis_index("yl")
    held = jnp.zeros((NX * NYL,) + own.shape, own.dtype)
    for back in range(NX):
        for flip in range(NYL):
            route = [
                (i * NYL + j, (i + back) % NX * NYL + (j ^ flip))
                for i in range(NX)
                for j in range(NYL)
            ]
            piece = lax.ppermute(own, ("x", "yl"), route) if back or flip else own
            at = (x - back) % NX * NYL + (yl ^ flip)
            held = lax.dynamic_update_index_in_dim(held, piece, at, 0)
    return held.reshape(NX * NYL * own.shape[0], own.shape[1])


def project(heads_out, weight):
    tok = heads_out.shape[0]
    width = weight.shape[0]
    depth = width // (NX * NYL)
    rows = tok // (NYH * NC)
    spread = jnp.broadcast_to(heads_out[None], (NZ,) + heads_out.shape)
    all_z = lax.all_to_all(spread, "z", split_axis=0, concat_axis=0, tiled=True)
    part = lax.dot_general(
        all_z.reshape(NZ * tok, -1),
        weight,
        (((1,), (1,)), ((), ())),
        preferred_element_type=jnp.float32,
    ).astype(jnp.bfloat16)
    part = part.reshape(NZ, NYH, NC, rows, width)
    c = lax.axis_index("c")
    got = lax.ppermute(lax.dynamic_index_in_dim(part, 1 - c, 2, False), "c", SWAP)
    part = add(lax.dynamic_index_in_dim(part, c, 2, False), got)
    part = lax.all_to_all(
        part.reshape(NZ * NYH, rows, width), ("z", "yh"), split_axis=0, concat_axis=0, tiled=True
    )
    part = part.reshape(NZ, NYH, rows, NX * NYL, depth)
    total = part[:, 0].astype(jnp.float32) + part[:, 1].astype(jnp.float32)
    return total.transpose(1, 2, 0, 3).reshape(rows, NX * NYL * NZ * depth)


def expert_kernel(count, core_ref, *refs):
    own, other = refs[:count], refs[count : 2 * count]
    gate_w, up_w, down_w = refs[2 * count : 2 * count + 3]
    send, keep = refs[2 * count + 3 : 3 * count + 3], refs[3 * count + 3 : 4 * count + 3]
    gate_sum, up_sum, hidden = refs[4 * count + 3 :]
    step = pl.program_id(0)
    high = own[0].shape[0]

    def contract(parts, first):
        rows = jnp.concatenate([part[...] for part in parts], axis=0)
        gate = jnp.dot(rows, gate_w[...], preferred_element_type=jnp.float32)
        up = jnp.dot(rows, up_w[...], preferred_element_type=jnp.float32)
        if first:
            gate_sum[...], up_sum[...] = gate, up
        else:
            gate_sum[...] += gate
            up_sum[...] += up

    def expand(outs):
        value = jnp.dot(hidden[...], down_w[...], preferred_element_type=jnp.float32)
        for i, out in enumerate(outs):
            out[...] = value[i * high : (i + 1) * high].astype(out.dtype)

    @pl.when(step == 0)
    def _():
        contract(own, True)

    @pl.when(step == 1)
    def _():
        contract(own, False)

    @pl.when((step == 2) | (step == 3))
    def _():
        contract(other, False)

    @pl.when(step == 3)
    def _():
        gate = gate_sum[...]
        hidden[...] = (gate / (1.0 + jnp.exp(-gate)) * up_sum[...]).astype(hidden.dtype)

    @pl.when((step == 4) | (step == 5))
    def _():
        expand(send)

    @pl.when(step >= 6)
    def _():
        expand(keep)


def expert_part(core, own, other, w_gate, w_up, w_down):
    count = len(own)
    high, half = own[0].shape
    quarter = half // 2
    units = w_gate.shape[1]

    def place(first):
        return pl.BlockSpec((high, quarter), lambda s, c: (0, jnp.clip(s - first, 0, 1)))

    def in_quarter(s, c):
        s = jnp.minimum(s, 3)
        return jnp.where(s < 2, 2 * c[0] + s, 2 * (1 - c[0]) + s - 2)

    def out_quarter(s, c):
        s = jnp.maximum(s, 4) - 4
        return jnp.where(s < 2, 2 * (1 - c[0]) + s, 2 * c[0] + s - 2)

    rows = count * high
    outs = pl.pallas_call(
        functools.partial(expert_kernel, count),
        grid_spec=pltpu.PrefetchScalarGridSpec(
            num_scalar_prefetch=1,
            grid=(8,),
            in_specs=[place(0)] * count
            + [place(2)] * count
            + [
                pl.BlockSpec((quarter, units), lambda s, c: (in_quarter(s, c), 0)),
                pl.BlockSpec((quarter, units), lambda s, c: (in_quarter(s, c), 0)),
                pl.BlockSpec((units, quarter), lambda s, c: (0, out_quarter(s, c))),
            ],
            out_specs=[place(4)] * count + [place(6)] * count,
            scratch_shapes=[
                pltpu.VMEM((rows, units), jnp.float32),
                pltpu.VMEM((rows, units), jnp.float32),
                pltpu.VMEM((rows, units), jnp.bfloat16),
            ],
        ),
        out_shape=[jax.ShapeDtypeStruct((high, half), jnp.bfloat16)] * (2 * count),
        compiler_params=pltpu.CompilerParams(vmem_limit_bytes=48 * 1024 * 1024),
        cost_estimate=pl.CostEstimate(
            flops=6 * rows * 2 * half * units,
            bytes_accessed=12 * half * units + 8 * rows * half,
            transcendentals=rows * units,
        ),
        name="expert_part",
    )(core, *own, *other, w_gate, w_up, w_down)
    return outs[:count], outs[count:]


def experts_of(own, w_gate, w_up, w_down):
    cut = own.shape[0] // 32 * 16
    c = lax.axis_index("c").astype(jnp.int32).reshape(1)

    def run(*blocks):
        other = [lax.ppermute(block, "c", SWAP) for block in blocks]
        send, keep = expert_part(c, blocks, other, w_gate, w_up, w_down)
        return [add(mine, lax.ppermute(his, "c", SWAP)) for mine, his in zip(keep, send)]

    def near(block):
        return lax.ppermute(block, "z", UP), lax.ppermute(block, "z", DOWN)

    def far(below, above):
        return jnp.concatenate(
            [lax.ppermute(below[:cut], "z", UP), lax.ppermute(above[cut:], "z", DOWN)], axis=0
        )

    def near_back(below, above):
        return lax.ppermute(below, "z", DOWN), lax.ppermute(above, "z", UP)

    over = lax.ppermute(own, "yh", SWAP)
    below, above = near(own)
    far_own = far(below, above)
    far_over = lax.ppermute(far_own, "yh", SWAP)
    over_below, over_above = near(after(over, below, above))
    own, over = run(after(own, below, above), over)
    below, above, far_own = run(after(below, own), above, far_own)
    over_below, over_above, far_over = run(after(over_below, far_own), over_above, far_over)
    over_back = near_back(over_below, over_above)
    far_own = add(far_own, lax.ppermute(far_over, "yh", SWAP))
    over = lax.ppermute(add(over, *over_back), "yh", SWAP)
    from_above = lax.ppermute(far_own[:cut], "z", DOWN)
    from_below = lax.ppermute(far_own[cut:], "z", UP)
    below = jnp.concatenate([add(below[:cut], from_above), below[cut:]], axis=0)
    above = jnp.concatenate([above[:cut], add(above[cut:], from_below)], axis=0)
    return add(own, *near_back(below, above), over)


def per_device(
    stream_in,
    queries,
    rotated_key_heads,
    values,
    doc_ids,
    out_proj,
    norm_gain,
    router,
    w_gate,
    w_up,
    w_down,
    routes,
):
    heads_out, gathered = attention(queries, rotated_key_heads, values, doc_ids)
    summed = project(heads_out, gather_projection(after(out_proj, gathered)))
    resid = stream_in.astype(jnp.float32) + summed.astype(jnp.float32)
    width = resid.shape[1]
    normed = (
        resid * lax.rsqrt(jnp.mean(resid * resid, axis=1, keepdims=True) + 1e-05) * norm_gain
    ).astype(jnp.bfloat16)
    logits = jnp.dot(normed.astype(jnp.float32), router, precision=lax.Precision.HIGHEST)
    experts = router.shape[1]
    rows = normed.shape[0]
    cap = 2 * rows * 9 // 32
    slots = experts * cap
    c = lax.axis_index("c")
    half = width // 2

    def columns(array, core):
        return lax.dynamic_slice_in_dim(array, core * half, half, axis=1)

    def in_order(mine, his, axis):
        return jnp.where(
            c == 0,
            jnp.concatenate([mine, his], axis=axis),
            jnp.concatenate([his, mine], axis=axis),
        )

    pair_routes = in_order(routes, lax.ppermute(routes, "c", SWAP), 0)
    pair_normed = in_order(columns(normed, c), lax.ppermute(columns(normed, 1 - c), "c", SWAP), 0)
    rows2 = 2 * rows
    hits = pair_routes[:, :, None] == jnp.arange(experts, dtype=jnp.int32)
    flat_hits = hits.astype(jnp.int32).reshape(rows2 * 2, experts)
    before = jnp.cumsum(flat_hits, axis=0) - flat_hits
    slot = jnp.sum(before.reshape(rows2, 2, experts) * hits.astype(jnp.int32), axis=-1)
    target = pair_routes * cap + slot
    placed = target[:, :, None] == jnp.arange(slots, dtype=jnp.int32)[None, None, :]
    chooser = jnp.any(placed, axis=1).astype(jnp.bfloat16).T
    own_hits = routes[:, :, None] == jnp.arange(experts, dtype=jnp.int32)
    pair_logits = jnp.sum(jnp.where(own_hits, logits[:, None, :], 0.0), axis=-1)
    first_gate = 1.0 / (1.0 + jnp.exp(pair_logits[:, 1] - pair_logits[:, 0]))
    second_gate = 1.0 / (1.0 + jnp.exp(pair_logits[:, 0] - pair_logits[:, 1]))
    own_gates = jnp.stack([first_gate, second_gate], axis=1)
    gate_pair = in_order(own_gates, lax.ppermute(own_gates, "c", SWAP), 0)
    combiner = jnp.sum(jnp.where(placed, gate_pair[:, :, None], 0.0), axis=1)

    packed = jnp.dot(chooser, pair_normed, preferred_element_type=jnp.float32).astype(jnp.bfloat16)
    arrived = lax.all_to_all(
        packed.reshape(experts, cap, half), ("x", "yl"), split_axis=0, concat_axis=0, tiled=True
    ).reshape(slots, half)
    home = experts_of(arrived, w_gate, w_up, w_down)
    returned = lax.all_to_all(
        home.reshape(experts, cap, half), ("x", "yl"), split_axis=0, concat_axis=0, tiled=True
    ).reshape(slots, half)
    mixture = jnp.dot(combiner, returned.astype(jnp.float32), precision=lax.Precision.HIGHEST)
    mine = lax.dynamic_slice_in_dim(mixture, c * rows, rows, axis=0)
    his = lax.dynamic_slice_in_dim(mixture, (1 - c) * rows, rows, axis=0)
    mixture = in_order(mine, lax.ppermute(his, "c", SWAP), 1)
    return (resid + mixture).astype(jnp.bfloat16)


def solution(mesh):
    fine = Mesh(mesh.devices.reshape(NX, NYL, NZ, NYH, NC), ("x", "yl", "z", "yh", "c"))
    ctx, tp = ("x", "yl", "z"), ("yh", "c")
    placed = (
        P(ctx + tp, None),
        P(ctx, tp),
        P(ctx, tp),
        P(ctx, tp),
        P(ctx),
        P(tp, ctx),
        P(),
        P(),
        P(None, ctx + tp),
        P(None, ctx + tp),
        P(ctx + tp, None),
        P(ctx + tp, None),
    )
    return jax.shard_map(
        per_device, mesh=fine, in_specs=placed, out_specs=P(ctx + tp, None), check_vma=False
    )
```

```python
import functools

import jax
import jax.numpy as jnp
from jax import lax
from jax.experimental import pallas as pl
from jax.experimental.pallas import tpu as pltpu
from jax.sharding import Mesh, PartitionSpec as P

HEAD_WIDTH = 128
NX, NYL, NZ, NYH, NC = 4, 2, 4, 2, 2
SWAP = [(0, 1), (1, 0)]
UP = [(i, (i + 1) % NZ) for i in range(NZ)]
DOWN = [((i + 1) % NZ, i) for i in range(NZ)]


def add(*terms):
    total = terms[0].astype(jnp.float32)
    for term in terms[1:]:
        total = total + term.astype(jnp.float32)
    return total.astype(jnp.bfloat16)


def after(value, *others):
    return lax.optimization_barrier((value, *others))[0]


def from_behind(array, back, flip):
    route = [
        (x * NYL + yl, (x + back) * NYL + (yl ^ flip)) for x in range(NX - back) for yl in range(NYL)
    ]
    return lax.ppermute(array, ("x", "yl"), route)


def gather_keys(keys, values, doc_ids):
    tok = keys.shape[0]
    docs = jnp.pad(doc_ids.astype(jnp.bfloat16)[None, :], ((0, 15), (0, 0)))
    own = jnp.concatenate([keys, values, docs], axis=0)
    order = [(flip, back) for flip in range(NYL) for back in range(3)]
    pieces = [from_behind(own, back, flip) if flip or back else own for flip, back in order]
    here = jnp.concatenate(pieces, axis=0)
    below = lax.ppermute(here, "z", UP)
    above = lax.ppermute(here, "z", DOWN)
    half = here.shape[0] // 2
    far_first = lax.ppermute(below[:half], "z", UP)
    far_second = lax.ppermute(above[half:], "z", DOWN)
    x, yl, z = lax.axis_index("x"), lax.axis_index("yl"), lax.axis_index("z")
    at_x = x - jnp.arange(3, dtype=jnp.int32)
    at_yl = jnp.stack([yl, 1 - yl])
    at_z = (z + jnp.array([0, 3, 1, 2], jnp.int32)) % NZ
    base = (at_x[None, None, :] * NYL + at_yl[None, :, None]) * NZ + at_z[:, None, None]
    base = jnp.where(at_x[None, None, :] >= 0, base * tok, 1 << 30).reshape(-1)
    own_base = ((x * NYL + yl) * NZ + z) * tok
    return (here, below, above, far_first, far_second), jnp.append(base, own_base)


def attention_kernel(base, query, query_doc, here, below, above, far_a, far_b, out, *scratch):
    rows, keys, vals, bias, scores, peak, total, accum = scratch
    tok = query.shape[0]
    heads = query.shape[1] // HEAD_WIDTH
    width = HEAD_WIDTH
    step = here.shape[0] // 6
    blocks = [(ref, i * step) for ref in (here, below, above) for i in range(6)]
    blocks += [(ref, i * step) for ref in (far_a, far_b) for i in range(3)]
    count = len(blocks)
    wide = 4 * tok
    for h in range(heads):
        rows[h * tok : (h + 1) * tok] = query[:, h * width : (h + 1) * width]
    query_at = base[count] + lax.broadcasted_iota(jnp.int32, (tok, tok), 0)
    lane = lax.broadcasted_iota(jnp.int32, (tok, tok), 1)
    for i, (ref, first) in enumerate(blocks):
        keys[i * tok : (i + 1) * tok] = ref[first : first + tok]
        vals[i * tok : (i + 1) * tok] = ref[first + tok : first + 2 * tok]
        docs = ref[first + 2 * tok : first + step].astype(jnp.float32)[0:1]
        allowed = (docs == query_doc[...]) & (base[i] + lane <= query_at)
        bias[i // 4, :, (i % 4) * tok : (i % 4 + 1) * tok] = jnp.where(allowed, 0.0, -1e30)
    peak[...] = jnp.full(peak.shape, -1e30, jnp.float32)
    total[...] = jnp.zeros_like(total)
    accum[...] = jnp.zeros_like(accum)

    def lanes(array):
        return [array[:, i * width : (i + 1) * width] for i in range(wide // width)]

    @pl.loop(0, count // 4)
    def _(i):
        at = pl.ds(pl.multiple_of(i * wide, wide), wide)
        value = lax.dot_general(
            rows[...], keys[at], (((1,), (1,)), ((), ())), preferred_element_type=jnp.float32
        )
        value = value.reshape(heads, tok, wide) * (width ** (-0.5)) + bias[i][None]
        value = value.reshape(heads * tok, wide)
        scores[i] = value
        peak[...] = functools.reduce(jnp.maximum, lanes(value), peak[...])

    top = jnp.max(peak[...], axis=1, keepdims=True)
    peak[...] = jnp.broadcast_to(top, peak.shape)

    @pl.loop(0, count // 4)
    def _(i):
        at = pl.ds(pl.multiple_of(i * wide, wide), wide)
        expo = jnp.exp(scores[i] - jnp.concatenate([peak[...]] * (wide // width), axis=1))
        total[...] = functools.reduce(jnp.add, lanes(expo), total[...])
        accum[...] += jnp.dot(
            expo.astype(jnp.bfloat16), vals[at], preferred_element_type=jnp.float32
        )

    result = accum[...] / jnp.sum(total[...], axis=1, keepdims=True)
    for h in range(heads):
        out[:, h * width : (h + 1) * width] = result[h * tok : (h + 1) * tok].astype(out.dtype)


def attention(queries, keys, values, doc_ids):
    tok, columns = queries.shape
    heads = columns // HEAD_WIDTH
    arrays, base = gather_keys(keys, values, doc_ids)
    whole = pl.BlockSpec(memory_space=pltpu.VMEM)
    return pl.pallas_call(
        attention_kernel,
        in_specs=[pl.BlockSpec(memory_space=pltpu.SMEM)] + [whole] * 7,
        out_specs=whole,
        out_shape=jax.ShapeDtypeStruct(queries.shape, jnp.bfloat16),
        scratch_shapes=[
            pltpu.VMEM((heads * tok, HEAD_WIDTH), jnp.bfloat16),
            pltpu.VMEM((24 * tok, HEAD_WIDTH), jnp.bfloat16),
            pltpu.VMEM((24 * tok, HEAD_WIDTH), jnp.bfloat16),
            pltpu.VMEM((6, tok, 4 * tok), jnp.float32),
            pltpu.VMEM((6, heads * tok, 4 * tok), jnp.float32),
            pltpu.VMEM((heads * tok, HEAD_WIDTH), jnp.float32),
            pltpu.VMEM((heads * tok, HEAD_WIDTH), jnp.float32),
            pltpu.VMEM((heads * tok, HEAD_WIDTH), jnp.float32),
        ],
        compiler_params=pltpu.CompilerParams(vmem_limit_bytes=40 * 1024 * 1024),
        cost_estimate=pl.CostEstimate(
            flops=4 * heads * tok * 24 * tok * HEAD_WIDTH,
            bytes_accessed=4 * 24 * tok * HEAD_WIDTH,
            transcendentals=heads * tok * 24 * tok,
        ),
        name="attention",
    )(base, queries, doc_ids.astype(jnp.float32)[:, None], *arrays)


def gather_projection(out_proj):
    own = out_proj.T
    other = lax.ppermute(own, "yl", SWAP)
    first = lax.axis_index("yl") == 0
    pair = jnp.concatenate([jnp.where(first, own, other), jnp.where(first, other, own)], axis=0)
    return lax.all_gather(pair, "x", axis=0, tiled=True)


def project(heads_out, weight):
    tok = heads_out.shape[0]
    width = weight.shape[0]
    depth = width // (NX * NYL)
    rows = tok // (NYH * NC)
    spread = jnp.broadcast_to(heads_out[None], (NZ,) + heads_out.shape)
    all_z = lax.all_to_all(spread, "z", split_axis=0, concat_axis=0, tiled=True)
    part = lax.dot_general(
        all_z.reshape(NZ * tok, -1),
        weight,
        (((1,), (1,)), ((), ())),
        preferred_element_type=jnp.float32,
    ).astype(jnp.bfloat16)
    part = part.reshape(NZ, NYH, NC, rows, width)
    c = lax.axis_index("c")
    got = lax.ppermute(lax.dynamic_index_in_dim(part, 1 - c, 2, False), "c", SWAP)
    part = add(lax.dynamic_index_in_dim(part, c, 2, False), got)
    part = lax.all_to_all(
        part.reshape(NZ * NYH, rows, width), ("z", "yh"), split_axis=0, concat_axis=0, tiled=True
    )
    part = part.reshape(NZ, NYH, rows, NX * NYL, depth)
    total = part[:, 0].astype(jnp.float32) + part[:, 1].astype(jnp.float32)
    return total.transpose(1, 2, 0, 3).reshape(rows, NX * NYL * NZ * depth)


def expert_kernel(count, core_ref, *refs):
    own, other = refs[:count], refs[count : 2 * count]
    gate_w, up_w, down_w = refs[2 * count : 2 * count + 3]
    send, keep = refs[2 * count + 3 : 3 * count + 3], refs[3 * count + 3 : 4 * count + 3]
    gate_sum, up_sum, hidden = refs[4 * count + 3 :]
    step = pl.program_id(0)
    high = own[0].shape[0]

    def contract(parts, first):
        rows = jnp.concatenate([part[...] for part in parts], axis=0)
        gate = jnp.dot(rows, gate_w[...], preferred_element_type=jnp.float32)
        up = jnp.dot(rows, up_w[...], preferred_element_type=jnp.float32)
        if first:
            gate_sum[...], up_sum[...] = gate, up
        else:
            gate_sum[...] += gate
            up_sum[...] += up

    def expand(outs):
        value = jnp.dot(hidden[...], down_w[...], preferred_element_type=jnp.float32)
        for i, out in enumerate(outs):
            out[...] = value[i * high : (i + 1) * high].astype(out.dtype)

    @pl.when(step == 0)
    def _():
        contract(own, True)

    @pl.when(step == 1)
    def _():
        contract(own, False)

    @pl.when((step == 2) | (step == 3))
    def _():
        contract(other, False)

    @pl.when(step == 3)
    def _():
        gate = gate_sum[...]
        hidden[...] = (gate / (1.0 + jnp.exp(-gate)) * up_sum[...]).astype(hidden.dtype)

    @pl.when((step == 4) | (step == 5))
    def _():
        expand(send)

    @pl.when(step >= 6)
    def _():
        expand(keep)


def expert_part(core, own, other, w_gate, w_up, w_down):
    count = len(own)
    high, half = own[0].shape
    quarter = half // 2
    units = w_gate.shape[1]

    def place(first):
        return pl.BlockSpec((high, quarter), lambda s, c: (0, jnp.clip(s - first, 0, 1)))

    def in_quarter(s, c):
        s = jnp.minimum(s, 3)
        return jnp.where(s < 2, 2 * c[0] + s, 2 * (1 - c[0]) + s - 2)

    def out_quarter(s, c):
        s = jnp.maximum(s, 4) - 4
        return jnp.where(s < 2, 2 * (1 - c[0]) + s, 2 * c[0] + s - 2)

    rows = count * high
    outs = pl.pallas_call(
        functools.partial(expert_kernel, count),
        grid_spec=pltpu.PrefetchScalarGridSpec(
            num_scalar_prefetch=1,
            grid=(8,),
            in_specs=[place(0)] * count
            + [place(2)] * count
            + [
                pl.BlockSpec((quarter, units), lambda s, c: (in_quarter(s, c), 0)),
                pl.BlockSpec((quarter, units), lambda s, c: (in_quarter(s, c), 0)),
                pl.BlockSpec((units, quarter), lambda s, c: (0, out_quarter(s, c))),
            ],
            out_specs=[place(4)] * count + [place(6)] * count,
            scratch_shapes=[
                pltpu.VMEM((rows, units), jnp.float32),
                pltpu.VMEM((rows, units), jnp.float32),
                pltpu.VMEM((rows, units), jnp.bfloat16),
            ],
        ),
        out_shape=[jax.ShapeDtypeStruct((high, half), jnp.bfloat16)] * (2 * count),
        compiler_params=pltpu.CompilerParams(vmem_limit_bytes=48 * 1024 * 1024),
        cost_estimate=pl.CostEstimate(
            flops=6 * rows * 2 * half * units,
            bytes_accessed=12 * half * units + 8 * rows * half,
            transcendentals=rows * units,
        ),
        name="expert_part",
    )(core, *own, *other, w_gate, w_up, w_down)
    return outs[:count], outs[count:]


def experts_of(own, w_gate, w_up, w_down):
    cut = own.shape[0] // 32 * 16
    c = lax.axis_index("c").astype(jnp.int32).reshape(1)

    def run(*blocks):
        other = [lax.ppermute(block, "c", SWAP) for block in blocks]
        send, keep = expert_part(c, blocks, other, w_gate, w_up, w_down)
        return [add(mine, lax.ppermute(his, "c", SWAP)) for mine, his in zip(keep, send)]

    def near(block):
        return lax.ppermute(block, "z", UP), lax.ppermute(block, "z", DOWN)

    def near_back(below, above):
        return lax.ppermute(below, "z", DOWN), lax.ppermute(above, "z", UP)

    rest = own.shape[0] - cut
    over = lax.ppermute(own, "yh", SWAP)
    below, above = near(own)
    up = lax.ppermute(jnp.concatenate([below[:cut], over], axis=0), "z", UP)
    down = lax.ppermute(jnp.concatenate([above[cut:], over], axis=0), "z", DOWN)
    far_own = jnp.concatenate([up[:cut], down[:rest]], axis=0)
    over_below, over_above = up[cut:], down[rest:]
    far_over = jnp.concatenate(
        [lax.ppermute(over_below[:cut], "z", UP), lax.ppermute(over_above[cut:], "z", DOWN)], axis=0
    )
    own, over, below, above = run(own, over, below, above)
    far_own, over_below, over_above, far_over = run(
        after(far_own, own), over_below, over_above, far_over
    )
    over_back = near_back(over_below, over_above)
    far_own = add(far_own, lax.ppermute(far_over, "yh", SWAP))
    from_above = lax.ppermute(far_own[:cut], "z", DOWN)
    from_below = lax.ppermute(far_own[cut:], "z", UP)
    over = lax.ppermute(add(over, *over_back), "yh", SWAP)
    below = jnp.concatenate([add(below[:cut], from_above), below[cut:]], axis=0)
    above = jnp.concatenate([above[:cut], add(above[cut:], from_below)], axis=0)
    return add(own, *near_back(below, above), over)


def per_device(
    stream_in,
    queries,
    rotated_key_heads,
    values,
    doc_ids,
    out_proj,
    norm_gain,
    router,
    w_gate,
    w_up,
    w_down,
    routes,
):
    weight = gather_projection(out_proj)
    heads_out = attention(queries, rotated_key_heads, values, doc_ids)
    summed = project(heads_out, weight)
    resid = stream_in.astype(jnp.float32) + summed.astype(jnp.float32)
    width = resid.shape[1]
    normed = (
        resid * lax.rsqrt(jnp.mean(resid * resid, axis=1, keepdims=True) + 1e-05) * norm_gain
    ).astype(jnp.bfloat16)
    logits = jnp.dot(normed.astype(jnp.float32), router, precision=lax.Precision.HIGHEST)
    experts = router.shape[1]
    rows = normed.shape[0]
    cap = 2 * rows * 9 // 32
    slots = experts * cap
    c = lax.axis_index("c")
    half = width // 2

    def columns(array, core):
        return lax.dynamic_slice_in_dim(array, core * half, half, axis=1)

    def in_order(mine, his, axis):
        return jnp.where(
            c == 0,
            jnp.concatenate([mine, his], axis=axis),
            jnp.concatenate([his, mine], axis=axis),
        )

    pair_routes = in_order(routes, lax.ppermute(routes, "c", SWAP), 0)
    pair_normed = in_order(columns(normed, c), lax.ppermute(columns(normed, 1 - c), "c", SWAP), 0)
    rows2 = 2 * rows
    hits = pair_routes[:, :, None] == jnp.arange(experts, dtype=jnp.int32)
    flat_hits = hits.astype(jnp.int32).reshape(rows2 * 2, experts)
    before = jnp.cumsum(flat_hits, axis=0) - flat_hits
    slot = jnp.sum(before.reshape(rows2, 2, experts) * hits.astype(jnp.int32), axis=-1)
    target = pair_routes * cap + slot
    placed = target[:, :, None] == jnp.arange(slots, dtype=jnp.int32)[None, None, :]
    chooser = jnp.any(placed, axis=1).astype(jnp.bfloat16).T
    own_hits = routes[:, :, None] == jnp.arange(experts, dtype=jnp.int32)
    pair_logits = jnp.sum(jnp.where(own_hits, logits[:, None, :], 0.0), axis=-1)
    first_gate = 1.0 / (1.0 + jnp.exp(pair_logits[:, 1] - pair_logits[:, 0]))
    second_gate = 1.0 / (1.0 + jnp.exp(pair_logits[:, 0] - pair_logits[:, 1]))
    own_gates = jnp.stack([first_gate, second_gate], axis=1)
    gate_pair = in_order(own_gates, lax.ppermute(own_gates, "c", SWAP), 0)
    combiner = jnp.sum(jnp.where(placed, gate_pair[:, :, None], 0.0), axis=1)

    packed = jnp.dot(chooser, pair_normed, preferred_element_type=jnp.float32).astype(jnp.bfloat16)
    arrived = lax.all_to_all(
        packed.reshape(experts, cap, half), ("x", "yl"), split_axis=0, concat_axis=0, tiled=True
    ).reshape(slots, half)
    home = experts_of(arrived, w_gate, w_up, w_down)
    returned = lax.all_to_all(
        home.reshape(experts, cap, half), ("x", "yl"), split_axis=0, concat_axis=0, tiled=True
    ).reshape(slots, half)
    mixture = jnp.dot(combiner, returned.astype(jnp.float32), precision=lax.Precision.HIGHEST)
    mine = lax.dynamic_slice_in_dim(mixture, c * rows, rows, axis=0)
    his = lax.dynamic_slice_in_dim(mixture, (1 - c) * rows, rows, axis=0)
    mixture = in_order(mine, lax.ppermute(his, "c", SWAP), 1)
    return (resid + mixture).astype(jnp.bfloat16)


def solution(mesh):
    fine = Mesh(mesh.devices.reshape(NX, NYL, NZ, NYH, NC), ("x", "yl", "z", "yh", "c"))
    ctx, tp = ("x", "yl", "z"), ("yh", "c")
    placed = (
        P(ctx + tp, None),
        P(ctx, tp),
        P(ctx, tp),
        P(ctx, tp),
        P(ctx),
        P(tp, ctx),
        P(),
        P(),
        P(None, ctx + tp),
        P(None, ctx + tp),
        P(ctx + tp, None),
        P(ctx + tp, None),
    )
    return jax.shard_map(
        per_device, mesh=fine, in_specs=placed, out_specs=P(ctx + tp, None), check_vma=False
    )
```

```python
import functools

import jax
import jax.numpy as jnp
from jax import lax
from jax.experimental import pallas as pl
from jax.experimental.pallas import tpu as pltpu
from jax.sharding import Mesh, PartitionSpec as P

HEAD_WIDTH = 128
NX, NYL, NZ, NYH, NC = 4, 2, 4, 2, 2
SWAP = [(0, 1), (1, 0)]
UP = [(i, (i + 1) % NZ) for i in range(NZ)]
DOWN = [((i + 1) % NZ, i) for i in range(NZ)]


def add(*terms):
    total = terms[0].astype(jnp.float32)
    for term in terms[1:]:
        total = total + term.astype(jnp.float32)
    return total.astype(jnp.bfloat16)


def after(value, *others):
    return lax.optimization_barrier((value, *others))[0]


def from_behind(array, back, flip):
    route = [
        (x * NYL + yl, (x + back) * NYL + (yl ^ flip)) for x in range(NX - back) for yl in range(NYL)
    ]
    return lax.ppermute(array, ("x", "yl"), route)


def gather_keys(keys, values, doc_ids):
    tok = keys.shape[0]
    docs = jnp.pad(doc_ids.astype(jnp.bfloat16)[None, :], ((0, 15), (0, 0)))
    own = jnp.concatenate([keys, values, docs], axis=0)
    order = [(flip, back) for flip in range(NYL) for back in range(3)]
    pieces = [from_behind(own, back, flip) if flip or back else own for flip, back in order]
    here = jnp.concatenate(pieces, axis=0)
    below = lax.ppermute(here, "z", UP)
    above = lax.ppermute(here, "z", DOWN)
    half = here.shape[0] // 2
    far_first = lax.ppermute(below[:half], "z", UP)
    far_second = lax.ppermute(above[half:], "z", DOWN)
    x, yl, z = lax.axis_index("x"), lax.axis_index("yl"), lax.axis_index("z")
    at_x = x - jnp.arange(3, dtype=jnp.int32)
    at_yl = jnp.stack([yl, 1 - yl])
    at_z = (z + jnp.array([0, 3, 1, 2], jnp.int32)) % NZ
    base = (at_x[None, None, :] * NYL + at_yl[None, :, None]) * NZ + at_z[:, None, None]
    base = jnp.where(at_x[None, None, :] >= 0, base * tok, 1 << 30).reshape(-1)
    own_base = ((x * NYL + yl) * NZ + z) * tok
    return (here, below, above, far_first, far_second), jnp.append(base, own_base)


def attention_kernel(base, query, query_doc, here, below, above, far_a, far_b, out, *scratch):
    rows, keys, vals, bias, scores, peak, total, accum = scratch
    tok = query.shape[0]
    heads = query.shape[1] // HEAD_WIDTH
    width = HEAD_WIDTH
    step = here.shape[0] // 6
    blocks = [(ref, i * step) for ref in (here, below, above) for i in range(6)]
    blocks += [(ref, i * step) for ref in (far_a, far_b) for i in range(3)]
    count = len(blocks)
    wide = 4 * tok
    for h in range(heads):
        rows[h * tok : (h + 1) * tok] = query[:, h * width : (h + 1) * width]
    query_at = base[count] + lax.broadcasted_iota(jnp.int32, (tok, tok), 0)
    lane = lax.broadcasted_iota(jnp.int32, (tok, tok), 1)
    for i, (ref, first) in enumerate(blocks):
        keys[i * tok : (i + 1) * tok] = ref[first : first + tok]
        vals[i * tok : (i + 1) * tok] = ref[first + tok : first + 2 * tok]
        docs = ref[first + 2 * tok : first + step].astype(jnp.float32)[0:1]
        allowed = (docs == query_doc[...]) & (base[i] + lane <= query_at)
        bias[i // 4, :, (i % 4) * tok : (i % 4 + 1) * tok] = jnp.where(allowed, 0.0, -1e30)
    peak[...] = jnp.full(peak.shape, -1e30, jnp.float32)
    total[...] = jnp.zeros_like(total)
    accum[...] = jnp.zeros_like(accum)

    def lanes(array):
        return [array[:, i * width : (i + 1) * width] for i in range(wide // width)]

    @pl.loop(0, count // 4)
    def _(i):
        at = pl.ds(pl.multiple_of(i * wide, wide), wide)
        value = lax.dot_general(
            rows[...], keys[at], (((1,), (1,)), ((), ())), preferred_element_type=jnp.float32
        )
        value = value.reshape(heads, tok, wide) * (width ** (-0.5)) + bias[i][None]
        value = value.reshape(heads * tok, wide)
        scores[i] = value
        peak[...] = functools.reduce(jnp.maximum, lanes(value), peak[...])

    top = jnp.max(peak[...], axis=1, keepdims=True)
    peak[...] = jnp.broadcast_to(top, peak.shape)

    @pl.loop(0, count // 4)
    def _(i):
        at = pl.ds(pl.multiple_of(i * wide, wide), wide)
        expo = jnp.exp(scores[i] - jnp.concatenate([peak[...]] * (wide // width), axis=1))
        total[...] = functools.reduce(jnp.add, lanes(expo), total[...])
        accum[...] += jnp.dot(
            expo.astype(jnp.bfloat16), vals[at], preferred_element_type=jnp.float32
        )

    result = accum[...] / jnp.sum(total[...], axis=1, keepdims=True)
    for h in range(heads):
        out[:, h * width : (h + 1) * width] = result[h * tok : (h + 1) * tok].astype(out.dtype)


def attention(queries, keys, values, doc_ids):
    tok, columns = queries.shape
    heads = columns // HEAD_WIDTH
    arrays, base = gather_keys(keys, values, doc_ids)
    whole = pl.BlockSpec(memory_space=pltpu.VMEM)
    return pl.pallas_call(
        attention_kernel,
        in_specs=[pl.BlockSpec(memory_space=pltpu.SMEM)] + [whole] * 7,
        out_specs=whole,
        out_shape=jax.ShapeDtypeStruct(queries.shape, jnp.bfloat16),
        scratch_shapes=[
            pltpu.VMEM((heads * tok, HEAD_WIDTH), jnp.bfloat16),
            pltpu.VMEM((24 * tok, HEAD_WIDTH), jnp.bfloat16),
            pltpu.VMEM((24 * tok, HEAD_WIDTH), jnp.bfloat16),
            pltpu.VMEM((6, tok, 4 * tok), jnp.float32),
            pltpu.VMEM((6, heads * tok, 4 * tok), jnp.float32),
            pltpu.VMEM((heads * tok, HEAD_WIDTH), jnp.float32),
            pltpu.VMEM((heads * tok, HEAD_WIDTH), jnp.float32),
            pltpu.VMEM((heads * tok, HEAD_WIDTH), jnp.float32),
        ],
        compiler_params=pltpu.CompilerParams(vmem_limit_bytes=40 * 1024 * 1024),
        cost_estimate=pl.CostEstimate(
            flops=4 * heads * tok * 24 * tok * HEAD_WIDTH,
            bytes_accessed=4 * 24 * tok * HEAD_WIDTH,
            transcendentals=heads * tok * 24 * tok,
        ),
        name="attention",
    )(base, queries, doc_ids.astype(jnp.float32)[:, None], *arrays), arrays[0]


def gather_projection(out_proj):
    own = out_proj.T
    other = lax.ppermute(own, "yl", SWAP)
    first = lax.axis_index("yl") == 0
    pair = jnp.concatenate([jnp.where(first, own, other), jnp.where(first, other, own)], axis=0)
    return lax.all_gather(pair, "x", axis=0, tiled=True)


def project(heads_out, weight):
    tok = heads_out.shape[0]
    width = weight.shape[0]
    depth = width // (NX * NYL)
    rows = tok // (NYH * NC)
    spread = jnp.broadcast_to(heads_out[None], (NZ,) + heads_out.shape)
    all_z = lax.all_to_all(spread, "z", split_axis=0, concat_axis=0, tiled=True)
    part = lax.dot_general(
        all_z.reshape(NZ * tok, -1),
        weight,
        (((1,), (1,)), ((), ())),
        preferred_element_type=jnp.float32,
    ).astype(jnp.bfloat16)
    part = part.reshape(NZ, NYH, NC, rows, width)
    c = lax.axis_index("c")
    got = lax.ppermute(lax.dynamic_index_in_dim(part, 1 - c, 2, False), "c", SWAP)
    part = add(lax.dynamic_index_in_dim(part, c, 2, False), got)
    part = lax.all_to_all(
        part.reshape(NZ * NYH, rows, width), ("z", "yh"), split_axis=0, concat_axis=0, tiled=True
    )
    part = part.reshape(NZ, NYH, rows, NX * NYL, depth)
    total = part[:, 0].astype(jnp.float32) + part[:, 1].astype(jnp.float32)
    return total.transpose(1, 2, 0, 3).reshape(rows, NX * NYL * NZ * depth)


def expert_kernel(count, core_ref, *refs):
    own, other = refs[:count], refs[count : 2 * count]
    gate_w, up_w, down_w = refs[2 * count : 2 * count + 3]
    send, keep = refs[2 * count + 3 : 3 * count + 3], refs[3 * count + 3 : 4 * count + 3]
    gate_sum, up_sum, hidden = refs[4 * count + 3 :]
    step = pl.program_id(0)
    high = own[0].shape[0]

    def contract(parts, first):
        rows = jnp.concatenate([part[...] for part in parts], axis=0)
        gate = jnp.dot(rows, gate_w[...], preferred_element_type=jnp.float32)
        up = jnp.dot(rows, up_w[...], preferred_element_type=jnp.float32)
        if first:
            gate_sum[...], up_sum[...] = gate, up
        else:
            gate_sum[...] += gate
            up_sum[...] += up

    def expand(outs):
        value = jnp.dot(hidden[...], down_w[...], preferred_element_type=jnp.float32)
        for i, out in enumerate(outs):
            out[...] = value[i * high : (i + 1) * high].astype(out.dtype)

    @pl.when(step == 0)
    def _():
        contract(own, True)

    @pl.when(step == 1)
    def _():
        contract(own, False)

    @pl.when((step == 2) | (step == 3))
    def _():
        contract(other, False)

    @pl.when(step == 3)
    def _():
        gate = gate_sum[...]
        hidden[...] = (gate / (1.0 + jnp.exp(-gate)) * up_sum[...]).astype(hidden.dtype)

    @pl.when((step == 4) | (step == 5))
    def _():
        expand(send)

    @pl.when(step >= 6)
    def _():
        expand(keep)


def expert_part(core, own, other, w_gate, w_up, w_down):
    count = len(own)
    high, half = own[0].shape
    quarter = half // 2
    units = w_gate.shape[1]

    def place(first):
        return pl.BlockSpec((high, quarter), lambda s, c: (0, jnp.clip(s - first, 0, 1)))

    def in_quarter(s, c):
        s = jnp.minimum(s, 3)
        return jnp.where(s < 2, 2 * c[0] + s, 2 * (1 - c[0]) + s - 2)

    def out_quarter(s, c):
        s = jnp.maximum(s, 4) - 4
        return jnp.where(s < 2, 2 * (1 - c[0]) + s, 2 * c[0] + s - 2)

    rows = count * high
    outs = pl.pallas_call(
        functools.partial(expert_kernel, count),
        grid_spec=pltpu.PrefetchScalarGridSpec(
            num_scalar_prefetch=1,
            grid=(8,),
            in_specs=[place(0)] * count
            + [place(2)] * count
            + [
                pl.BlockSpec((quarter, units), lambda s, c: (in_quarter(s, c), 0)),
                pl.BlockSpec((quarter, units), lambda s, c: (in_quarter(s, c), 0)),
                pl.BlockSpec((units, quarter), lambda s, c: (0, out_quarter(s, c))),
            ],
            out_specs=[place(4)] * count + [place(6)] * count,
            scratch_shapes=[
                pltpu.VMEM((rows, units), jnp.float32),
                pltpu.VMEM((rows, units), jnp.float32),
                pltpu.VMEM((rows, units), jnp.bfloat16),
            ],
        ),
        out_shape=[jax.ShapeDtypeStruct((high, half), jnp.bfloat16)] * (2 * count),
        compiler_params=pltpu.CompilerParams(vmem_limit_bytes=48 * 1024 * 1024),
        cost_estimate=pl.CostEstimate(
            flops=6 * rows * 2 * half * units,
            bytes_accessed=12 * half * units + 8 * rows * half,
            transcendentals=rows * units,
        ),
        name="expert_part",
    )(core, *own, *other, w_gate, w_up, w_down)
    return outs[:count], outs[count:]


def experts_of(own, w_gate, w_up, w_down):
    cut = own.shape[0] // 32 * 16
    c = lax.axis_index("c").astype(jnp.int32).reshape(1)

    def run(*blocks):
        other = [lax.ppermute(block, "c", SWAP) for block in blocks]
        return expert_part(c, blocks, other, w_gate, w_up, w_down)

    def summed(parts):
        send, keep = parts
        return [add(mine, lax.ppermute(his, "c", SWAP)) for mine, his in zip(keep, send)]

    def near(block):
        return lax.ppermute(block, "z", UP), lax.ppermute(block, "z", DOWN)

    def near_back(below, above):
        return lax.ppermute(below, "z", DOWN), lax.ppermute(above, "z", UP)

    rest = own.shape[0] - cut
    over = lax.ppermute(own, "yh", SWAP)
    below, above = near(own)
    up = lax.ppermute(jnp.concatenate([below[:cut], over], axis=0), "z", UP)
    down = lax.ppermute(jnp.concatenate([above[cut:], over], axis=0), "z", DOWN)
    far_own = jnp.concatenate([up[:cut], down[:rest]], axis=0)
    over_below, over_above = up[cut:], down[rest:]
    far_over = lax.ppermute(far_own, "yh", SWAP)
    own, over, below, above = summed(run(own, over, below, above))
    own_back = near_back(below, above)
    parts = run(after(far_own, own, over, below, above), over_below, over_above)
    far_over = after(far_over, *own_back, parts[1][-1])
    last = run(far_over)
    far_own, over_below, over_above = summed(parts)
    over_back = near_back(over_below, over_above)
    (far_over,) = summed(last)
    far_own = add(far_own, lax.ppermute(far_over, "yh", SWAP))
    over = lax.ppermute(add(over, *over_back), "yh", SWAP)
    far_own = lax.ppermute(after(far_own, *over_back), "z", [(i, (i + 2) % NZ) for i in range(NZ)])
    return add(own, *own_back, far_own, over)


def per_device(
    stream_in,
    queries,
    rotated_key_heads,
    values,
    doc_ids,
    out_proj,
    norm_gain,
    router,
    w_gate,
    w_up,
    w_down,
    routes,
):
    heads_out, gathered = attention(queries, rotated_key_heads, values, doc_ids)
    summed = project(heads_out, gather_projection(after(out_proj, gathered)))
    resid = stream_in.astype(jnp.float32) + summed.astype(jnp.float32)
    width = resid.shape[1]
    normed = (
        resid * lax.rsqrt(jnp.mean(resid * resid, axis=1, keepdims=True) + 1e-05) * norm_gain
    ).astype(jnp.bfloat16)
    logits = jnp.dot(normed.astype(jnp.float32), router, precision=lax.Precision.HIGHEST)
    experts = router.shape[1]
    rows = normed.shape[0]
    cap = 2 * rows * 9 // 32
    slots = experts * cap
    c = lax.axis_index("c")
    half = width // 2

    def columns(array, core):
        return lax.dynamic_slice_in_dim(array, core * half, half, axis=1)

    def in_order(mine, his, axis):
        return jnp.where(
            c == 0,
            jnp.concatenate([mine, his], axis=axis),
            jnp.concatenate([his, mine], axis=axis),
        )

    pair_routes = in_order(routes, lax.ppermute(routes, "c", SWAP), 0)
    pair_normed = in_order(columns(normed, c), lax.ppermute(columns(normed, 1 - c), "c", SWAP), 0)
    rows2 = 2 * rows
    hits = pair_routes[:, :, None] == jnp.arange(experts, dtype=jnp.int32)
    flat_hits = hits.astype(jnp.int32).reshape(rows2 * 2, experts)
    before = jnp.cumsum(flat_hits, axis=0) - flat_hits
    slot = jnp.sum(before.reshape(rows2, 2, experts) * hits.astype(jnp.int32), axis=-1)
    target = pair_routes * cap + slot
    placed = target[:, :, None] == jnp.arange(slots, dtype=jnp.int32)[None, None, :]
    chooser = jnp.any(placed, axis=1).astype(jnp.bfloat16).T
    own_hits = routes[:, :, None] == jnp.arange(experts, dtype=jnp.int32)
    pair_logits = jnp.sum(jnp.where(own_hits, logits[:, None, :], 0.0), axis=-1)
    first_gate = 1.0 / (1.0 + jnp.exp(pair_logits[:, 1] - pair_logits[:, 0]))
    second_gate = 1.0 / (1.0 + jnp.exp(pair_logits[:, 0] - pair_logits[:, 1]))
    own_gates = jnp.stack([first_gate, second_gate], axis=1)
    gate_pair = in_order(own_gates, lax.ppermute(own_gates, "c", SWAP), 0)
    combiner = jnp.sum(jnp.where(placed, gate_pair[:, :, None], 0.0), axis=1)

    packed = jnp.dot(chooser, pair_normed, preferred_element_type=jnp.float32).astype(jnp.bfloat16)
    arrived = lax.all_to_all(
        packed.reshape(experts, cap, half), ("x", "yl"), split_axis=0, concat_axis=0, tiled=True
    ).reshape(slots, half)
    home = experts_of(arrived, w_gate, w_up, w_down)
    returned = lax.all_to_all(
        home.reshape(experts, cap, half), ("x", "yl"), split_axis=0, concat_axis=0, tiled=True
    ).reshape(slots, half)
    mixture = jnp.dot(combiner, returned.astype(jnp.float32), precision=lax.Precision.HIGHEST)
    mine = lax.dynamic_slice_in_dim(mixture, c * rows, rows, axis=0)
    his = lax.dynamic_slice_in_dim(mixture, (1 - c) * rows, rows, axis=0)
    mixture = in_order(mine, lax.ppermute(his, "c", SWAP), 1)
    return (resid + mixture).astype(jnp.bfloat16)


def solution(mesh):
    fine = Mesh(mesh.devices.reshape(NX, NYL, NZ, NYH, NC), ("x", "yl", "z", "yh", "c"))
    ctx, tp = ("x", "yl", "z"), ("yh", "c")
    placed = (
        P(ctx + tp, None),
        P(ctx, tp),
        P(ctx, tp),
        P(ctx, tp),
        P(ctx),
        P(tp, ctx),
        P(),
        P(),
        P(None, ctx + tp),
        P(None, ctx + tp),
        P(ctx + tp, None),
        P(ctx + tp, None),
    )
    return jax.shard_map(
        per_device, mesh=fine, in_specs=placed, out_specs=P(ctx + tp, None), check_vma=False
    )
```

```python
import functools

import jax
import jax.numpy as jnp
from jax import lax
from jax.experimental import pallas as pl
from jax.experimental.pallas import tpu as pltpu
from jax.sharding import Mesh, PartitionSpec as P

HEAD_WIDTH = 128
NX, NYL, NZ, NYH, NC = 4, 2, 4, 2, 2
SWAP = [(0, 1), (1, 0)]
UP = [(i, (i + 1) % NZ) for i in range(NZ)]
DOWN = [((i + 1) % NZ, i) for i in range(NZ)]
FAR = [(i, (i + 2) % NZ) for i in range(NZ)]


def add(*terms):
    total = terms[0].astype(jnp.float32)
    for term in terms[1:]:
        total = total + term.astype(jnp.float32)
    return total.astype(jnp.bfloat16)


def after(value, *others):
    return lax.optimization_barrier((value, *others))[0]


def over_ctx(array, move):
    route = []
    for x in range(NX):
        for yl in range(NYL):
            to_x, to_yl = move(x, yl)
            if to_x < NX:
                route.append((x * NYL + yl, to_x * NYL + to_yl))
    return lax.ppermute(array, ("x", "yl"), route)


def gather_keys(keys, values, doc_ids):
    tok = keys.shape[0]
    docs = jnp.pad(doc_ids.astype(jnp.bfloat16)[None, :], ((0, 15), (0, 0)))
    own = jnp.concatenate([keys, values, docs], axis=0)
    size = own.shape[0]
    one = over_ctx(own, lambda x, yl: (x + 1, yl))
    two = over_ctx(own, lambda x, yl: (x + 2, yl))
    one_other = over_ctx(own, lambda x, yl: (x + 1, 1 - yl))
    other = over_ctx(own, lambda x, yl: (x, 1) if yl == 0 else (x + 2, 0))
    x, yl, z = lax.axis_index("x"), lax.axis_index("yl"), lax.axis_index("z")
    up = jnp.concatenate([other, one_other, one, jnp.where(z == NZ - 1, two, own)], axis=0)
    down = jnp.concatenate([other, one_other, one, jnp.where(z == 0, own, two)], axis=0)
    below = lax.ppermute(up, "z", UP)
    above = lax.ppermute(down, "z", DOWN)
    far = lax.ppermute(jnp.where(z < 2, own, two), "z", FAR)
    far_up = lax.ppermute(below[: 2 * size], "z", UP)
    far_down = lax.ppermute(above[2 * size : 3 * size], "z", DOWN)

    def base(at_x, at_yl, at_z):
        return jnp.where(at_x >= 0, ((at_x * NYL + at_yl) * NZ + at_z) * tok, 1 << 30)

    def column(at_z):
        return [
            base(jnp.where(yl == 1, x, x - 2), 1 - yl, at_z),
            base(x - 1, 1 - yl, at_z),
            base(x - 1, yl, at_z),
            base(jnp.where(at_z < z, x, x - 2), yl, at_z),
        ]

    bases = [base(x, yl, z), base(x - 2, yl, z)] + column(z)[:3]
    for step in (NZ - 1, 1, 2):
        bases += column((z + step) % NZ)
    return (own, two, up, below, above, far_up, far_down, far), jnp.stack(bases), (one, two, one_other, other)


def attention_kernel(base, query, query_doc, own, two, mid, below, above, far_up, far_down, far, out, *scratch):
    rows, keys, vals, bias, scores, peak, total, accum = scratch
    tok = query.shape[0]
    heads = query.shape[1] // HEAD_WIDTH
    width = HEAD_WIDTH
    step = own.shape[0]
    blocks = []
    for ref, count in (
        (own, 1), (two, 1), (mid, 3), (below, 4), (above, 4), (far_up, 2), (far_down, 1), (far, 1)
    ):
        blocks += [(ref, i * step) for i in range(count)]
    per = bias.shape[2] // tok
    wide = per * tok
    for h in range(heads):
        rows[h * tok : (h + 1) * tok] = query[:, h * width : (h + 1) * width]
    query_at = base[0] + lax.broadcasted_iota(jnp.int32, (tok, tok), 0)
    lane = lax.broadcasted_iota(jnp.int32, (tok, tok), 1)
    for i in range(per * bias.shape[0]):
        at = pl.ds(i * tok, tok)
        if i < len(blocks):
            ref, first = blocks[i]
            keys[at] = ref[first : first + tok]
            vals[at] = ref[first + tok : first + 2 * tok]
            docs = ref[first + 2 * tok : first + step].astype(jnp.float32)[0:1]
            allowed = (docs == query_doc[...]) & (base[i] + lane <= query_at)
            mask = jnp.where(allowed, 0.0, -1e30)
        else:
            keys[at] = jnp.zeros((tok, width), jnp.bfloat16)
            vals[at] = jnp.zeros((tok, width), jnp.bfloat16)
            mask = jnp.full((tok, tok), -1e30, jnp.float32)
        bias[i // per, :, (i % per) * tok : (i % per + 1) * tok] = mask
    peak[...] = jnp.full(peak.shape, -1e30, jnp.float32)
    total[...] = jnp.zeros_like(total)
    accum[...] = jnp.zeros_like(accum)

    def lanes(array):
        return [array[:, i * width : (i + 1) * width] for i in range(wide // width)]

    @pl.loop(0, bias.shape[0])
    def _(i):
        at = pl.ds(pl.multiple_of(i * wide, wide), wide)
        value = lax.dot_general(
            rows[...], keys[at], (((1,), (1,)), ((), ())), preferred_element_type=jnp.float32
        )
        value = value.reshape(heads, tok, wide) * (width ** (-0.5)) + bias[i][None]
        value = value.reshape(heads * tok, wide)
        scores[i] = value
        peak[...] = functools.reduce(jnp.maximum, lanes(value), peak[...])

    top = jnp.max(peak[...], axis=1, keepdims=True)
    peak[...] = jnp.broadcast_to(top, peak.shape)

    @pl.loop(0, bias.shape[0])
    def _(i):
        at = pl.ds(pl.multiple_of(i * wide, wide), wide)
        expo = jnp.exp(scores[i] - jnp.concatenate([peak[...]] * (wide // width), axis=1))
        total[...] = functools.reduce(jnp.add, lanes(expo), total[...])
        accum[...] += jnp.dot(
            expo.astype(jnp.bfloat16), vals[at], preferred_element_type=jnp.float32
        )

    result = accum[...] / jnp.sum(total[...], axis=1, keepdims=True)
    for h in range(heads):
        out[:, h * width : (h + 1) * width] = result[h * tok : (h + 1) * tok].astype(out.dtype)


def attention(queries, keys, values, doc_ids):
    tok, columns = queries.shape
    heads = columns // HEAD_WIDTH
    arrays, base, first = gather_keys(keys, values, doc_ids)
    whole = pl.BlockSpec(memory_space=pltpu.VMEM)
    turns, wide = 3, 6 * tok
    out = pl.pallas_call(
        attention_kernel,
        in_specs=[pl.BlockSpec(memory_space=pltpu.SMEM)] + [whole] * (2 + len(arrays)),
        out_specs=whole,
        out_shape=jax.ShapeDtypeStruct(queries.shape, jnp.bfloat16),
        scratch_shapes=[
            pltpu.VMEM((heads * tok, HEAD_WIDTH), jnp.bfloat16),
            pltpu.VMEM((turns * wide, HEAD_WIDTH), jnp.bfloat16),
            pltpu.VMEM((turns * wide, HEAD_WIDTH), jnp.bfloat16),
            pltpu.VMEM((turns, tok, wide), jnp.float32),
            pltpu.VMEM((turns, heads * tok, wide), jnp.float32),
            pltpu.VMEM((heads * tok, HEAD_WIDTH), jnp.float32),
            pltpu.VMEM((heads * tok, HEAD_WIDTH), jnp.float32),
            pltpu.VMEM((heads * tok, HEAD_WIDTH), jnp.float32),
        ],
        compiler_params=pltpu.CompilerParams(vmem_limit_bytes=40 * 1024 * 1024),
        cost_estimate=pl.CostEstimate(
            flops=4 * heads * tok * turns * wide * HEAD_WIDTH,
            bytes_accessed=4 * turns * wide * HEAD_WIDTH,
            transcendentals=heads * tok * turns * wide,
        ),
        name="attention",
    )(base, queries, doc_ids.astype(jnp.float32)[:, None], *arrays)
    return out, first


def gather_projection(out_proj, earlier):
    own = out_proj.T
    other = after(lax.ppermute(own, "yl", SWAP), *earlier)
    first = lax.axis_index("yl") == 0
    pair = jnp.concatenate([jnp.where(first, own, other), jnp.where(first, other, own)], axis=0)
    return lax.all_gather(pair, "x", axis=0, tiled=True)


def project(heads_out, weight):
    tok = heads_out.shape[0]
    width = weight.shape[0]
    depth = width // (NX * NYL)
    rows = tok // (NYH * NC)
    spread = jnp.broadcast_to(heads_out[None], (NZ,) + heads_out.shape)
    all_z = lax.all_to_all(spread, "z", split_axis=0, concat_axis=0, tiled=True)
    part = lax.dot_general(
        all_z.reshape(NZ * tok, -1),
        weight,
        (((1,), (1,)), ((), ())),
        preferred_element_type=jnp.float32,
    ).astype(jnp.bfloat16)
    part = part.reshape(NZ, NYH, NC, rows, width)
    c = lax.axis_index("c")
    got = lax.ppermute(lax.dynamic_index_in_dim(part, 1 - c, 2, False), "c", SWAP)
    part = add(lax.dynamic_index_in_dim(part, c, 2, False), got)
    part = lax.all_to_all(
        part.reshape(NZ * NYH, rows, width), ("z", "yh"), split_axis=0, concat_axis=0, tiled=True
    )
    part = part.reshape(NZ, NYH, rows, NX * NYL, depth)
    total = part[:, 0].astype(jnp.float32) + part[:, 1].astype(jnp.float32)
    return total.transpose(1, 2, 0, 3).reshape(rows, NX * NYL * NZ * depth)


def expert_kernel(count, core_ref, *refs):
    own, other = refs[:count], refs[count : 2 * count]
    gate_w, up_w, down_w = refs[2 * count : 2 * count + 3]
    send, keep = refs[2 * count + 3 : 3 * count + 3], refs[3 * count + 3 : 4 * count + 3]
    gate_sum, up_sum, hidden = refs[4 * count + 3 :]
    step = pl.program_id(0)
    high = own[0].shape[0]

    def contract(parts, first):
        rows = jnp.concatenate([part[...] for part in parts], axis=0)
        gate = jnp.dot(rows, gate_w[...], preferred_element_type=jnp.float32)
        up = jnp.dot(rows, up_w[...], preferred_element_type=jnp.float32)
        if first:
            gate_sum[...], up_sum[...] = gate, up
        else:
            gate_sum[...] += gate
            up_sum[...] += up

    def expand(outs):
        value = jnp.dot(hidden[...], down_w[...], preferred_element_type=jnp.float32)
        for i, out in enumerate(outs):
            out[...] = value[i * high : (i + 1) * high].astype(out.dtype)

    @pl.when(step == 0)
    def _():
        contract(own, True)

    @pl.when(step == 1)
    def _():
        contract(own, False)

    @pl.when((step == 2) | (step == 3))
    def _():
        contract(other, False)

    @pl.when(step == 3)
    def _():
        gate = gate_sum[...]
        hidden[...] = (gate / (1.0 + jnp.exp(-gate)) * up_sum[...]).astype(hidden.dtype)

    @pl.when((step == 4) | (step == 5))
    def _():
        expand(send)

    @pl.when(step >= 6)
    def _():
        expand(keep)


def expert_part(core, own, other, w_gate, w_up, w_down):
    count = len(own)
    high, half = own[0].shape
    quarter = half // 2
    units = w_gate.shape[1]

    def place(first):
        return pl.BlockSpec((high, quarter), lambda s, c: (0, jnp.clip(s - first, 0, 1)))

    def in_quarter(s, c):
        s = jnp.minimum(s, 3)
        return jnp.where(s < 2, 2 * c[0] + s, 2 * (1 - c[0]) + s - 2)

    def out_quarter(s, c):
        s = jnp.maximum(s, 4) - 4
        return jnp.where(s < 2, 2 * (1 - c[0]) + s, 2 * c[0] + s - 2)

    rows = count * high
    outs = pl.pallas_call(
        functools.partial(expert_kernel, count),
        grid_spec=pltpu.PrefetchScalarGridSpec(
            num_scalar_prefetch=1,
            grid=(8,),
            in_specs=[place(0)] * count
            + [place(2)] * count
            + [
                pl.BlockSpec((quarter, units), lambda s, c: (in_quarter(s, c), 0)),
                pl.BlockSpec((quarter, units), lambda s, c: (in_quarter(s, c), 0)),
                pl.BlockSpec((units, quarter), lambda s, c: (0, out_quarter(s, c))),
            ],
            out_specs=[place(4)] * count + [place(6)] * count,
            scratch_shapes=[
                pltpu.VMEM((rows, units), jnp.float32),
                pltpu.VMEM((rows, units), jnp.float32),
                pltpu.VMEM((rows, units), jnp.bfloat16),
            ],
        ),
        out_shape=[jax.ShapeDtypeStruct((high, half), jnp.bfloat16)] * (2 * count),
        compiler_params=pltpu.CompilerParams(vmem_limit_bytes=48 * 1024 * 1024),
        cost_estimate=pl.CostEstimate(
            flops=6 * rows * 2 * half * units,
            bytes_accessed=12 * half * units + 8 * rows * half,
            transcendentals=rows * units,
        ),
        name="expert_part",
    )(core, *own, *other, w_gate, w_up, w_down)
    return outs[:count], outs[count:]


def experts_of(own, w_gate, w_up, w_down):
    cut = own.shape[0] // 32 * 16
    c = lax.axis_index("c").astype(jnp.int32).reshape(1)

    def run(*blocks):
        other = [lax.ppermute(block, "c", SWAP) for block in blocks]
        return expert_part(c, blocks, other, w_gate, w_up, w_down)

    def summed(parts):
        send, keep = parts
        return [add(mine, lax.ppermute(his, "c", SWAP)) for mine, his in zip(keep, send)]

    def near(block):
        return lax.ppermute(block, "z", UP), lax.ppermute(block, "z", DOWN)

    def near_back(below, above):
        return lax.ppermute(below, "z", DOWN), lax.ppermute(above, "z", UP)

    rest = own.shape[0] - cut
    over = lax.ppermute(own, "yh", SWAP)
    below, above = near(own)
    up = lax.ppermute(jnp.concatenate([below[:cut], over], axis=0), "z", UP)
    down = lax.ppermute(jnp.concatenate([above[cut:], over], axis=0), "z", DOWN)
    far_own = jnp.concatenate([up[:cut], down[:rest]], axis=0)
    over_below, over_above = up[cut:], down[rest:]
    far_over = lax.ppermute(far_own, "yh", SWAP)
    own, over, below, above = summed(run(own, over, below, above))
    own_back = near_back(below, above)
    parts = run(after(far_own, own, over, below, above), over_below, over_above)
    far_over = after(far_over, *own_back, parts[1][-1])
    last = run(far_over)
    far_own, over_below, over_above = summed(parts)
    over_back = near_back(over_below, over_above)
    (far_over,) = summed(last)
    far_own = add(far_own, lax.ppermute(far_over, "yh", SWAP))
    over = lax.ppermute(add(over, *over_back), "yh", SWAP)
    far_own = lax.ppermute(after(far_own, *over_back), "z", FAR)
    return add(own, *own_back, far_own, over)


def per_device(
    stream_in,
    queries,
    rotated_key_heads,
    values,
    doc_ids,
    out_proj,
    norm_gain,
    router,
    w_gate,
    w_up,
    w_down,
    routes,
):
    heads_out, first_keys = attention(queries, rotated_key_heads, values, doc_ids)
    summed = project(heads_out, gather_projection(out_proj, first_keys))
    resid = stream_in.astype(jnp.float32) + summed.astype(jnp.float32)
    width = resid.shape[1]
    normed = (
        resid * lax.rsqrt(jnp.mean(resid * resid, axis=1, keepdims=True) + 1e-05) * norm_gain
    ).astype(jnp.bfloat16)
    logits = jnp.dot(normed.astype(jnp.float32), router, precision=lax.Precision.HIGHEST)
    experts = router.shape[1]
    rows = normed.shape[0]
    cap = 2 * rows * 9 // 32
    slots = experts * cap
    c = lax.axis_index("c")
    half = width // 2

    def columns(array, core):
        return lax.dynamic_slice_in_dim(array, core * half, half, axis=1)

    def in_order(mine, his, axis):
        return jnp.where(
            c == 0,
            jnp.concatenate([mine, his], axis=axis),
            jnp.concatenate([his, mine], axis=axis),
        )

    pair_routes = in_order(routes, lax.ppermute(routes, "c", SWAP), 0)
    pair_normed = in_order(columns(normed, c), lax.ppermute(columns(normed, 1 - c), "c", SWAP), 0)
    rows2 = 2 * rows
    hits = pair_routes[:, :, None] == jnp.arange(experts, dtype=jnp.int32)
    flat_hits = hits.astype(jnp.int32).reshape(rows2 * 2, experts)
    before = jnp.cumsum(flat_hits, axis=0) - flat_hits
    slot = jnp.sum(before.reshape(rows2, 2, experts) * hits.astype(jnp.int32), axis=-1)
    target = pair_routes * cap + slot
    placed = target[:, :, None] == jnp.arange(slots, dtype=jnp.int32)[None, None, :]
    chooser = jnp.any(placed, axis=1).astype(jnp.bfloat16).T
    own_hits = routes[:, :, None] == jnp.arange(experts, dtype=jnp.int32)
    pair_logits = jnp.sum(jnp.where(own_hits, logits[:, None, :], 0.0), axis=-1)
    first_gate = 1.0 / (1.0 + jnp.exp(pair_logits[:, 1] - pair_logits[:, 0]))
    second_gate = 1.0 / (1.0 + jnp.exp(pair_logits[:, 0] - pair_logits[:, 1]))
    own_gates = jnp.stack([first_gate, second_gate], axis=1)
    gate_pair = in_order(own_gates, lax.ppermute(own_gates, "c", SWAP), 0)
    combiner = jnp.sum(jnp.where(placed, gate_pair[:, :, None], 0.0), axis=1)

    packed = jnp.dot(chooser, pair_normed, preferred_element_type=jnp.float32).astype(jnp.bfloat16)
    arrived = lax.all_to_all(
        packed.reshape(experts, cap, half), ("x", "yl"), split_axis=0, concat_axis=0, tiled=True
    ).reshape(slots, half)
    home = experts_of(arrived, w_gate, w_up, w_down)
    returned = lax.all_to_all(
        home.reshape(experts, cap, half), ("x", "yl"), split_axis=0, concat_axis=0, tiled=True
    ).reshape(slots, half)
    mixture = jnp.dot(combiner, returned.astype(jnp.float32), precision=lax.Precision.HIGHEST)
    mine = lax.dynamic_slice_in_dim(mixture, c * rows, rows, axis=0)
    his = lax.dynamic_slice_in_dim(mixture, (1 - c) * rows, rows, axis=0)
    mixture = in_order(mine, lax.ppermute(his, "c", SWAP), 1)
    return (resid + mixture).astype(jnp.bfloat16)


def solution(mesh):
    fine = Mesh(mesh.devices.reshape(NX, NYL, NZ, NYH, NC), ("x", "yl", "z", "yh", "c"))
    ctx, tp = ("x", "yl", "z"), ("yh", "c")
    placed = (
        P(ctx + tp, None),
        P(ctx, tp),
        P(ctx, tp),
        P(ctx, tp),
        P(ctx),
        P(tp, ctx),
        P(),
        P(),
        P(None, ctx + tp),
        P(None, ctx + tp),
        P(ctx + tp, None),
        P(ctx + tp, None),
    )
    return jax.shard_map(
        per_device, mesh=fine, in_specs=placed, out_specs=P(ctx + tp, None), check_vma=False
    )
```

```python
import functools

import jax
import jax.numpy as jnp
from jax import lax
from jax.experimental import pallas as pl
from jax.experimental.pallas import tpu as pltpu
from jax.sharding import Mesh, PartitionSpec as P

HEAD_WIDTH = 128
NX, NYL, NZ, NYH, NC = 4, 2, 4, 2, 2
SWAP = [(0, 1), (1, 0)]
UP = [(i, (i + 1) % NZ) for i in range(NZ)]
DOWN = [((i + 1) % NZ, i) for i in range(NZ)]
FAR = [(i, (i + 2) % NZ) for i in range(NZ)]


def add(*terms):
    total = terms[0].astype(jnp.float32)
    for term in terms[1:]:
        total = total + term.astype(jnp.float32)
    return total.astype(jnp.bfloat16)


def after(value, *others):
    return lax.optimization_barrier((value, *others))[0]


def over_ctx(array, move):
    route = []
    for x in range(NX):
        for yl in range(NYL):
            to_x, to_yl = move(x, yl)
            if to_x < NX:
                route.append((x * NYL + yl, to_x * NYL + to_yl))
    return lax.ppermute(array, ("x", "yl"), route)


def gather_keys(keys, values, doc_ids):
    tok = keys.shape[0]
    docs = jnp.pad(doc_ids.astype(jnp.bfloat16)[None, :], ((0, 15), (0, 0)))
    own = jnp.concatenate([keys, values, docs], axis=0)
    size = own.shape[0]
    one = over_ctx(own, lambda x, yl: (x + 1, yl))
    two = over_ctx(own, lambda x, yl: (x + 2, yl))
    one_other = over_ctx(own, lambda x, yl: (x + 1, 1 - yl))
    other = over_ctx(own, lambda x, yl: (x, 1) if yl == 0 else (x + 2, 0))
    x, yl, z = lax.axis_index("x"), lax.axis_index("yl"), lax.axis_index("z")
    up = jnp.concatenate([other, one_other, one, jnp.where(z == NZ - 1, two, own)], axis=0)
    down = jnp.concatenate([other, one_other, one, jnp.where(z == 0, own, two)], axis=0)
    below = lax.ppermute(up, "z", UP)
    above = lax.ppermute(down, "z", DOWN)
    far = lax.ppermute(jnp.where(z < 2, own, two), "z", FAR)
    far_up = lax.ppermute(below[: 2 * size], "z", UP)
    far_down = lax.ppermute(above[2 * size : 3 * size], "z", DOWN)

    def base(at_x, at_yl, at_z):
        return jnp.where(at_x >= 0, ((at_x * NYL + at_yl) * NZ + at_z) * tok, 1 << 30)

    def column(at_z):
        return [
            base(jnp.where(yl == 1, x, x - 2), 1 - yl, at_z),
            base(x - 1, 1 - yl, at_z),
            base(x - 1, yl, at_z),
            base(jnp.where(at_z < z, x, x - 2), yl, at_z),
        ]

    bases = [base(x, yl, z), base(x - 2, yl, z)] + column(z)[:3]
    for step in (NZ - 1, 1, 2):
        bases += column((z + step) % NZ)
    return (own, two, up, below, above, far_up, far_down, far), jnp.stack(bases), (one, two, one_other, other)


def attention_kernel(base, query, query_doc, own, two, mid, below, above, far_up, far_down, far, out, *scratch):
    rows, keys, vals, bias, scores, peak, total, accum = scratch
    tok = query.shape[0]
    heads = query.shape[1] // HEAD_WIDTH
    width = HEAD_WIDTH
    step = own.shape[0]
    blocks = []
    for ref, count in (
        (own, 1), (two, 1), (mid, 3), (below, 4), (above, 4), (far_up, 2), (far_down, 1), (far, 1)
    ):
        blocks += [(ref, i * step) for i in range(count)]
    per = bias.shape[2] // tok
    wide = per * tok
    for h in range(heads):
        rows[h * tok : (h + 1) * tok] = query[:, h * width : (h + 1) * width]
    query_at = base[0] + lax.broadcasted_iota(jnp.int32, (tok, tok), 0)
    lane = lax.broadcasted_iota(jnp.int32, (tok, tok), 1)
    for i in range(per * bias.shape[0]):
        at = pl.ds(i * tok, tok)
        if i < len(blocks):
            ref, first = blocks[i]
            keys[at] = ref[first : first + tok]
            vals[at] = ref[first + tok : first + 2 * tok]
            docs = ref[first + 2 * tok : first + step].astype(jnp.float32)[0:1]
            allowed = (docs == query_doc[...]) & (base[i] + lane <= query_at)
            mask = jnp.where(allowed, 0.0, -1e30)
        else:
            keys[at] = jnp.zeros((tok, width), jnp.bfloat16)
            vals[at] = jnp.zeros((tok, width), jnp.bfloat16)
            mask = jnp.full((tok, tok), -1e30, jnp.float32)
        bias[i // per, :, (i % per) * tok : (i % per + 1) * tok] = mask
    peak[...] = jnp.full(peak.shape, -1e30, jnp.float32)
    total[...] = jnp.zeros_like(total)
    accum[...] = jnp.zeros_like(accum)

    def lanes(array):
        return [array[:, i * width : (i + 1) * width] for i in range(wide // width)]

    @pl.loop(0, bias.shape[0])
    def _(i):
        at = pl.ds(pl.multiple_of(i * wide, wide), wide)
        value = lax.dot_general(
            rows[...], keys[at], (((1,), (1,)), ((), ())), preferred_element_type=jnp.float32
        )
        value = value.reshape(heads, tok, wide) * (width ** (-0.5)) + bias[i][None]
        value = value.reshape(heads * tok, wide)
        scores[i] = value
        peak[...] = functools.reduce(jnp.maximum, lanes(value), peak[...])

    top = jnp.max(peak[...], axis=1, keepdims=True)
    peak[...] = jnp.broadcast_to(top, peak.shape)

    @pl.loop(0, bias.shape[0])
    def _(i):
        at = pl.ds(pl.multiple_of(i * wide, wide), wide)
        expo = jnp.exp(scores[i] - jnp.concatenate([peak[...]] * (wide // width), axis=1))
        total[...] = functools.reduce(jnp.add, lanes(expo), total[...])
        accum[...] += jnp.dot(
            expo.astype(jnp.bfloat16), vals[at], preferred_element_type=jnp.float32
        )

    result = accum[...] / jnp.sum(total[...], axis=1, keepdims=True)
    for h in range(heads):
        out[:, h * width : (h + 1) * width] = result[h * tok : (h + 1) * tok].astype(out.dtype)


def attention(queries, keys, values, doc_ids):
    tok, columns = queries.shape
    heads = columns // HEAD_WIDTH
    arrays, base, first = gather_keys(keys, values, doc_ids)
    whole = pl.BlockSpec(memory_space=pltpu.VMEM)
    turns, wide = 3, 6 * tok
    out = pl.pallas_call(
        attention_kernel,
        in_specs=[pl.BlockSpec(memory_space=pltpu.SMEM)] + [whole] * (2 + len(arrays)),
        out_specs=whole,
        out_shape=jax.ShapeDtypeStruct(queries.shape, jnp.bfloat16),
        scratch_shapes=[
            pltpu.VMEM((heads * tok, HEAD_WIDTH), jnp.bfloat16),
            pltpu.VMEM((turns * wide, HEAD_WIDTH), jnp.bfloat16),
            pltpu.VMEM((turns * wide, HEAD_WIDTH), jnp.bfloat16),
            pltpu.VMEM((turns, tok, wide), jnp.float32),
            pltpu.VMEM((turns, heads * tok, wide), jnp.float32),
            pltpu.VMEM((heads * tok, HEAD_WIDTH), jnp.float32),
            pltpu.VMEM((heads * tok, HEAD_WIDTH), jnp.float32),
            pltpu.VMEM((heads * tok, HEAD_WIDTH), jnp.float32),
        ],
        compiler_params=pltpu.CompilerParams(vmem_limit_bytes=40 * 1024 * 1024),
        cost_estimate=pl.CostEstimate(
            flops=4 * heads * tok * turns * wide * HEAD_WIDTH,
            bytes_accessed=4 * turns * wide * HEAD_WIDTH,
            transcendentals=heads * tok * turns * wide,
        ),
        name="attention",
    )(base, queries, doc_ids.astype(jnp.float32)[:, None], *arrays)
    return out, first


def gather_projection(out_proj, earlier):
    own = out_proj.T
    other = after(lax.ppermute(own, "yl", SWAP), *earlier)
    first = lax.axis_index("yl") == 0
    pair = jnp.concatenate([jnp.where(first, own, other), jnp.where(first, other, own)], axis=0)
    return lax.all_gather(pair, "x", axis=0, tiled=True)


def project(heads_out, weight):
    tok = heads_out.shape[0]
    width = weight.shape[0]
    depth = width // (NX * NYL)
    rows = tok // (NYH * NC)
    spread = jnp.broadcast_to(heads_out[None], (NZ,) + heads_out.shape)
    all_z = lax.all_to_all(spread, "z", split_axis=0, concat_axis=0, tiled=True)
    part = lax.dot_general(
        all_z.reshape(NZ * tok, -1),
        weight,
        (((1,), (1,)), ((), ())),
        preferred_element_type=jnp.float32,
    ).astype(jnp.bfloat16)
    part = part.reshape(NZ, NYH, NC, rows, width)
    c = lax.axis_index("c")
    got = lax.ppermute(lax.dynamic_index_in_dim(part, 1 - c, 2, False), "c", SWAP)
    part = add(lax.dynamic_index_in_dim(part, c, 2, False), got)
    part = lax.all_to_all(
        part.reshape(NZ * NYH, rows, width), ("z", "yh"), split_axis=0, concat_axis=0, tiled=True
    )
    part = part.reshape(NZ, NYH, rows, NX * NYL, depth)
    total = part[:, 0].astype(jnp.float32) + part[:, 1].astype(jnp.float32)
    return total.transpose(1, 2, 0, 3).reshape(rows, NX * NYL * NZ * depth)


def expert_kernel(count, core_ref, *refs):
    own, other = refs[:count], refs[count : 2 * count]
    gate_w, up_w, down_w = refs[2 * count : 2 * count + 3]
    send, keep = refs[2 * count + 3 : 3 * count + 3], refs[3 * count + 3 : 4 * count + 3]
    gate_sum, up_sum, hidden = refs[4 * count + 3 :]
    step = pl.program_id(0)
    high = own[0].shape[0]

    def contract(parts, first):
        rows = jnp.concatenate([part[...] for part in parts], axis=0)
        gate = jnp.dot(rows, gate_w[...], preferred_element_type=jnp.float32)
        up = jnp.dot(rows, up_w[...], preferred_element_type=jnp.float32)
        if first:
            gate_sum[...], up_sum[...] = gate, up
        else:
            gate_sum[...] += gate
            up_sum[...] += up

    def expand(outs):
        value = jnp.dot(hidden[...], down_w[...], preferred_element_type=jnp.float32)
        for i, out in enumerate(outs):
            out[...] = value[i * high : (i + 1) * high].astype(out.dtype)

    @pl.when(step == 0)
    def _():
        contract(own, True)

    @pl.when(step == 1)
    def _():
        contract(own, False)

    @pl.when((step == 2) | (step == 3))
    def _():
        contract(other, False)

    @pl.when(step == 3)
    def _():
        gate = gate_sum[...]
        hidden[...] = (gate / (1.0 + jnp.exp(-gate)) * up_sum[...]).astype(hidden.dtype)

    @pl.when((step == 4) | (step == 5))
    def _():
        expand(send)

    @pl.when(step >= 6)
    def _():
        expand(keep)


def expert_part(core, own, other, w_gate, w_up, w_down):
    count = len(own)
    high, half = own[0].shape
    quarter = half // 2
    units = w_gate.shape[1]

    def place(first):
        return pl.BlockSpec((high, quarter), lambda s, c: (0, jnp.clip(s - first, 0, 1)))

    def in_quarter(s, c):
        s = jnp.minimum(s, 3)
        return jnp.where(s < 2, 2 * c[0] + s, 2 * (1 - c[0]) + s - 2)

    def out_quarter(s, c):
        s = jnp.maximum(s, 4) - 4
        return jnp.where(s < 2, 2 * (1 - c[0]) + s, 2 * c[0] + s - 2)

    rows = count * high
    outs = pl.pallas_call(
        functools.partial(expert_kernel, count),
        grid_spec=pltpu.PrefetchScalarGridSpec(
            num_scalar_prefetch=1,
            grid=(8,),
            in_specs=[place(0)] * count
            + [place(2)] * count
            + [
                pl.BlockSpec((quarter, units), lambda s, c: (in_quarter(s, c), 0)),
                pl.BlockSpec((quarter, units), lambda s, c: (in_quarter(s, c), 0)),
                pl.BlockSpec((units, quarter), lambda s, c: (0, out_quarter(s, c))),
            ],
            out_specs=[place(4)] * count + [place(6)] * count,
            scratch_shapes=[
                pltpu.VMEM((rows, units), jnp.float32),
                pltpu.VMEM((rows, units), jnp.float32),
                pltpu.VMEM((rows, units), jnp.bfloat16),
            ],
        ),
        out_shape=[jax.ShapeDtypeStruct((high, half), jnp.bfloat16)] * (2 * count),
        compiler_params=pltpu.CompilerParams(vmem_limit_bytes=48 * 1024 * 1024),
        cost_estimate=pl.CostEstimate(
            flops=6 * rows * 2 * half * units,
            bytes_accessed=12 * half * units + 8 * rows * half,
            transcendentals=rows * units,
        ),
        name="expert_part",
    )(core, *own, *other, w_gate, w_up, w_down)
    return outs[:count], outs[count:]


def experts_of(own, w_gate, w_up, w_down):
    c = lax.axis_index("c").astype(jnp.int32).reshape(1)

    def run(*blocks):
        other = [lax.ppermute(block, "c", SWAP) for block in blocks]
        return expert_part(c, blocks, other, w_gate, w_up, w_down)

    def summed(parts):
        send, keep = parts
        return [add(mine, lax.ppermute(his, "c", SWAP)) for mine, his in zip(keep, send)]

    def near(block):
        return lax.ppermute(block, "z", UP), lax.ppermute(block, "z", DOWN)

    def near_back(below, above):
        return lax.ppermute(below, "z", DOWN), lax.ppermute(above, "z", UP)

    over = lax.ppermute(own, "yh", SWAP)
    below, above = near(own)
    over_below = lax.ppermute(over, "z", UP)
    far_own = lax.ppermute(above, "z", DOWN)
    over_above = lax.ppermute(above, "yh", SWAP)
    far_over = lax.ppermute(far_own, "yh", SWAP)
    parts = after(run(own, over, below, above), far_own, over_below, over_above)
    own, over, below, above = summed(parts)
    own_back = near_back(below, above)
    parts = run(after(far_own, own, over, below, above), over_below, over_above)
    far_over = after(far_over, *own_back, parts[1][-1])
    far_own, over_below, over_above = summed(parts)
    over_back = near_back(over_below, over_above)
    last = run(after(far_over, over_below, over_above))
    (last_sum,) = summed(last)
    far_over = lax.ppermute(
        last_sum, ("z", "yh"), [(NYH * a + i, NYH * b + 1 - i) for a, b in FAR for i in range(NYH)]
    )
    far_own = lax.ppermute(after(far_own, *over_back), "z", FAR)
    over = lax.ppermute(add(over, *over_back), "yh", SWAP)
    return add(own, *own_back, far_own, far_over, over)


def per_device(
    stream_in,
    queries,
    rotated_key_heads,
    values,
    doc_ids,
    out_proj,
    norm_gain,
    router,
    w_gate,
    w_up,
    w_down,
    routes,
):
    heads_out, first_keys = attention(queries, rotated_key_heads, values, doc_ids)
    summed = project(heads_out, gather_projection(out_proj, first_keys))
    resid = stream_in.astype(jnp.float32) + summed.astype(jnp.float32)
    width = resid.shape[1]
    normed = (
        resid * lax.rsqrt(jnp.mean(resid * resid, axis=1, keepdims=True) + 1e-05) * norm_gain
    ).astype(jnp.bfloat16)
    logits = jnp.dot(normed.astype(jnp.float32), router, precision=lax.Precision.HIGHEST)
    experts = router.shape[1]
    rows = normed.shape[0]
    cap = 2 * rows * 9 // 32
    slots = experts * cap
    c = lax.axis_index("c")
    half = width // 2

    def columns(array, core):
        return lax.dynamic_slice_in_dim(array, core * half, half, axis=1)

    def in_order(mine, his, axis):
        return jnp.where(
            c == 0,
            jnp.concatenate([mine, his], axis=axis),
            jnp.concatenate([his, mine], axis=axis),
        )

    pair_routes = in_order(routes, lax.ppermute(routes, "c", SWAP), 0)
    pair_normed = in_order(columns(normed, c), lax.ppermute(columns(normed, 1 - c), "c", SWAP), 0)
    rows2 = 2 * rows
    hits = pair_routes[:, :, None] == jnp.arange(experts, dtype=jnp.int32)
    flat_hits = hits.astype(jnp.int32).reshape(rows2 * 2, experts)
    before = jnp.cumsum(flat_hits, axis=0) - flat_hits
    slot = jnp.sum(before.reshape(rows2, 2, experts) * hits.astype(jnp.int32), axis=-1)
    target = pair_routes * cap + slot
    placed = target[:, :, None] == jnp.arange(slots, dtype=jnp.int32)[None, None, :]
    chooser = jnp.any(placed, axis=1).astype(jnp.bfloat16).T
    own_hits = routes[:, :, None] == jnp.arange(experts, dtype=jnp.int32)
    pair_logits = jnp.sum(jnp.where(own_hits, logits[:, None, :], 0.0), axis=-1)
    first_gate = 1.0 / (1.0 + jnp.exp(pair_logits[:, 1] - pair_logits[:, 0]))
    second_gate = 1.0 / (1.0 + jnp.exp(pair_logits[:, 0] - pair_logits[:, 1]))
    own_gates = jnp.stack([first_gate, second_gate], axis=1)
    gate_pair = in_order(own_gates, lax.ppermute(own_gates, "c", SWAP), 0)
    combiner = jnp.sum(jnp.where(placed, gate_pair[:, :, None], 0.0), axis=1)

    packed = jnp.dot(chooser, pair_normed, preferred_element_type=jnp.float32).astype(jnp.bfloat16)
    arrived = lax.all_to_all(
        packed.reshape(experts, cap, half), ("x", "yl"), split_axis=0, concat_axis=0, tiled=True
    ).reshape(slots, half)
    home = experts_of(arrived, w_gate, w_up, w_down)
    returned = lax.all_to_all(
        home.reshape(experts, cap, half), ("x", "yl"), split_axis=0, concat_axis=0, tiled=True
    ).reshape(slots, half)
    mixture = jnp.dot(combiner, returned.astype(jnp.float32), precision=lax.Precision.HIGHEST)
    mine = lax.dynamic_slice_in_dim(mixture, c * rows, rows, axis=0)
    his = lax.dynamic_slice_in_dim(mixture, (1 - c) * rows, rows, axis=0)
    mixture = in_order(mine, lax.ppermute(his, "c", SWAP), 1)
    return (resid + mixture).astype(jnp.bfloat16)


def solution(mesh):
    fine = Mesh(mesh.devices.reshape(NX, NYL, NZ, NYH, NC), ("x", "yl", "z", "yh", "c"))
    ctx, tp = ("x", "yl", "z"), ("yh", "c")
    placed = (
        P(ctx + tp, None),
        P(ctx, tp),
        P(ctx, tp),
        P(ctx, tp),
        P(ctx),
        P(tp, ctx),
        P(),
        P(),
        P(None, ctx + tp),
        P(None, ctx + tp),
        P(ctx + tp, None),
        P(ctx + tp, None),
    )
    return jax.shard_map(
        per_device, mesh=fine, in_specs=placed, out_specs=P(ctx + tp, None), check_vma=False
    )
```

```python
import functools

import jax
import jax.numpy as jnp
from jax import lax
from jax.experimental import pallas as pl
from jax.experimental.pallas import tpu as pltpu
from jax.sharding import Mesh, PartitionSpec as P

HEAD_WIDTH = 128
NX, NYL, NZ, NYH, NC = 4, 2, 4, 2, 2
SWAP = [(0, 1), (1, 0)]
UP = [(i, (i + 1) % NZ) for i in range(NZ)]
DOWN = [((i + 1) % NZ, i) for i in range(NZ)]
FAR = [(i, (i + 2) % NZ) for i in range(NZ)]


def add(*terms):
    total = terms[0].astype(jnp.float32)
    for term in terms[1:]:
        total = total + term.astype(jnp.float32)
    return total.astype(jnp.bfloat16)


def after(value, *others):
    return lax.optimization_barrier((value, *others))[0]


def over_ctx(array, move):
    route = []
    for x in range(NX):
        for yl in range(NYL):
            to_x, to_yl = move(x, yl)
            if to_x < NX:
                route.append((x * NYL + yl, to_x * NYL + to_yl))
    return lax.ppermute(array, ("x", "yl"), route)


def gather_keys(keys, values, doc_ids):
    tok = keys.shape[0]
    docs = jnp.pad(doc_ids.astype(jnp.bfloat16)[None, :], ((0, 15), (0, 0)))
    own = jnp.concatenate([keys, values, docs], axis=0)
    size = own.shape[0]
    one = over_ctx(own, lambda x, yl: (x + 1, yl))
    two = over_ctx(own, lambda x, yl: (x + 2, yl))
    one_other = over_ctx(own, lambda x, yl: (x + 1, 1 - yl))
    other = over_ctx(own, lambda x, yl: (x, 1) if yl == 0 else (x + 2, 0))
    x, yl, z = lax.axis_index("x"), lax.axis_index("yl"), lax.axis_index("z")
    up = jnp.concatenate([other, one_other, one, jnp.where(z == NZ - 1, two, own)], axis=0)
    down = jnp.concatenate([other, one_other, one, jnp.where(z == 0, own, two)], axis=0)
    below = lax.ppermute(up, "z", UP)
    above = lax.ppermute(down, "z", DOWN)
    far = lax.ppermute(jnp.where(z < 2, own, two), "z", FAR)
    far_up = lax.ppermute(below[: 2 * size], "z", UP)
    far_down = lax.ppermute(above[2 * size : 3 * size], "z", DOWN)

    def base(at_x, at_yl, at_z):
        return jnp.where(at_x >= 0, ((at_x * NYL + at_yl) * NZ + at_z) * tok, 1 << 30)

    def column(at_z):
        return [
            base(jnp.where(yl == 1, x, x - 2), 1 - yl, at_z),
            base(x - 1, 1 - yl, at_z),
            base(x - 1, yl, at_z),
            base(jnp.where(at_z < z, x, x - 2), yl, at_z),
        ]

    bases = [base(x, yl, z), base(x - 2, yl, z)] + column(z)[:3]
    for step in (NZ - 1, 1, 2):
        bases += column((z + step) % NZ)
    return (own, two, up, below, above, far_up, far_down, far), jnp.stack(bases), (one, two, one_other, other)


def attention_kernel(base, query, query_doc, own, two, mid, below, above, far_up, far_down, far, out, *scratch):
    rows, keys, vals, bias, scores, peak, total, accum = scratch
    tok = query.shape[0]
    heads = query.shape[1] // HEAD_WIDTH
    width = HEAD_WIDTH
    step = own.shape[0]
    blocks = []
    for ref, count in (
        (own, 1), (two, 1), (mid, 3), (below, 4), (above, 4), (far_up, 2), (far_down, 1), (far, 1)
    ):
        blocks += [(ref, i * step) for i in range(count)]
    per = bias.shape[2] // tok
    wide = per * tok
    for h in range(heads):
        rows[h * tok : (h + 1) * tok] = query[:, h * width : (h + 1) * width]
    query_at = base[0] + lax.broadcasted_iota(jnp.int32, (tok, tok), 0)
    lane = lax.broadcasted_iota(jnp.int32, (tok, tok), 1)
    for i in range(per * bias.shape[0]):
        at = pl.ds(i * tok, tok)
        if i < len(blocks):
            ref, first = blocks[i]
            keys[at] = ref[first : first + tok]
            vals[at] = ref[first + tok : first + 2 * tok]
            docs = ref[first + 2 * tok : first + step].astype(jnp.float32)[0:1]
            allowed = (docs == query_doc[...]) & (base[i] + lane <= query_at)
            mask = jnp.where(allowed, 0.0, -1e30)
        else:
            keys[at] = jnp.zeros((tok, width), jnp.bfloat16)
            vals[at] = jnp.zeros((tok, width), jnp.bfloat16)
            mask = jnp.full((tok, tok), -1e30, jnp.float32)
        bias[i // per, :, (i % per) * tok : (i % per + 1) * tok] = mask
    peak[...] = jnp.full(peak.shape, -1e30, jnp.float32)
    total[...] = jnp.zeros_like(total)
    accum[...] = jnp.zeros_like(accum)

    def lanes(array):
        return [array[:, i * width : (i + 1) * width] for i in range(wide // width)]

    @pl.loop(0, bias.shape[0])
    def _(i):
        at = pl.ds(pl.multiple_of(i * wide, wide), wide)
        value = lax.dot_general(
            rows[...], keys[at], (((1,), (1,)), ((), ())), preferred_element_type=jnp.float32
        )
        value = value.reshape(heads, tok, wide) * (width ** (-0.5)) + bias[i][None]
        value = value.reshape(heads * tok, wide)
        scores[i] = value
        peak[...] = functools.reduce(jnp.maximum, lanes(value), peak[...])

    top = jnp.max(peak[...], axis=1, keepdims=True)
    peak[...] = jnp.broadcast_to(top, peak.shape)

    @pl.loop(0, bias.shape[0])
    def _(i):
        at = pl.ds(pl.multiple_of(i * wide, wide), wide)
        expo = jnp.exp(scores[i] - jnp.concatenate([peak[...]] * (wide // width), axis=1))
        total[...] = functools.reduce(jnp.add, lanes(expo), total[...])
        accum[...] += jnp.dot(
            expo.astype(jnp.bfloat16), vals[at], preferred_element_type=jnp.float32
        )

    result = accum[...] / jnp.sum(total[...], axis=1, keepdims=True)
    for h in range(heads):
        out[:, h * width : (h + 1) * width] = result[h * tok : (h + 1) * tok].astype(out.dtype)


def attention(queries, keys, values, doc_ids):
    tok, columns = queries.shape
    heads = columns // HEAD_WIDTH
    arrays, base, first = gather_keys(keys, values, doc_ids)
    whole = pl.BlockSpec(memory_space=pltpu.VMEM)
    turns, wide = 3, 6 * tok
    out = pl.pallas_call(
        attention_kernel,
        in_specs=[pl.BlockSpec(memory_space=pltpu.SMEM)] + [whole] * (2 + len(arrays)),
        out_specs=whole,
        out_shape=jax.ShapeDtypeStruct(queries.shape, jnp.bfloat16),
        scratch_shapes=[
            pltpu.VMEM((heads * tok, HEAD_WIDTH), jnp.bfloat16),
            pltpu.VMEM((turns * wide, HEAD_WIDTH), jnp.bfloat16),
            pltpu.VMEM((turns * wide, HEAD_WIDTH), jnp.bfloat16),
            pltpu.VMEM((turns, tok, wide), jnp.float32),
            pltpu.VMEM((turns, heads * tok, wide), jnp.float32),
            pltpu.VMEM((heads * tok, HEAD_WIDTH), jnp.float32),
            pltpu.VMEM((heads * tok, HEAD_WIDTH), jnp.float32),
            pltpu.VMEM((heads * tok, HEAD_WIDTH), jnp.float32),
        ],
        compiler_params=pltpu.CompilerParams(vmem_limit_bytes=40 * 1024 * 1024),
        cost_estimate=pl.CostEstimate(
            flops=4 * heads * tok * turns * wide * HEAD_WIDTH,
            bytes_accessed=4 * turns * wide * HEAD_WIDTH,
            transcendentals=heads * tok * turns * wide,
        ),
        name="attention",
    )(base, queries, doc_ids.astype(jnp.float32)[:, None], *arrays)
    return out, first


def gather_projection(out_proj, earlier):
    own = out_proj.T
    other = after(lax.ppermute(own, "yl", SWAP), *earlier)
    first = lax.axis_index("yl") == 0
    pair = jnp.concatenate([jnp.where(first, own, other), jnp.where(first, other, own)], axis=0)
    return lax.all_gather(pair, "x", axis=0, tiled=True)


def project(heads_out, weight):
    tok = heads_out.shape[0]
    width = weight.shape[0]
    depth = width // (NX * NYL)
    rows = tok // (NYH * NC)
    spread = jnp.broadcast_to(heads_out[None], (NZ,) + heads_out.shape)
    all_z = lax.all_to_all(spread, "z", split_axis=0, concat_axis=0, tiled=True)
    part = lax.dot_general(
        all_z.reshape(NZ * tok, -1),
        weight,
        (((1,), (1,)), ((), ())),
        preferred_element_type=jnp.float32,
    ).astype(jnp.bfloat16)
    part = part.reshape(NZ, NYH, NC, rows, width)
    c = lax.axis_index("c")
    got = lax.ppermute(lax.dynamic_index_in_dim(part, 1 - c, 2, False), "c", SWAP)
    part = add(lax.dynamic_index_in_dim(part, c, 2, False), got)
    part = lax.all_to_all(
        part.reshape(NZ * NYH, rows, width), ("z", "yh"), split_axis=0, concat_axis=0, tiled=True
    )
    part = part.reshape(NZ, NYH, rows, NX * NYL, depth)
    total = part[:, 0].astype(jnp.float32) + part[:, 1].astype(jnp.float32)
    return total.transpose(1, 2, 0, 3).reshape(rows, NX * NYL * NZ * depth)


def expert_kernel(count, core_ref, *refs):
    own, other = refs[:count], refs[count : 2 * count]
    gate_w, up_w, down_w = refs[2 * count : 2 * count + 3]
    send, keep = refs[2 * count + 3 : 3 * count + 3], refs[3 * count + 3 : 4 * count + 3]
    gate_sum, up_sum, hidden = refs[4 * count + 3 :]
    step = pl.program_id(0)
    high = own[0].shape[0]

    def contract(parts, first):
        rows = jnp.concatenate([part[...] for part in parts], axis=0)
        gate = jnp.dot(rows, gate_w[...], preferred_element_type=jnp.float32)
        up = jnp.dot(rows, up_w[...], preferred_element_type=jnp.float32)
        if first:
            gate_sum[...], up_sum[...] = gate, up
        else:
            gate_sum[...] += gate
            up_sum[...] += up

    def expand(outs):
        value = jnp.dot(hidden[...], down_w[...], preferred_element_type=jnp.float32)
        for i, out in enumerate(outs):
            out[...] = value[i * high : (i + 1) * high].astype(out.dtype)

    @pl.when(step == 0)
    def _():
        contract(own, True)

    @pl.when(step == 1)
    def _():
        contract(own, False)

    @pl.when((step == 2) | (step == 3))
    def _():
        contract(other, False)

    @pl.when(step == 3)
    def _():
        gate = gate_sum[...]
        hidden[...] = (gate / (1.0 + jnp.exp(-gate)) * up_sum[...]).astype(hidden.dtype)

    @pl.when((step == 4) | (step == 5))
    def _():
        expand(send)

    @pl.when(step >= 6)
    def _():
        expand(keep)


def expert_part(core, own, other, w_gate, w_up, w_down):
    count = len(own)
    high, half = own[0].shape
    quarter = half // 2
    units = w_gate.shape[1]

    def place(first):
        return pl.BlockSpec((high, quarter), lambda s, c: (0, jnp.clip(s - first, 0, 1)))

    def in_quarter(s, c):
        s = jnp.minimum(s, 3)
        return jnp.where(s < 2, 2 * c[0] + s, 2 * (1 - c[0]) + s - 2)

    def out_quarter(s, c):
        s = jnp.maximum(s, 4) - 4
        return jnp.where(s < 2, 2 * (1 - c[0]) + s, 2 * c[0] + s - 2)

    rows = count * high
    outs = pl.pallas_call(
        functools.partial(expert_kernel, count),
        grid_spec=pltpu.PrefetchScalarGridSpec(
            num_scalar_prefetch=1,
            grid=(8,),
            in_specs=[place(0)] * count
            + [place(2)] * count
            + [
                pl.BlockSpec((quarter, units), lambda s, c: (in_quarter(s, c), 0)),
                pl.BlockSpec((quarter, units), lambda s, c: (in_quarter(s, c), 0)),
                pl.BlockSpec((units, quarter), lambda s, c: (0, out_quarter(s, c))),
            ],
            out_specs=[place(4)] * count + [place(6)] * count,
            scratch_shapes=[
                pltpu.VMEM((rows, units), jnp.float32),
                pltpu.VMEM((rows, units), jnp.float32),
                pltpu.VMEM((rows, units), jnp.bfloat16),
            ],
        ),
        out_shape=[jax.ShapeDtypeStruct((high, half), jnp.bfloat16)] * (2 * count),
        compiler_params=pltpu.CompilerParams(vmem_limit_bytes=48 * 1024 * 1024),
        cost_estimate=pl.CostEstimate(
            flops=6 * rows * 2 * half * units,
            bytes_accessed=12 * half * units + 8 * rows * half,
            transcendentals=rows * units,
        ),
        name="expert_part",
    )(core, *own, *other, w_gate, w_up, w_down)
    return outs[:count], outs[count:]


def experts_of(own, w_gate, w_up, w_down):
    c = lax.axis_index("c").astype(jnp.int32).reshape(1)

    def run(*blocks):
        other = [lax.ppermute(block, "c", SWAP) for block in blocks]
        return expert_part(c, blocks, other, w_gate, w_up, w_down)

    def summed(parts):
        send, keep = parts
        return [add(mine, lax.ppermute(his, "c", SWAP)) for mine, his in zip(keep, send)]

    def near(block):
        return lax.ppermute(block, "z", UP), lax.ppermute(block, "z", DOWN)

    def near_back(below, above):
        return lax.ppermute(below, "z", DOWN), lax.ppermute(above, "z", UP)

    over = lax.ppermute(own, "yh", SWAP)
    below, above = near(own)
    over_below = lax.ppermute(over, "z", UP)
    far_own = lax.ppermute(above, "z", DOWN)
    over_above = lax.ppermute(above, "yh", SWAP)
    far_over = lax.ppermute(far_own, "yh", SWAP)
    first = run(own)
    second = run(after(over, first[1][0]), after(below, first[1][0]), after(above, first[1][0]))
    second = after(second, far_own, over_below, over_above)
    (own,) = summed(first)
    over, below, above = summed(second)
    own_back = near_back(below, above)
    third = run(after(far_own, below, above), over_below, over_above)
    last = run(after(far_over, *own_back, third[1][-1]))
    far_own, over_below, over_above = summed(third)
    over_back = near_back(over_below, over_above)
    (far_over,) = summed(last)
    far_own = add(far_own, lax.ppermute(far_over, "yh", SWAP))
    over = lax.ppermute(add(over, *over_back), "yh", SWAP)
    far_own = lax.ppermute(after(far_own, *over_back), "z", FAR)
    return add(own, *own_back, far_own, over)


def per_device(
    stream_in,
    queries,
    rotated_key_heads,
    values,
    doc_ids,
    out_proj,
    norm_gain,
    router,
    w_gate,
    w_up,
    w_down,
    routes,
):
    heads_out, first_keys = attention(queries, rotated_key_heads, values, doc_ids)
    summed = project(heads_out, gather_projection(out_proj, first_keys))
    resid = stream_in.astype(jnp.float32) + summed.astype(jnp.float32)
    width = resid.shape[1]
    normed = (
        resid * lax.rsqrt(jnp.mean(resid * resid, axis=1, keepdims=True) + 1e-05) * norm_gain
    ).astype(jnp.bfloat16)
    logits = jnp.dot(normed.astype(jnp.float32), router, precision=lax.Precision.HIGHEST)
    experts = router.shape[1]
    rows = normed.shape[0]
    cap = 2 * rows * 9 // 32
    slots = experts * cap
    c = lax.axis_index("c")
    half = width // 2

    def columns(array, core):
        return lax.dynamic_slice_in_dim(array, core * half, half, axis=1)

    def in_order(mine, his, axis):
        return jnp.where(
            c == 0,
            jnp.concatenate([mine, his], axis=axis),
            jnp.concatenate([his, mine], axis=axis),
        )

    pair_routes = in_order(routes, lax.ppermute(routes, "c", SWAP), 0)
    pair_normed = in_order(columns(normed, c), lax.ppermute(columns(normed, 1 - c), "c", SWAP), 0)
    rows2 = 2 * rows
    hits = pair_routes[:, :, None] == jnp.arange(experts, dtype=jnp.int32)
    flat_hits = hits.astype(jnp.int32).reshape(rows2 * 2, experts)
    before = jnp.cumsum(flat_hits, axis=0) - flat_hits
    slot = jnp.sum(before.reshape(rows2, 2, experts) * hits.astype(jnp.int32), axis=-1)
    target = pair_routes * cap + slot
    placed = target[:, :, None] == jnp.arange(slots, dtype=jnp.int32)[None, None, :]
    chooser = jnp.any(placed, axis=1).astype(jnp.bfloat16).T
    own_hits = routes[:, :, None] == jnp.arange(experts, dtype=jnp.int32)
    pair_logits = jnp.sum(jnp.where(own_hits, logits[:, None, :], 0.0), axis=-1)
    first_gate = 1.0 / (1.0 + jnp.exp(pair_logits[:, 1] - pair_logits[:, 0]))
    second_gate = 1.0 / (1.0 + jnp.exp(pair_logits[:, 0] - pair_logits[:, 1]))
    own_gates = jnp.stack([first_gate, second_gate], axis=1)
    gate_pair = in_order(own_gates, lax.ppermute(own_gates, "c", SWAP), 0)
    combiner = jnp.sum(jnp.where(placed, gate_pair[:, :, None], 0.0), axis=1)

    packed = jnp.dot(chooser, pair_normed, preferred_element_type=jnp.float32).astype(jnp.bfloat16)
    arrived = lax.all_to_all(
        packed.reshape(experts, cap, half), ("x", "yl"), split_axis=0, concat_axis=0, tiled=True
    ).reshape(slots, half)
    home = experts_of(arrived, w_gate, w_up, w_down)
    returned = lax.all_to_all(
        home.reshape(experts, cap, half), ("x", "yl"), split_axis=0, concat_axis=0, tiled=True
    ).reshape(slots, half)
    mixture = jnp.dot(combiner, returned.astype(jnp.float32), precision=lax.Precision.HIGHEST)
    mine = lax.dynamic_slice_in_dim(mixture, c * rows, rows, axis=0)
    his = lax.dynamic_slice_in_dim(mixture, (1 - c) * rows, rows, axis=0)
    mixture = in_order(mine, lax.ppermute(his, "c", SWAP), 1)
    return (resid + mixture).astype(jnp.bfloat16)


def solution(mesh):
    fine = Mesh(mesh.devices.reshape(NX, NYL, NZ, NYH, NC), ("x", "yl", "z", "yh", "c"))
    ctx, tp = ("x", "yl", "z"), ("yh", "c")
    placed = (
        P(ctx + tp, None),
        P(ctx, tp),
        P(ctx, tp),
        P(ctx, tp),
        P(ctx),
        P(tp, ctx),
        P(),
        P(),
        P(None, ctx + tp),
        P(None, ctx + tp),
        P(ctx + tp, None),
        P(ctx + tp, None),
    )
    return jax.shard_map(
        per_device, mesh=fine, in_specs=placed, out_specs=P(ctx + tp, None), check_vma=False
    )
```

```python
import functools

import jax
import jax.numpy as jnp
from jax import lax
from jax.experimental import pallas as pl
from jax.experimental.pallas import tpu as pltpu
from jax.sharding import Mesh, PartitionSpec as P

HEAD_WIDTH = 128
NX, NYL, NZ, NYH, NC = 4, 2, 4, 2, 2
SWAP = [(0, 1), (1, 0)]
UP = [(i, (i + 1) % NZ) for i in range(NZ)]
DOWN = [((i + 1) % NZ, i) for i in range(NZ)]
FAR = [(i, (i + 2) % NZ) for i in range(NZ)]


def add(*terms):
    total = terms[0].astype(jnp.float32)
    for term in terms[1:]:
        total = total + term.astype(jnp.float32)
    return total.astype(jnp.bfloat16)


def after(value, *others):
    return lax.optimization_barrier((value, *others))[0]


def over_ctx(array, move):
    route = []
    for x in range(NX):
        for yl in range(NYL):
            to_x, to_yl = move(x, yl)
            if to_x < NX:
                route.append((x * NYL + yl, to_x * NYL + to_yl))
    return lax.ppermute(array, ("x", "yl"), route)


def gather_keys(keys, values, doc_ids):
    tok = keys.shape[0]
    docs = jnp.pad(doc_ids.astype(jnp.bfloat16)[None, :], ((0, 15), (0, 0)))
    own = jnp.concatenate([keys, values, docs], axis=0)
    size = own.shape[0]
    one = over_ctx(own, lambda x, yl: (x + 1, yl))
    two = over_ctx(own, lambda x, yl: (x + 2, yl))
    one_other = over_ctx(own, lambda x, yl: (x + 1, 1 - yl))
    other = over_ctx(own, lambda x, yl: (x, 1) if yl == 0 else (x + 2, 0))
    x, yl, z = lax.axis_index("x"), lax.axis_index("yl"), lax.axis_index("z")
    up = jnp.concatenate([other, one_other, one, jnp.where(z == NZ - 1, two, own)], axis=0)
    down = jnp.concatenate([other, one_other, one, jnp.where(z == 0, own, two)], axis=0)
    below = lax.ppermute(up, "z", UP)
    above = lax.ppermute(down, "z", DOWN)
    far = lax.ppermute(jnp.where(z < 2, own, two), "z", FAR)
    far_up = lax.ppermute(below[: 2 * size], "z", UP)
    far_down = lax.ppermute(above[2 * size : 3 * size], "z", DOWN)

    def base(at_x, at_yl, at_z):
        return jnp.where(at_x >= 0, ((at_x * NYL + at_yl) * NZ + at_z) * tok, 1 << 30)

    def column(at_z):
        return [
            base(jnp.where(yl == 1, x, x - 2), 1 - yl, at_z),
            base(x - 1, 1 - yl, at_z),
            base(x - 1, yl, at_z),
            base(jnp.where(at_z < z, x, x - 2), yl, at_z),
        ]

    bases = [base(x, yl, z), base(x - 2, yl, z)] + column(z)[:3]
    for step in (NZ - 1, 1, 2):
        bases += column((z + step) % NZ)
    return (own, two, up, below, above, far_up, far_down, far), jnp.stack(bases), (one, two, one_other, other)


def attention_kernel(base, query, query_doc, own, two, mid, below, above, far_up, far_down, far, out, *scratch):
    rows, keys, vals, bias, scores, peak, total, accum = scratch
    tok = query.shape[0]
    heads = query.shape[1] // HEAD_WIDTH
    width = HEAD_WIDTH
    step = own.shape[0]
    blocks = []
    for ref, count in (
        (own, 1), (two, 1), (mid, 3), (below, 4), (above, 4), (far_up, 2), (far_down, 1), (far, 1)
    ):
        blocks += [(ref, i * step) for i in range(count)]
    per = bias.shape[2] // tok
    wide = per * tok
    for h in range(heads):
        rows[h * tok : (h + 1) * tok] = query[:, h * width : (h + 1) * width]
    query_at = base[0] + lax.broadcasted_iota(jnp.int32, (tok, tok), 0)
    lane = lax.broadcasted_iota(jnp.int32, (tok, tok), 1)
    for i in range(per * bias.shape[0]):
        at = pl.ds(i * tok, tok)
        if i < len(blocks):
            ref, first = blocks[i]
            keys[at] = ref[first : first + tok]
            vals[at] = ref[first + tok : first + 2 * tok]
            docs = ref[first + 2 * tok : first + step].astype(jnp.float32)[0:1]
            allowed = (docs == query_doc[...]) & (base[i] + lane <= query_at)
            mask = jnp.where(allowed, 0.0, -1e30)
        else:
            keys[at] = jnp.zeros((tok, width), jnp.bfloat16)
            vals[at] = jnp.zeros((tok, width), jnp.bfloat16)
            mask = jnp.full((tok, tok), -1e30, jnp.float32)
        bias[i // per, :, (i % per) * tok : (i % per + 1) * tok] = mask
    peak[...] = jnp.full(peak.shape, -1e30, jnp.float32)
    total[...] = jnp.zeros_like(total)
    accum[...] = jnp.zeros_like(accum)

    def lanes(array):
        return [array[:, i * width : (i + 1) * width] for i in range(wide // width)]

    @pl.loop(0, bias.shape[0])
    def _(i):
        at = pl.ds(pl.multiple_of(i * wide, wide), wide)
        value = lax.dot_general(
            rows[...], keys[at], (((1,), (1,)), ((), ())), preferred_element_type=jnp.float32
        )
        value = value.reshape(heads, tok, wide) * (width ** (-0.5)) + bias[i][None]
        value = value.reshape(heads * tok, wide)
        scores[i] = value
        peak[...] = functools.reduce(jnp.maximum, lanes(value), peak[...])

    top = jnp.max(peak[...], axis=1, keepdims=True)
    peak[...] = jnp.broadcast_to(top, peak.shape)

    @pl.loop(0, bias.shape[0])
    def _(i):
        at = pl.ds(pl.multiple_of(i * wide, wide), wide)
        expo = jnp.exp(scores[i] - jnp.concatenate([peak[...]] * (wide // width), axis=1))
        total[...] = functools.reduce(jnp.add, lanes(expo), total[...])
        accum[...] += jnp.dot(
            expo.astype(jnp.bfloat16), vals[at], preferred_element_type=jnp.float32
        )

    result = accum[...] / jnp.sum(total[...], axis=1, keepdims=True)
    for h in range(heads):
        out[:, h * width : (h + 1) * width] = result[h * tok : (h + 1) * tok].astype(out.dtype)


def attention(queries, keys, values, doc_ids):
    tok, columns = queries.shape
    heads = columns // HEAD_WIDTH
    arrays, base, first = gather_keys(keys, values, doc_ids)
    whole = pl.BlockSpec(memory_space=pltpu.VMEM)
    turns, wide = 3, 6 * tok
    out = pl.pallas_call(
        attention_kernel,
        in_specs=[pl.BlockSpec(memory_space=pltpu.SMEM)] + [whole] * (2 + len(arrays)),
        out_specs=whole,
        out_shape=jax.ShapeDtypeStruct(queries.shape, jnp.bfloat16),
        scratch_shapes=[
            pltpu.VMEM((heads * tok, HEAD_WIDTH), jnp.bfloat16),
            pltpu.VMEM((turns * wide, HEAD_WIDTH), jnp.bfloat16),
            pltpu.VMEM((turns * wide, HEAD_WIDTH), jnp.bfloat16),
            pltpu.VMEM((turns, tok, wide), jnp.float32),
            pltpu.VMEM((turns, heads * tok, wide), jnp.float32),
            pltpu.VMEM((heads * tok, HEAD_WIDTH), jnp.float32),
            pltpu.VMEM((heads * tok, HEAD_WIDTH), jnp.float32),
            pltpu.VMEM((heads * tok, HEAD_WIDTH), jnp.float32),
        ],
        compiler_params=pltpu.CompilerParams(vmem_limit_bytes=28 * 1024 * 1024),
        cost_estimate=pl.CostEstimate(
            flops=4 * heads * tok * turns * wide * HEAD_WIDTH,
            bytes_accessed=4 * turns * wide * HEAD_WIDTH,
            transcendentals=heads * tok * turns * wide,
        ),
        name="attention",
    )(base, queries, doc_ids.astype(jnp.float32)[:, None], *arrays)
    return out, first


def gather_projection(out_proj, earlier):
    own = out_proj.T
    other = after(lax.ppermute(own, "yl", SWAP), *earlier)
    first = lax.axis_index("yl") == 0
    pair = jnp.concatenate([jnp.where(first, own, other), jnp.where(first, other, own)], axis=0)
    return lax.all_gather(pair, "x", axis=0, tiled=True)


def project(heads_out, weight):
    tok = heads_out.shape[0]
    width = weight.shape[0]
    depth = width // (NX * NYL)
    rows = tok // (NYH * NC)
    spread = jnp.broadcast_to(heads_out[None], (NZ,) + heads_out.shape)
    all_z = lax.all_to_all(spread, "z", split_axis=0, concat_axis=0, tiled=True)
    part = lax.dot_general(
        all_z.reshape(NZ * tok, -1),
        weight,
        (((1,), (1,)), ((), ())),
        preferred_element_type=jnp.float32,
    ).astype(jnp.bfloat16)
    part = part.reshape(NZ, NYH, NC, rows, width)
    c = lax.axis_index("c")
    got = lax.ppermute(lax.dynamic_index_in_dim(part, 1 - c, 2, False), "c", SWAP)
    part = add(lax.dynamic_index_in_dim(part, c, 2, False), got)
    part = lax.all_to_all(
        part.reshape(NZ * NYH, rows, width), ("z", "yh"), split_axis=0, concat_axis=0, tiled=True
    )
    part = part.reshape(NZ, NYH, rows, NX * NYL, depth)
    total = part[:, 0].astype(jnp.float32) + part[:, 1].astype(jnp.float32)
    return total.transpose(1, 2, 0, 3).reshape(rows, NX * NYL * NZ * depth)


def expert_kernel(count, core_ref, *refs):
    own, other = refs[:count], refs[count : 2 * count]
    gate_w, up_w, down_w = refs[2 * count : 2 * count + 3]
    send, keep = refs[2 * count + 3 : 3 * count + 3], refs[3 * count + 3 : 4 * count + 3]
    gate_sum, up_sum, hidden = refs[4 * count + 3 :]
    step = pl.program_id(0)
    high = own[0].shape[0]

    def contract(parts, first):
        rows = jnp.concatenate([part[...] for part in parts], axis=0)
        gate = jnp.dot(rows, gate_w[...], preferred_element_type=jnp.float32)
        up = jnp.dot(rows, up_w[...], preferred_element_type=jnp.float32)
        if first:
            gate_sum[...], up_sum[...] = gate, up
        else:
            gate_sum[...] += gate
            up_sum[...] += up

    def expand(outs):
        value = jnp.dot(hidden[...], down_w[...], preferred_element_type=jnp.float32)
        for i, out in enumerate(outs):
            out[...] = value[i * high : (i + 1) * high].astype(out.dtype)

    @pl.when(step == 0)
    def _():
        contract(own, True)

    @pl.when(step == 1)
    def _():
        contract(own, False)

    @pl.when((step == 2) | (step == 3))
    def _():
        contract(other, False)

    @pl.when(step == 3)
    def _():
        gate = gate_sum[...]
        hidden[...] = (gate / (1.0 + jnp.exp(-gate)) * up_sum[...]).astype(hidden.dtype)

    @pl.when((step == 4) | (step == 5))
    def _():
        expand(send)

    @pl.when(step >= 6)
    def _():
        expand(keep)


def expert_part(core, own, other, w_gate, w_up, w_down):
    count = len(own)
    high, half = own[0].shape
    quarter = half // 2
    units = w_gate.shape[1]

    def place(first):
        return pl.BlockSpec((high, quarter), lambda s, c: (0, jnp.clip(s - first, 0, 1)))

    def in_quarter(s, c):
        s = jnp.minimum(s, 3)
        return jnp.where(s < 2, 2 * c[0] + s, 2 * (1 - c[0]) + s - 2)

    def out_quarter(s, c):
        s = jnp.maximum(s, 4) - 4
        return jnp.where(s < 2, 2 * (1 - c[0]) + s, 2 * c[0] + s - 2)

    rows = count * high
    outs = pl.pallas_call(
        functools.partial(expert_kernel, count),
        grid_spec=pltpu.PrefetchScalarGridSpec(
            num_scalar_prefetch=1,
            grid=(8,),
            in_specs=[place(0)] * count
            + [place(2)] * count
            + [
                pl.BlockSpec((quarter, units), lambda s, c: (in_quarter(s, c), 0)),
                pl.BlockSpec((quarter, units), lambda s, c: (in_quarter(s, c), 0)),
                pl.BlockSpec((units, quarter), lambda s, c: (0, out_quarter(s, c))),
            ],
            out_specs=[place(4)] * count + [place(6)] * count,
            scratch_shapes=[
                pltpu.VMEM((rows, units), jnp.float32),
                pltpu.VMEM((rows, units), jnp.float32),
                pltpu.VMEM((rows, units), jnp.bfloat16),
            ],
        ),
        out_shape=[jax.ShapeDtypeStruct((high, half), jnp.bfloat16)] * (2 * count),
        compiler_params=pltpu.CompilerParams(vmem_limit_bytes=32 * 1024 * 1024),
        cost_estimate=pl.CostEstimate(
            flops=6 * rows * 2 * half * units,
            bytes_accessed=12 * half * units + 8 * rows * half,
            transcendentals=rows * units,
        ),
        name="expert_part",
    )(core, *own, *other, w_gate, w_up, w_down)
    return outs[:count], outs[count:]


def experts_of(own, w_gate, w_up, w_down):
    c = lax.axis_index("c").astype(jnp.int32).reshape(1)

    def run(*blocks):
        other = [lax.ppermute(block, "c", SWAP) for block in blocks]
        return expert_part(c, blocks, other, w_gate, w_up, w_down)

    def summed(parts):
        send, keep = parts
        return [add(mine, lax.ppermute(his, "c", SWAP)) for mine, his in zip(keep, send)]

    def near(block):
        return lax.ppermute(block, "z", UP), lax.ppermute(block, "z", DOWN)

    def near_back(below, above):
        return lax.ppermute(below, "z", DOWN), lax.ppermute(above, "z", UP)

    over = lax.ppermute(own, "yh", SWAP)
    below, above = near(own)
    over_below = lax.ppermute(over, "z", UP)
    far_own = lax.ppermute(above, "z", DOWN)
    over_above = lax.ppermute(above, "yh", SWAP)
    far_over = lax.ppermute(far_own, "yh", SWAP)
    first = run(own)
    second = run(after(over, first[1][0]), after(below, first[1][0]), after(above, first[1][0]))
    second = after(second, far_own, over_below, over_above)
    (own,) = summed(first)
    over, below, above = summed(second)
    own_back = near_back(below, above)
    third = run(after(far_own, below, above), over_below, over_above)
    last = run(after(far_over, *own_back, third[1][-1]))
    far_own, over_below, over_above = summed(third)
    over_back = near_back(over_below, over_above)
    (far_over,) = summed(last)
    far_own = add(far_own, lax.ppermute(far_over, "yh", SWAP))
    over = lax.ppermute(add(over, *over_back), "yh", SWAP)
    far_own = lax.ppermute(after(far_own, *over_back), "z", FAR)
    return add(own, *own_back, far_own, over)


def per_device(
    stream_in,
    queries,
    rotated_key_heads,
    values,
    doc_ids,
    out_proj,
    norm_gain,
    router,
    w_gate,
    w_up,
    w_down,
    routes,
):
    heads_out, first_keys = attention(queries, rotated_key_heads, values, doc_ids)
    summed = project(heads_out, gather_projection(out_proj, first_keys))
    resid = stream_in.astype(jnp.float32) + summed.astype(jnp.float32)
    width = resid.shape[1]
    normed = (
        resid * lax.rsqrt(jnp.mean(resid * resid, axis=1, keepdims=True) + 1e-05) * norm_gain
    ).astype(jnp.bfloat16)
    logits = jnp.dot(normed.astype(jnp.float32), router, precision=lax.Precision.HIGHEST)
    experts = router.shape[1]
    rows = normed.shape[0]
    cap = 2 * rows * 9 // 32
    slots = experts * cap
    c = lax.axis_index("c")
    half = width // 2

    def columns(array, core):
        return lax.dynamic_slice_in_dim(array, core * half, half, axis=1)

    def in_order(mine, his, axis):
        return jnp.where(
            c == 0,
            jnp.concatenate([mine, his], axis=axis),
            jnp.concatenate([his, mine], axis=axis),
        )

    pair_routes = in_order(routes, lax.ppermute(routes, "c", SWAP), 0)
    pair_normed = in_order(columns(normed, c), lax.ppermute(columns(normed, 1 - c), "c", SWAP), 0)
    rows2 = 2 * rows
    hits = pair_routes[:, :, None] == jnp.arange(experts, dtype=jnp.int32)
    flat_hits = hits.astype(jnp.int32).reshape(rows2 * 2, experts)
    before = jnp.cumsum(flat_hits, axis=0) - flat_hits
    slot = jnp.sum(before.reshape(rows2, 2, experts) * hits.astype(jnp.int32), axis=-1)
    target = pair_routes * cap + slot
    placed = target[:, :, None] == jnp.arange(slots, dtype=jnp.int32)[None, None, :]
    chooser = jnp.any(placed, axis=1).astype(jnp.bfloat16).T
    own_hits = routes[:, :, None] == jnp.arange(experts, dtype=jnp.int32)
    pair_logits = jnp.sum(jnp.where(own_hits, logits[:, None, :], 0.0), axis=-1)
    first_gate = 1.0 / (1.0 + jnp.exp(pair_logits[:, 1] - pair_logits[:, 0]))
    second_gate = 1.0 / (1.0 + jnp.exp(pair_logits[:, 0] - pair_logits[:, 1]))
    own_gates = jnp.stack([first_gate, second_gate], axis=1)
    gate_pair = in_order(own_gates, lax.ppermute(own_gates, "c", SWAP), 0)
    combiner = jnp.sum(jnp.where(placed, gate_pair[:, :, None], 0.0), axis=1)

    packed = jnp.dot(chooser, pair_normed, preferred_element_type=jnp.float32).astype(jnp.bfloat16)
    arrived = lax.all_to_all(
        packed.reshape(experts, cap, half), ("x", "yl"), split_axis=0, concat_axis=0, tiled=True
    ).reshape(slots, half)
    home = experts_of(arrived, w_gate, w_up, w_down)
    returned = lax.all_to_all(
        home.reshape(experts, cap, half), ("x", "yl"), split_axis=0, concat_axis=0, tiled=True
    ).reshape(slots, half)
    mixture = jnp.dot(combiner, returned.astype(jnp.float32), precision=lax.Precision.HIGHEST)
    mine = lax.dynamic_slice_in_dim(mixture, c * rows, rows, axis=0)
    his = lax.dynamic_slice_in_dim(mixture, (1 - c) * rows, rows, axis=0)
    mixture = in_order(mine, lax.ppermute(his, "c", SWAP), 1)
    return (resid + mixture).astype(jnp.bfloat16)


def solution(mesh):
    fine = Mesh(mesh.devices.reshape(NX, NYL, NZ, NYH, NC), ("x", "yl", "z", "yh", "c"))
    ctx, tp = ("x", "yl", "z"), ("yh", "c")
    placed = (
        P(ctx + tp, None),
        P(ctx, tp),
        P(ctx, tp),
        P(ctx, tp),
        P(ctx),
        P(tp, ctx),
        P(),
        P(),
        P(None, ctx + tp),
        P(None, ctx + tp),
        P(ctx + tp, None),
        P(ctx + tp, None),
    )
    return jax.shard_map(
        per_device, mesh=fine, in_specs=placed, out_specs=P(ctx + tp, None), check_vma=False
    )
```

```python
import functools

import jax
import jax.numpy as jnp
from jax import lax
from jax.experimental import pallas as pl
from jax.experimental.pallas import tpu as pltpu
from jax.sharding import Mesh, PartitionSpec as P

HEAD_WIDTH = 128
NX, NYL, NZ, NYH, NC = 4, 2, 4, 2, 2
SWAP = [(0, 1), (1, 0)]
UP = [(i, (i + 1) % NZ) for i in range(NZ)]
DOWN = [((i + 1) % NZ, i) for i in range(NZ)]
FAR = [(i, (i + 2) % NZ) for i in range(NZ)]


def add(*terms):
    total = terms[0].astype(jnp.float32)
    for term in terms[1:]:
        total = total + term.astype(jnp.float32)
    return total.astype(jnp.bfloat16)


def after(value, *others):
    return lax.optimization_barrier((value, *others))[0]


def over_ctx(array, move):
    route = []
    for x in range(NX):
        for yl in range(NYL):
            to_x, to_yl = move(x, yl)
            if to_x < NX:
                route.append((x * NYL + yl, to_x * NYL + to_yl))
    return lax.ppermute(array, ("x", "yl"), route)


def gather_keys(keys, values, doc_ids):
    tok = keys.shape[0]
    docs = jnp.pad(doc_ids.astype(jnp.bfloat16)[None, :], ((0, 15), (0, 0)))
    own = jnp.concatenate([keys, values, docs], axis=0)
    size = own.shape[0]
    one = over_ctx(own, lambda x, yl: (x + 1, yl))
    two = over_ctx(own, lambda x, yl: (x + 2, yl))
    one_other = over_ctx(own, lambda x, yl: (x + 1, 1 - yl))
    other = over_ctx(own, lambda x, yl: (x, 1) if yl == 0 else (x + 2, 0))
    x, yl, z = lax.axis_index("x"), lax.axis_index("yl"), lax.axis_index("z")
    up = jnp.concatenate([other, one_other, one, jnp.where(z == NZ - 1, two, own)], axis=0)
    down = jnp.concatenate([other, one_other, one, jnp.where(z == 0, own, two)], axis=0)
    below = lax.ppermute(up, "z", UP)
    above = lax.ppermute(down, "z", DOWN)
    far = lax.ppermute(jnp.where(z < 2, own, two), "z", FAR)
    far_up = lax.ppermute(below[: 2 * size], "z", UP)
    far_down = lax.ppermute(above[2 * size : 3 * size], "z", DOWN)

    def base(at_x, at_yl, at_z):
        return jnp.where(at_x >= 0, ((at_x * NYL + at_yl) * NZ + at_z) * tok, 1 << 30)

    def column(at_z):
        return [
            base(jnp.where(yl == 1, x, x - 2), 1 - yl, at_z),
            base(x - 1, 1 - yl, at_z),
            base(x - 1, yl, at_z),
            base(jnp.where(at_z < z, x, x - 2), yl, at_z),
        ]

    bases = [base(x, yl, z), base(x - 2, yl, z)] + column(z)[:3]
    for step in (NZ - 1, 1, 2):
        bases += column((z + step) % NZ)
    return (own, two, up, below, above, far_up, far_down, far), jnp.stack(bases), (one, two, one_other, other)


def attention_kernel(base, query, query_doc, own, two, mid, below, above, far_up, far_down, far, out, *scratch):
    rows, keys, vals, bias, scores, peak, total, accum = scratch
    tok = query.shape[0]
    heads = query.shape[1] // HEAD_WIDTH
    width = HEAD_WIDTH
    step = own.shape[0]
    blocks = []
    for ref, count in (
        (own, 1), (two, 1), (mid, 3), (below, 4), (above, 4), (far_up, 2), (far_down, 1), (far, 1)
    ):
        blocks += [(ref, i * step) for i in range(count)]
    per = bias.shape[2] // tok
    wide = per * tok
    for h in range(heads):
        rows[h * tok : (h + 1) * tok] = query[:, h * width : (h + 1) * width]
    query_at = base[0] + lax.broadcasted_iota(jnp.int32, (tok, tok), 0)
    lane = lax.broadcasted_iota(jnp.int32, (tok, tok), 1)
    for i in range(per * bias.shape[0]):
        at = pl.ds(i * tok, tok)
        if i < len(blocks):
            ref, first = blocks[i]
            keys[at] = ref[first : first + tok]
            vals[at] = ref[first + tok : first + 2 * tok]
            docs = ref[first + 2 * tok : first + step].astype(jnp.float32)[0:1]
            allowed = (docs == query_doc[...]) & (base[i] + lane <= query_at)
            mask = jnp.where(allowed, 0.0, -1e30)
        else:
            keys[at] = jnp.zeros((tok, width), jnp.bfloat16)
            vals[at] = jnp.zeros((tok, width), jnp.bfloat16)
            mask = jnp.full((tok, tok), -1e30, jnp.float32)
        bias[i // per, :, (i % per) * tok : (i % per + 1) * tok] = mask
    peak[...] = jnp.full(peak.shape, -1e30, jnp.float32)
    total[...] = jnp.zeros_like(total)
    accum[...] = jnp.zeros_like(accum)

    def lanes(array):
        return [array[:, i * width : (i + 1) * width] for i in range(wide // width)]

    @pl.loop(0, bias.shape[0])
    def _(i):
        at = pl.ds(pl.multiple_of(i * wide, wide), wide)
        value = lax.dot_general(
            rows[...], keys[at], (((1,), (1,)), ((), ())), preferred_element_type=jnp.float32
        )
        value = value.reshape(heads, tok, wide) * (width ** (-0.5)) + bias[i][None]
        value = value.reshape(heads * tok, wide)
        scores[i] = value
        peak[...] = functools.reduce(jnp.maximum, lanes(value), peak[...])

    top = jnp.max(peak[...], axis=1, keepdims=True)
    peak[...] = jnp.broadcast_to(top, peak.shape)

    @pl.loop(0, bias.shape[0])
    def _(i):
        at = pl.ds(pl.multiple_of(i * wide, wide), wide)
        expo = jnp.exp(scores[i] - jnp.concatenate([peak[...]] * (wide // width), axis=1))
        total[...] = functools.reduce(jnp.add, lanes(expo), total[...])
        accum[...] += jnp.dot(
            expo.astype(jnp.bfloat16), vals[at], preferred_element_type=jnp.float32
        )

    result = accum[...] / jnp.sum(total[...], axis=1, keepdims=True)
    for h in range(heads):
        out[:, h * width : (h + 1) * width] = result[h * tok : (h + 1) * tok].astype(out.dtype)


def attention(queries, keys, values, doc_ids):
    tok, columns = queries.shape
    heads = columns // HEAD_WIDTH
    arrays, base, first = gather_keys(keys, values, doc_ids)
    whole = pl.BlockSpec(memory_space=pltpu.VMEM)
    turns, wide = 3, 6 * tok
    out = pl.pallas_call(
        attention_kernel,
        in_specs=[pl.BlockSpec(memory_space=pltpu.SMEM)] + [whole] * (2 + len(arrays)),
        out_specs=whole,
        out_shape=jax.ShapeDtypeStruct(queries.shape, jnp.bfloat16),
        scratch_shapes=[
            pltpu.VMEM((heads * tok, HEAD_WIDTH), jnp.bfloat16),
            pltpu.VMEM((turns * wide, HEAD_WIDTH), jnp.bfloat16),
            pltpu.VMEM((turns * wide, HEAD_WIDTH), jnp.bfloat16),
            pltpu.VMEM((turns, tok, wide), jnp.float32),
            pltpu.VMEM((turns, heads * tok, wide), jnp.float32),
            pltpu.VMEM((heads * tok, HEAD_WIDTH), jnp.float32),
            pltpu.VMEM((heads * tok, HEAD_WIDTH), jnp.float32),
            pltpu.VMEM((heads * tok, HEAD_WIDTH), jnp.float32),
        ],
        compiler_params=pltpu.CompilerParams(vmem_limit_bytes=28 * 1024 * 1024),
        cost_estimate=pl.CostEstimate(
            flops=4 * heads * tok * turns * wide * HEAD_WIDTH,
            bytes_accessed=4 * turns * wide * HEAD_WIDTH,
            transcendentals=heads * tok * turns * wide,
        ),
        name="attention",
    )(base, queries, doc_ids.astype(jnp.float32)[:, None], *arrays)
    return out, first


def gather_projection(out_proj, earlier):
    own = out_proj.T
    other = after(lax.ppermute(own, "yl", SWAP), *earlier)
    first = lax.axis_index("yl") == 0
    pair = jnp.concatenate([jnp.where(first, own, other), jnp.where(first, other, own)], axis=0)
    return lax.all_gather(pair, "x", axis=0, tiled=True)


def project(heads_out, weight):
    tok = heads_out.shape[0]
    width = weight.shape[0]
    depth = width // (NX * NYL)
    rows = tok // (NYH * NC)
    spread = jnp.broadcast_to(heads_out[None], (NZ,) + heads_out.shape)
    all_z = lax.all_to_all(spread, "z", split_axis=0, concat_axis=0, tiled=True)
    part = lax.dot_general(
        all_z.reshape(NZ * tok, -1),
        weight,
        (((1,), (1,)), ((), ())),
        preferred_element_type=jnp.float32,
    ).astype(jnp.bfloat16)
    part = part.reshape(NZ, NYH, NC, rows, width)
    c = lax.axis_index("c")
    got = lax.ppermute(lax.dynamic_index_in_dim(part, 1 - c, 2, False), "c", SWAP)
    part = add(lax.dynamic_index_in_dim(part, c, 2, False), got)
    part = lax.all_to_all(
        part.reshape(NZ * NYH, rows, width), ("z", "yh"), split_axis=0, concat_axis=0, tiled=True
    )
    part = part.reshape(NZ, NYH, rows, NX * NYL, depth)
    total = part[:, 0].astype(jnp.float32) + part[:, 1].astype(jnp.float32)
    return total.transpose(1, 2, 0, 3).reshape(rows, NX * NYL * NZ * depth)


def expert_kernel(count, core_ref, *refs):
    own, other = refs[:count], refs[count : 2 * count]
    gate_w, up_w, down_w = refs[2 * count : 2 * count + 3]
    send, keep = refs[2 * count + 3 : 3 * count + 3], refs[3 * count + 3 : 4 * count + 3]
    gate_sum, up_sum, hidden = refs[4 * count + 3 :]
    step = pl.program_id(0)
    high = own[0].shape[0]

    def contract(parts, first):
        rows = jnp.concatenate([part[...] for part in parts], axis=0)
        gate = jnp.dot(rows, gate_w[...], preferred_element_type=jnp.float32)
        up = jnp.dot(rows, up_w[...], preferred_element_type=jnp.float32)
        if first:
            gate_sum[...], up_sum[...] = gate, up
        else:
            gate_sum[...] += gate
            up_sum[...] += up

    def expand(outs):
        value = jnp.dot(hidden[...], down_w[...], preferred_element_type=jnp.float32)
        for i, out in enumerate(outs):
            out[...] = value[i * high : (i + 1) * high].astype(out.dtype)

    @pl.when(step == 0)
    def _():
        contract(own, True)

    @pl.when(step == 1)
    def _():
        contract(own, False)

    @pl.when((step == 2) | (step == 3))
    def _():
        contract(other, False)

    @pl.when(step == 3)
    def _():
        gate = gate_sum[...]
        hidden[...] = (gate / (1.0 + jnp.exp(-gate)) * up_sum[...]).astype(hidden.dtype)

    @pl.when((step == 4) | (step == 5))
    def _():
        expand(send)

    @pl.when(step >= 6)
    def _():
        expand(keep)


def expert_part(core, own, other, w_gate, w_up, w_down):
    count = len(own)
    high, half = own[0].shape
    quarter = half // 2
    units = w_gate.shape[1]

    def place(first):
        return pl.BlockSpec((high, quarter), lambda s, c: (0, jnp.clip(s - first, 0, 1)))

    def in_quarter(s, c):
        s = jnp.minimum(s, 3)
        return jnp.where(s < 2, 2 * c[0] + s, 2 * (1 - c[0]) + s - 2)

    def out_quarter(s, c):
        s = jnp.maximum(s, 4) - 4
        return jnp.where(s < 2, 2 * (1 - c[0]) + s, 2 * c[0] + s - 2)

    rows = count * high
    outs = pl.pallas_call(
        functools.partial(expert_kernel, count),
        grid_spec=pltpu.PrefetchScalarGridSpec(
            num_scalar_prefetch=1,
            grid=(8,),
            in_specs=[place(0)] * count
            + [place(2)] * count
            + [
                pl.BlockSpec((quarter, units), lambda s, c: (in_quarter(s, c), 0)),
                pl.BlockSpec((quarter, units), lambda s, c: (in_quarter(s, c), 0)),
                pl.BlockSpec((units, quarter), lambda s, c: (0, out_quarter(s, c))),
            ],
            out_specs=[place(4)] * count + [place(6)] * count,
            scratch_shapes=[
                pltpu.VMEM((rows, units), jnp.float32),
                pltpu.VMEM((rows, units), jnp.float32),
                pltpu.VMEM((rows, units), jnp.bfloat16),
            ],
        ),
        out_shape=[jax.ShapeDtypeStruct((high, half), jnp.bfloat16)] * (2 * count),
        compiler_params=pltpu.CompilerParams(vmem_limit_bytes=(30 if count > 1 else 20) * 1024 * 1024),
        cost_estimate=pl.CostEstimate(
            flops=6 * rows * 2 * half * units,
            bytes_accessed=12 * half * units + 8 * rows * half,
            transcendentals=rows * units,
        ),
        name="expert_part",
    )(core, *own, *other, w_gate, w_up, w_down)
    return outs[:count], outs[count:]


def experts_of(own, w_gate, w_up, w_down):
    c = lax.axis_index("c").astype(jnp.int32).reshape(1)

    def run(*blocks):
        other = [lax.ppermute(block, "c", SWAP) for block in blocks]
        return expert_part(c, blocks, other, w_gate, w_up, w_down)

    def summed(parts):
        send, keep = parts
        return [add(mine, lax.ppermute(his, "c", SWAP)) for mine, his in zip(keep, send)]

    def near(block):
        return lax.ppermute(block, "z", UP), lax.ppermute(block, "z", DOWN)

    def near_back(below, above):
        return lax.ppermute(below, "z", DOWN), lax.ppermute(above, "z", UP)

    over = lax.ppermute(own, "yh", SWAP)
    below, above = near(own)
    over_below = lax.ppermute(over, "z", UP)
    far_own = lax.ppermute(above, "z", DOWN)
    over_above = lax.ppermute(above, "yh", SWAP)
    far_over = lax.ppermute(far_own, "yh", SWAP)
    first = run(own)
    second = run(after(over, first[1][0]), after(below, first[1][0]), after(above, first[1][0]))
    second = after(second, far_own, over_below, over_above)
    (own,) = summed(first)
    over, below, above = summed(second)
    own_back = near_back(below, above)
    third = run(after(far_own, below, above), over_below, over_above)
    last = run(after(far_over, *own_back, third[1][-1]))
    far_own, over_below, over_above = summed(third)
    over_back = near_back(over_below, over_above)
    (far_over,) = summed(last)
    far_own = add(far_own, lax.ppermute(far_over, "yh", SWAP))
    over = lax.ppermute(add(over, *over_back), "yh", SWAP)
    far_own = lax.ppermute(after(far_own, *over_back), "z", FAR)
    return add(own, *own_back, far_own, over)


def per_device(
    stream_in,
    queries,
    rotated_key_heads,
    values,
    doc_ids,
    out_proj,
    norm_gain,
    router,
    w_gate,
    w_up,
    w_down,
    routes,
):
    heads_out, first_keys = attention(queries, rotated_key_heads, values, doc_ids)
    summed = project(heads_out, gather_projection(out_proj, first_keys))
    resid = stream_in.astype(jnp.float32) + summed.astype(jnp.float32)
    width = resid.shape[1]
    normed = (
        resid * lax.rsqrt(jnp.mean(resid * resid, axis=1, keepdims=True) + 1e-05) * norm_gain
    ).astype(jnp.bfloat16)
    logits = jnp.dot(normed.astype(jnp.float32), router, precision=lax.Precision.HIGHEST)
    experts = router.shape[1]
    rows = normed.shape[0]
    cap = 2 * rows * 9 // 32
    slots = experts * cap
    c = lax.axis_index("c")
    half = width // 2

    def columns(array, core):
        return lax.dynamic_slice_in_dim(array, core * half, half, axis=1)

    def in_order(mine, his, axis):
        return jnp.where(
            c == 0,
            jnp.concatenate([mine, his], axis=axis),
            jnp.concatenate([his, mine], axis=axis),
        )

    pair_routes = in_order(routes, lax.ppermute(routes, "c", SWAP), 0)
    pair_normed = in_order(columns(normed, c), lax.ppermute(columns(normed, 1 - c), "c", SWAP), 0)
    rows2 = 2 * rows
    hits = pair_routes[:, :, None] == jnp.arange(experts, dtype=jnp.int32)
    flat_hits = hits.astype(jnp.int32).reshape(rows2 * 2, experts)
    before = jnp.cumsum(flat_hits, axis=0) - flat_hits
    slot = jnp.sum(before.reshape(rows2, 2, experts) * hits.astype(jnp.int32), axis=-1)
    target = pair_routes * cap + slot
    placed = target[:, :, None] == jnp.arange(slots, dtype=jnp.int32)[None, None, :]
    chooser = jnp.any(placed, axis=1).astype(jnp.bfloat16).T
    own_hits = routes[:, :, None] == jnp.arange(experts, dtype=jnp.int32)
    pair_logits = jnp.sum(jnp.where(own_hits, logits[:, None, :], 0.0), axis=-1)
    first_gate = 1.0 / (1.0 + jnp.exp(pair_logits[:, 1] - pair_logits[:, 0]))
    second_gate = 1.0 / (1.0 + jnp.exp(pair_logits[:, 0] - pair_logits[:, 1]))
    own_gates = jnp.stack([first_gate, second_gate], axis=1)
    gate_pair = in_order(own_gates, lax.ppermute(own_gates, "c", SWAP), 0)
    combiner = jnp.sum(jnp.where(placed, gate_pair[:, :, None], 0.0), axis=1)

    packed = jnp.dot(chooser, pair_normed, preferred_element_type=jnp.float32).astype(jnp.bfloat16)
    arrived = lax.all_to_all(
        packed.reshape(experts, cap, half), ("x", "yl"), split_axis=0, concat_axis=0, tiled=True
    ).reshape(slots, half)
    home = experts_of(arrived, w_gate, w_up, w_down)
    returned = lax.all_to_all(
        home.reshape(experts, cap, half), ("x", "yl"), split_axis=0, concat_axis=0, tiled=True
    ).reshape(slots, half)
    mixture = jnp.dot(combiner, returned.astype(jnp.float32), precision=lax.Precision.HIGHEST)
    mine = lax.dynamic_slice_in_dim(mixture, c * rows, rows, axis=0)
    his = lax.dynamic_slice_in_dim(mixture, (1 - c) * rows, rows, axis=0)
    mixture = in_order(mine, lax.ppermute(his, "c", SWAP), 1)
    return (resid + mixture).astype(jnp.bfloat16)


def solution(mesh):
    fine = Mesh(mesh.devices.reshape(NX, NYL, NZ, NYH, NC), ("x", "yl", "z", "yh", "c"))
    ctx, tp = ("x", "yl", "z"), ("yh", "c")
    placed = (
        P(ctx + tp, None),
        P(ctx, tp),
        P(ctx, tp),
        P(ctx, tp),
        P(ctx),
        P(tp, ctx),
        P(),
        P(),
        P(None, ctx + tp),
        P(None, ctx + tp),
        P(ctx + tp, None),
        P(ctx + tp, None),
    )
    return jax.shard_map(
        per_device, mesh=fine, in_specs=placed, out_specs=P(ctx + tp, None), check_vma=False
    )
```

```python
import functools

import jax
import jax.numpy as jnp
from jax import lax
from jax.experimental import pallas as pl
from jax.experimental.pallas import tpu as pltpu
from jax.sharding import Mesh, PartitionSpec as P

HEAD_WIDTH = 128
NX, NYL, NZ, NYH, NC = 4, 2, 4, 2, 2
SWAP = [(0, 1), (1, 0)]
UP = [(i, (i + 1) % NZ) for i in range(NZ)]
DOWN = [((i + 1) % NZ, i) for i in range(NZ)]
FAR = [(i, (i + 2) % NZ) for i in range(NZ)]


def add(*terms):
    total = terms[0].astype(jnp.float32)
    for term in terms[1:]:
        total = total + term.astype(jnp.float32)
    return total.astype(jnp.bfloat16)


def after(value, *others):
    return lax.optimization_barrier((value, *others))[0]


def over_ctx(array, move):
    route = []
    for x in range(NX):
        for yl in range(NYL):
            to_x, to_yl = move(x, yl)
            if to_x < NX:
                route.append((x * NYL + yl, to_x * NYL + to_yl))
    return lax.ppermute(array, ("x", "yl"), route)


def gather_keys(keys, values, doc_ids):
    tok = keys.shape[0]
    docs = jnp.pad(doc_ids.astype(jnp.bfloat16)[None, :], ((0, 15), (0, 0)))
    own = jnp.concatenate([keys, values, docs], axis=0)
    size = own.shape[0]
    one = over_ctx(own, lambda x, yl: (x + 1, yl))
    two = over_ctx(own, lambda x, yl: (x + 2, yl))
    one_other = over_ctx(own, lambda x, yl: (x + 1, 1 - yl))
    other = over_ctx(own, lambda x, yl: (x, 1) if yl == 0 else (x + 2, 0))
    x, yl, z = lax.axis_index("x"), lax.axis_index("yl"), lax.axis_index("z")
    up = jnp.concatenate([other, one_other, one, jnp.where(z == NZ - 1, two, own)], axis=0)
    down = jnp.concatenate([other, one_other, one, jnp.where(z == 0, own, two)], axis=0)
    below = lax.ppermute(up, "z", UP)
    above = lax.ppermute(down, "z", DOWN)
    far = lax.ppermute(jnp.where(z < 2, own, two), "z", FAR)
    far_up = lax.ppermute(below[: 2 * size], "z", UP)
    far_down = lax.ppermute(above[2 * size : 3 * size], "z", DOWN)

    def base(at_x, at_yl, at_z):
        return jnp.where(at_x >= 0, ((at_x * NYL + at_yl) * NZ + at_z) * tok, 1 << 30)

    def column(at_z):
        return [
            base(jnp.where(yl == 1, x, x - 2), 1 - yl, at_z),
            base(x - 1, 1 - yl, at_z),
            base(x - 1, yl, at_z),
            base(jnp.where(at_z < z, x, x - 2), yl, at_z),
        ]

    bases = [base(x, yl, z), base(x - 2, yl, z)] + column(z)[:3]
    for step in (NZ - 1, 1, 2):
        bases += column((z + step) % NZ)
    return (own, two, up, below, above, far_up, far_down, far), jnp.stack(bases), (one, two, one_other, other)


def attention_kernel(base, query, query_doc, own, two, mid, below, above, far_up, far_down, far, out, *scratch):
    rows, keys, vals, bias, scores, peak, total, accum = scratch
    tok = query.shape[0]
    heads = query.shape[1] // HEAD_WIDTH
    width = HEAD_WIDTH
    step = own.shape[0]
    blocks = []
    for ref, count in (
        (own, 1), (two, 1), (mid, 3), (below, 4), (above, 4), (far_up, 2), (far_down, 1), (far, 1)
    ):
        blocks += [(ref, i * step) for i in range(count)]
    per = bias.shape[2] // tok
    wide = per * tok
    for h in range(heads):
        rows[h * tok : (h + 1) * tok] = query[:, h * width : (h + 1) * width]
    query_at = base[0] + lax.broadcasted_iota(jnp.int32, (tok, tok), 0)
    lane = lax.broadcasted_iota(jnp.int32, (tok, tok), 1)
    for i in range(per * bias.shape[0]):
        at = pl.ds(i * tok, tok)
        if i < len(blocks):
            ref, first = blocks[i]
            keys[at] = ref[first : first + tok]
            vals[at] = ref[first + tok : first + 2 * tok]
            docs = ref[first + 2 * tok : first + step].astype(jnp.float32)[0:1]
            allowed = (docs == query_doc[...]) & (base[i] + lane <= query_at)
            mask = jnp.where(allowed, 0.0, -1e30)
        else:
            keys[at] = jnp.zeros((tok, width), jnp.bfloat16)
            vals[at] = jnp.zeros((tok, width), jnp.bfloat16)
            mask = jnp.full((tok, tok), -1e30, jnp.float32)
        bias[i // per, :, (i % per) * tok : (i % per + 1) * tok] = mask
    peak[...] = jnp.full(peak.shape, -1e30, jnp.float32)
    total[...] = jnp.zeros_like(total)
    accum[...] = jnp.zeros_like(accum)

    def lanes(array):
        return [array[:, i * width : (i + 1) * width] for i in range(wide // width)]

    @pl.loop(0, bias.shape[0])
    def _(i):
        at = pl.ds(pl.multiple_of(i * wide, wide), wide)
        value = lax.dot_general(
            rows[...], keys[at], (((1,), (1,)), ((), ())), preferred_element_type=jnp.float32
        )
        value = value.reshape(heads, tok, wide) * (width ** (-0.5)) + bias[i][None]
        value = value.reshape(heads * tok, wide)
        scores[i] = value
        peak[...] = functools.reduce(jnp.maximum, lanes(value), peak[...])

    top = jnp.max(peak[...], axis=1, keepdims=True)
    peak[...] = jnp.broadcast_to(top, peak.shape)

    @pl.loop(0, bias.shape[0])
    def _(i):
        at = pl.ds(pl.multiple_of(i * wide, wide), wide)
        expo = jnp.exp(scores[i] - jnp.concatenate([peak[...]] * (wide // width), axis=1))
        total[...] = functools.reduce(jnp.add, lanes(expo), total[...])
        accum[...] += jnp.dot(
            expo.astype(jnp.bfloat16), vals[at], preferred_element_type=jnp.float32
        )

    result = accum[...] / jnp.sum(total[...], axis=1, keepdims=True)
    for h in range(heads):
        out[:, h * width : (h + 1) * width] = result[h * tok : (h + 1) * tok].astype(out.dtype)


def attention(queries, keys, values, doc_ids):
    tok, columns = queries.shape
    heads = columns // HEAD_WIDTH
    arrays, base, first = gather_keys(keys, values, doc_ids)
    whole = pl.BlockSpec(memory_space=pltpu.VMEM)
    turns, wide = 3, 6 * tok
    out = pl.pallas_call(
        attention_kernel,
        in_specs=[pl.BlockSpec(memory_space=pltpu.SMEM)] + [whole] * (2 + len(arrays)),
        out_specs=whole,
        out_shape=jax.ShapeDtypeStruct(queries.shape, jnp.bfloat16),
        scratch_shapes=[
            pltpu.VMEM((heads * tok, HEAD_WIDTH), jnp.bfloat16),
            pltpu.VMEM((turns * wide, HEAD_WIDTH), jnp.bfloat16),
            pltpu.VMEM((turns * wide, HEAD_WIDTH), jnp.bfloat16),
            pltpu.VMEM((turns, tok, wide), jnp.float32),
            pltpu.VMEM((turns, heads * tok, wide), jnp.float32),
            pltpu.VMEM((heads * tok, HEAD_WIDTH), jnp.float32),
            pltpu.VMEM((heads * tok, HEAD_WIDTH), jnp.float32),
            pltpu.VMEM((heads * tok, HEAD_WIDTH), jnp.float32),
        ],
        compiler_params=pltpu.CompilerParams(vmem_limit_bytes=28 * 1024 * 1024),
        cost_estimate=pl.CostEstimate(
            flops=4 * heads * tok * turns * wide * HEAD_WIDTH,
            bytes_accessed=4 * turns * wide * HEAD_WIDTH,
            transcendentals=heads * tok * turns * wide,
        ),
        name="attention",
    )(base, queries, doc_ids.astype(jnp.float32)[:, None], *arrays)
    return out, first


def gather_projection(out_proj, earlier):
    own = out_proj.T
    other = after(lax.ppermute(own, "yl", SWAP), *earlier)
    first = lax.axis_index("yl") == 0
    pair = jnp.concatenate([jnp.where(first, own, other), jnp.where(first, other, own)], axis=0)
    return lax.all_gather(pair, "x", axis=0, tiled=True)


def project(heads_out, weight):
    tok = heads_out.shape[0]
    width = weight.shape[0]
    depth = width // (NX * NYL)
    rows = tok // (NYH * NC)
    spread = jnp.broadcast_to(heads_out[None], (NZ,) + heads_out.shape)
    all_z = lax.all_to_all(spread, "z", split_axis=0, concat_axis=0, tiled=True)
    part = lax.dot_general(
        all_z.reshape(NZ * tok, -1),
        weight,
        (((1,), (1,)), ((), ())),
        preferred_element_type=jnp.float32,
    ).astype(jnp.bfloat16)
    part = part.reshape(NZ, NYH, NC, rows, width)
    c = lax.axis_index("c")
    got = lax.ppermute(lax.dynamic_index_in_dim(part, 1 - c, 2, False), "c", SWAP)
    part = add(lax.dynamic_index_in_dim(part, c, 2, False), got)
    part = lax.all_to_all(
        part.reshape(NZ * NYH, rows, width), ("z", "yh"), split_axis=0, concat_axis=0, tiled=True
    )
    part = part.reshape(NZ, NYH, rows, NX * NYL, depth)
    total = part[:, 0].astype(jnp.float32) + part[:, 1].astype(jnp.float32)
    return total.transpose(1, 2, 0, 3).reshape(rows, NX * NYL * NZ * depth)


def expert_kernel(count, core_ref, *refs):
    own, other = refs[:count], refs[count : 2 * count]
    gate_w, up_w, down_w = refs[2 * count : 2 * count + 3]
    send, keep = refs[2 * count + 3 : 3 * count + 3], refs[3 * count + 3 : 4 * count + 3]
    gate_sum, up_sum, hidden = refs[4 * count + 3 :]
    step = pl.program_id(0)
    high = own[0].shape[0]

    def contract(parts, first):
        rows = jnp.concatenate([part[...] for part in parts], axis=0)
        gate = jnp.dot(rows, gate_w[...], preferred_element_type=jnp.float32)
        up = jnp.dot(rows, up_w[...], preferred_element_type=jnp.float32)
        if first:
            gate_sum[...], up_sum[...] = gate, up
        else:
            gate_sum[...] += gate
            up_sum[...] += up

    def expand(outs):
        value = jnp.dot(hidden[...], down_w[...], preferred_element_type=jnp.float32)
        for i, out in enumerate(outs):
            out[...] = value[i * high : (i + 1) * high].astype(out.dtype)

    @pl.when(step == 0)
    def _():
        contract(own, True)

    @pl.when(step == 1)
    def _():
        contract(own, False)

    @pl.when((step == 2) | (step == 3))
    def _():
        contract(other, False)

    @pl.when(step == 3)
    def _():
        gate = gate_sum[...]
        hidden[...] = (gate / (1.0 + jnp.exp(-gate)) * up_sum[...]).astype(hidden.dtype)

    @pl.when((step == 4) | (step == 5))
    def _():
        expand(send)

    @pl.when(step >= 6)
    def _():
        expand(keep)


def expert_part(core, own, other, w_gate, w_up, w_down):
    count = len(own)
    high, half = own[0].shape
    quarter = half // 2
    units = w_gate.shape[1]

    def place(first):
        return pl.BlockSpec((high, quarter), lambda s, c: (0, jnp.clip(s - first, 0, 1)))

    def in_quarter(s, c):
        s = jnp.minimum(s, 3)
        return jnp.where(s < 2, 2 * c[0] + s, 2 * (1 - c[0]) + s - 2)

    def out_quarter(s, c):
        s = jnp.maximum(s, 4) - 4
        return jnp.where(s < 2, 2 * (1 - c[0]) + s, 2 * c[0] + s - 2)

    rows = count * high
    outs = pl.pallas_call(
        functools.partial(expert_kernel, count),
        grid_spec=pltpu.PrefetchScalarGridSpec(
            num_scalar_prefetch=1,
            grid=(8,),
            in_specs=[place(0)] * count
            + [place(2)] * count
            + [
                pl.BlockSpec((quarter, units), lambda s, c: (in_quarter(s, c), 0)),
                pl.BlockSpec((quarter, units), lambda s, c: (in_quarter(s, c), 0)),
                pl.BlockSpec((units, quarter), lambda s, c: (0, out_quarter(s, c))),
            ],
            out_specs=[place(4)] * count + [place(6)] * count,
            scratch_shapes=[
                pltpu.VMEM((rows, units), jnp.float32),
                pltpu.VMEM((rows, units), jnp.float32),
                pltpu.VMEM((rows, units), jnp.bfloat16),
            ],
        ),
        out_shape=[jax.ShapeDtypeStruct((high, half), jnp.bfloat16)] * (2 * count),
        compiler_params=pltpu.CompilerParams(vmem_limit_bytes=32 * 1024 * 1024),
        cost_estimate=pl.CostEstimate(
            flops=6 * rows * 2 * half * units if count > 1 else 1,
            bytes_accessed=12 * half * units + 8 * rows * half,
            transcendentals=rows * units,
        ),
        name="expert_part",
    )(core, *own, *other, w_gate, w_up, w_down)
    return outs[:count], outs[count:]


def experts_of(own, w_gate, w_up, w_down):
    c = lax.axis_index("c").astype(jnp.int32).reshape(1)

    def run(*blocks):
        other = [lax.ppermute(block, "c", SWAP) for block in blocks]
        return expert_part(c, blocks, other, w_gate, w_up, w_down)

    def summed(parts):
        send, keep = parts
        return [add(mine, lax.ppermute(his, "c", SWAP)) for mine, his in zip(keep, send)]

    def near(block):
        return lax.ppermute(block, "z", UP), lax.ppermute(block, "z", DOWN)

    def near_back(below, above):
        return lax.ppermute(below, "z", DOWN), lax.ppermute(above, "z", UP)

    over = lax.ppermute(own, "yh", SWAP)
    below, above = near(own)
    over_below = lax.ppermute(over, "z", UP)
    far_own = lax.ppermute(above, "z", DOWN)
    over_above = lax.ppermute(above, "yh", SWAP)
    far_over = lax.ppermute(far_own, "yh", SWAP)
    first = run(own)
    second = run(after(over, first[1][0]), after(below, first[1][0]), after(above, first[1][0]))
    second = after(second, far_own, over_below, over_above)
    (own,) = summed(first)
    over, below, above = summed(second)
    own_back = near_back(below, above)
    third = run(after(far_own, below, above), over_below, over_above)
    last = run(after(far_over, third[1][-1]))
    far_own, over_below, over_above = summed(after(third, *own_back))
    over_back = near_back(over_below, over_above)
    (far_over,) = summed(last)
    far_own = add(far_own, lax.ppermute(far_over, "yh", SWAP))
    over = lax.ppermute(add(over, *over_back), "yh", SWAP)
    far_own = lax.ppermute(after(far_own, *over_back), "z", FAR)
    return add(own, *own_back, far_own, over)


def per_device(
    stream_in,
    queries,
    rotated_key_heads,
    values,
    doc_ids,
    out_proj,
    norm_gain,
    router,
    w_gate,
    w_up,
    w_down,
    routes,
):
    heads_out, first_keys = attention(queries, rotated_key_heads, values, doc_ids)
    summed = project(heads_out, gather_projection(out_proj, first_keys))
    resid = stream_in.astype(jnp.float32) + summed.astype(jnp.float32)
    width = resid.shape[1]
    normed = (
        resid * lax.rsqrt(jnp.mean(resid * resid, axis=1, keepdims=True) + 1e-05) * norm_gain
    ).astype(jnp.bfloat16)
    logits = jnp.dot(normed.astype(jnp.float32), router, precision=lax.Precision.HIGHEST)
    experts = router.shape[1]
    rows = normed.shape[0]
    cap = 2 * rows * 9 // 32
    slots = experts * cap
    c = lax.axis_index("c")
    half = width // 2

    def columns(array, core):
        return lax.dynamic_slice_in_dim(array, core * half, half, axis=1)

    def in_order(mine, his, axis):
        return jnp.where(
            c == 0,
            jnp.concatenate([mine, his], axis=axis),
            jnp.concatenate([his, mine], axis=axis),
        )

    pair_routes = in_order(routes, lax.ppermute(routes, "c", SWAP), 0)
    pair_normed = in_order(columns(normed, c), lax.ppermute(columns(normed, 1 - c), "c", SWAP), 0)
    rows2 = 2 * rows
    hits = pair_routes[:, :, None] == jnp.arange(experts, dtype=jnp.int32)
    flat_hits = hits.astype(jnp.int32).reshape(rows2 * 2, experts)
    before = jnp.cumsum(flat_hits, axis=0) - flat_hits
    slot = jnp.sum(before.reshape(rows2, 2, experts) * hits.astype(jnp.int32), axis=-1)
    target = pair_routes * cap + slot
    placed = target[:, :, None] == jnp.arange(slots, dtype=jnp.int32)[None, None, :]
    chooser = jnp.any(placed, axis=1).astype(jnp.bfloat16).T
    own_hits = routes[:, :, None] == jnp.arange(experts, dtype=jnp.int32)
    pair_logits = jnp.sum(jnp.where(own_hits, logits[:, None, :], 0.0), axis=-1)
    first_gate = 1.0 / (1.0 + jnp.exp(pair_logits[:, 1] - pair_logits[:, 0]))
    second_gate = 1.0 / (1.0 + jnp.exp(pair_logits[:, 0] - pair_logits[:, 1]))
    own_gates = jnp.stack([first_gate, second_gate], axis=1)
    gate_pair = in_order(own_gates, lax.ppermute(own_gates, "c", SWAP), 0)
    combiner = jnp.sum(jnp.where(placed, gate_pair[:, :, None], 0.0), axis=1)

    packed = jnp.dot(chooser, pair_normed, preferred_element_type=jnp.float32).astype(jnp.bfloat16)
    arrived = lax.all_to_all(
        packed.reshape(experts, cap, half), ("x", "yl"), split_axis=0, concat_axis=0, tiled=True
    ).reshape(slots, half)
    home = experts_of(arrived, w_gate, w_up, w_down)
    returned = lax.all_to_all(
        home.reshape(experts, cap, half), ("x", "yl"), split_axis=0, concat_axis=0, tiled=True
    ).reshape(slots, half)
    mixture = jnp.dot(combiner, returned.astype(jnp.float32), precision=lax.Precision.HIGHEST)
    mine = lax.dynamic_slice_in_dim(mixture, c * rows, rows, axis=0)
    his = lax.dynamic_slice_in_dim(mixture, (1 - c) * rows, rows, axis=0)
    mixture = in_order(mine, lax.ppermute(his, "c", SWAP), 1)
    return (resid + mixture).astype(jnp.bfloat16)


def solution(mesh):
    fine = Mesh(mesh.devices.reshape(NX, NYL, NZ, NYH, NC), ("x", "yl", "z", "yh", "c"))
    ctx, tp = ("x", "yl", "z"), ("yh", "c")
    placed = (
        P(ctx + tp, None),
        P(ctx, tp),
        P(ctx, tp),
        P(ctx, tp),
        P(ctx),
        P(tp, ctx),
        P(),
        P(),
        P(None, ctx + tp),
        P(None, ctx + tp),
        P(ctx + tp, None),
        P(ctx + tp, None),
    )
    return jax.shard_map(
        per_device, mesh=fine, in_specs=placed, out_specs=P(ctx + tp, None), check_vma=False
    )
```
